256 devices in a mesh: shard: 8 (over z_hi, core), replica: 32 (over x, z_lo, y).
Axes of the slice: x: 4, y: 4, z: 8 (z_hi: 4, z_lo: 2; z = z_hi * 2 + z_lo), core: 2. Of those that a mesh axis runs over, the one named last changes fastest.
Arguments:
- tokens: bfloat16 [40960, 1024], P(('shard', 'replica')), may hold values from -6 to 6
- cotangent: bfloat16 [40960, 1024], P(('shard', 'replica')), may hold values from -6 to 6
- gain_one: bfloat16 [1024], P('shard'), may hold values from 0.5 to 1.5
- gain_two: bfloat16 [1024], P('shard'), may hold values from 0.5 to 1.5
- w_qkv: bfloat16 [1024, 2048], P('shard'), may hold values from -0.1875 to 0.1875
- w_out: bfloat16 [1024, 1024], P(None, 'shard'), may hold values from -1.5 to 1.5
- w_router: bfloat16 [1024, 10], P('shard'), may hold values from -0.09375 to 0.09375
- w_gate_up: bfloat16 [10, 1024, 1024], P(None, 'shard'), may hold values from -0.1875 to 0.1875
- w_down: bfloat16 [10, 512, 1024], P(None, None, 'shard'), may hold values from -1 to 1
- routes: int32 [40960, 8], P(('shard', 'replica')), may hold values from 0 to 9, all different within a row
- slot_order: int32 [256, 1280], P(('shard', 'replica')), may hold values from 0 to 1279, each once within a row
Outputs:
- layer_out: bfloat16 [40960, 1024], P(('shard', 'replica'))
- grad_tokens: bfloat16 [40960, 1024], P(('shard', 'replica'))
- grad_gain_one: float32 [1024], P('shard')
- grad_gain_two: float32 [1024], P('shard')
- grad_qkv: float32 [1024, 2048], P('shard')
- grad_out: float32 [1024, 1024], P(None, 'shard')
- grad_router: float32 [1024, 10], P('shard')
- grad_gate_up: float32 [10, 1024, 1024], P(None, 'shard')
- grad_down: float32 [10, 512, 1024], P(None, None, 'shard')
The draws below stay inside these ranges and needn't reach their ends.
Inputs may be any that keep to these rules, and one draw needn't show every extreme that they name: `routes`: each row names 8 different experts. `slot_order`: each row is a permutation of one device's pairs t * 8 + r.
All inputs are finite; a program needn't handle non-finite values.
Results may differ from the reference program's by a relative error of at most 0.03.
Values may be sent and summed in bfloat16 or wider, within the bound.
No kernel may reach another device: no remote copies, remote signals or barrier semaphores. Data moves between devices by JAX's collectives and lax.ppermute only.
A program may use at most 192 MiB of HBM per device.

```python
import math
import jax
import jax.numpy as jnp
from jax import lax

D = 1024
HEADS = 16
KV_HEADS = 8
HD = 64
F = 512
TOPK = 8
EXPERTS = 10
TOK_DEV = 160
CAP = 144
TOKENS = 40960
N_SHARD = 8
DEVICES = 256


def level_of(own_key, dims, cuts, low, largest):
    loudness = 1.0
    for dim, parts in cuts:
        steps = jax.random.uniform(jax.random.fold_in(jax.random.fold_in(own_key, 6), dim), (parts,), jnp.float32, low / len(cuts), largest / len(cuts))
        loudness = loudness * jnp.repeat(jnp.exp(steps), dims[dim] // parts).reshape((-1,) + (1,) * (len(dims) - 1 - dim))
    return loudness


def choose_distinct(key, rows, number_of, top, lift):
    order = jax.random.permutation(jax.random.fold_in(key, 1), number_of)
    pull = order
    for power in range(3):
        pull = pull * pull // number_of
    pull = pull * lift // number_of
    chance = jax.random.randint(jax.random.fold_in(key, 2), (rows, number_of), 0, 4096) + pull
    sure = jax.random.permutation(jax.random.fold_in(key, 3), rows)[jnp.arange(number_of) % rows]
    chance = jnp.where(jnp.arange(rows)[:, None] == sure[None, :], 1 << 14, chance)
    priority = chance * number_of + jnp.arange(number_of)
    return lax.top_k(priority.astype(jnp.int32), top)[1].astype(jnp.int32)


def gaussian(stream_key, shape, scale, most, shards=(), held_as=jnp.bfloat16):
    factor_of = level_of(stream_key, shape, shards, -0.22, 0.18) if shards else 1.0
    drawn = jax.random.normal(stream_key, shape, jnp.float32) * scale * factor_of
    return jnp.minimum(jnp.maximum(drawn, -most), most).astype(held_as)


def setup_inputs(seed: int = 0) -> dict:
    keys = jax.random.split(jax.random.key(seed), 12)
    tokens = gaussian(keys[0], (TOKENS, D), 1.0, 6.0, ((0, 256),))
    cotangent = gaussian(keys[1], (TOKENS, D), 1.0, 6.0, ((0, 256),))
    gain_one = jnp.clip(1.0 + 0.1 * jax.random.normal(keys[2], (D,), jnp.float32), 0.5, 1.5).astype(jnp.bfloat16)
    gain_two = jnp.clip(1.0 + 0.1 * jax.random.normal(keys[3], (D,), jnp.float32), 0.5, 1.5).astype(jnp.bfloat16)
    w_qkv = gaussian(keys[4], (D, (HEADS + 2 * KV_HEADS) * HD), D ** -0.5, 0.1875, ((0, 8),))
    w_out = gaussian(keys[5], (HEADS * HD, D), (max(HEADS * HD // 64, 1)) ** -0.5, 1.5, ((1, 8),))
    w_router = gaussian(keys[6], (D, EXPERTS), (0.5 / D ** 0.5), 0.09375, ((0, 8),))
    w_gate_up = gaussian(keys[7], (EXPERTS, D, 2 * F), D ** -0.5, 0.1875, ((1, 8),))
    w_down = gaussian(keys[8], (EXPERTS, F, D), (max(F // 16, 1)) ** -0.5, 1.0, ((2, 8),))
    routes = choose_distinct(keys[9], TOKENS, EXPERTS, TOPK, 6553)
    slot_order = jax.vmap(lambda own: jax.random.permutation(own, TOK_DEV * TOPK))(jax.random.split(keys[10], DEVICES)).reshape((DEVICES, TOK_DEV * TOPK)).astype(jnp.int32)
    return dict(tokens=tokens, cotangent=cotangent, gain_one=gain_one, gain_two=gain_two, w_qkv=w_qkv, w_out=w_out, w_router=w_router, w_gate_up=w_gate_up, w_down=w_down, routes=routes, slot_order=slot_order)


EPSILON = 1e-06
ROPE_BASE = 10000.0

@jax.custom_vjp
def low(v):
    return lax.optimization_barrier(v.astype(jnp.bfloat16)).astype(jnp.float32)

@jax.custom_vjp
def low_back(v):
    return v

def low_keep(v):
    return (low(v), None)

def low_pass(kept, grad):
    return (grad,)

def back_keep(v):
    return (v, None)

def back_low(kept, grad):
    return (low(grad),)
low.defvjp(low_keep, low_pass)
low_back.defvjp(back_keep, back_low)

def matmul(left, right):
    return jnp.dot(left, right, precision=lax.Precision.HIGHEST, preferred_element_type=jnp.float32)

def einsum_high(form, left, right):
    return jnp.einsum(form, left, right, precision=lax.Precision.HIGHEST, preferred_element_type=jnp.float32)

def rope_tables(length, head_size):
    half_width = head_size // 2
    position = jnp.arange(length).astype(jnp.float32)[:, None]
    frequency = ROPE_BASE ** (-jnp.arange(half_width).astype(jnp.float32) / half_width)
    angles = position * frequency[None, :]
    return (jnp.cos(angles)[:, None, :], jnp.sin(angles)[:, None, :])

def rotate(values, cosine, sine, direction):
    half_width = values.shape[-1] // 2
    first = values[..., :half_width]
    second = values[..., half_width:]
    return jnp.concatenate([first * cosine - direction * second * sine, second * cosine + direction * first * sine], axis=-1)

def slot_plan(route_ids, order_row):
    pair_expert = route_ids.reshape(-1).astype(jnp.int32)
    ordered = pair_expert[order_row]
    onehot_rows = (ordered[:, None] == jnp.arange(EXPERTS, dtype=jnp.int32)[None, :]).astype(jnp.int32)
    earlier = jnp.cumsum(onehot_rows, axis=0) - onehot_rows
    ordered_slot = lax.optimization_barrier(jnp.sum(earlier * onehot_rows, axis=1)).astype(jnp.int32)
    pair_slot = jnp.zeros_like(pair_expert).at[order_row].set(ordered_slot)
    total_slots = EXPERTS * CAP
    target = jnp.where(pair_slot < CAP, pair_expert * CAP + pair_slot, total_slots).astype(jnp.int32)
    pair_count = pair_expert.shape[0]
    pair_table = jnp.full((total_slots + 1,), pair_count, jnp.int32).at[target].set(jnp.arange(pair_count, dtype=jnp.int32))
    return (target, pair_table[:total_slots])

def layer(hidden_in, gain_one, gain_two, w_qkv, w_out, w_router, w_gate_up, w_down, route_ids, order_row):
    length = hidden_in.shape[0]
    target, pair_table = slot_plan(route_ids, order_row)
    cosine, sine = rope_tables(length, HD)
    width_q = HEADS * HD
    width_k = KV_HEADS * HD
    normed = hidden_in * lax.rsqrt(lax.optimization_barrier(jnp.mean(hidden_in * hidden_in, axis=-1, keepdims=True)) + EPSILON)
    normed = low(normed * gain_one)
    projected = low_back(matmul(normed, w_qkv))
    queries = low(rotate(projected[:, :width_q].reshape(length, HEADS, HD), cosine, sine, 1.0))
    key_rows = low(rotate(projected[:, width_q:width_q + width_k].reshape(length, KV_HEADS, HD), cosine, sine, 1.0))
    value_rows = low(projected[:, width_q + width_k:].reshape(length, KV_HEADS, HD))
    grouped = queries.reshape(length, KV_HEADS, HEADS // KV_HEADS, HD)
    scores = low_back(einsum_high('qhgd,khd->hgqk', grouped, key_rows) * (1.0 / math.sqrt(HD)))
    causal = jnp.arange(length)[:, None] >= jnp.arange(length)[None, :]
    scores = jnp.where(causal, scores, -1e+30)
    weights = low(jax.nn.softmax(scores, axis=-1))
    attended = einsum_high('hgqk,khd->qhgd', weights, value_rows).reshape(length, width_q)
    attended = low(low_back(attended))
    branch = low_back(matmul(attended, w_out))
    middle = hidden_in + branch
    normed_two = middle * lax.rsqrt(lax.optimization_barrier(jnp.mean(middle * middle, axis=-1, keepdims=True)) + EPSILON)
    normed_two = low(normed_two * gain_two)
    logits = low_back(matmul(normed_two, w_router))
    chosen = jnp.take_along_axis(logits, route_ids, axis=1)
    gates = jax.nn.softmax(chosen, axis=-1)
    padded = jnp.concatenate([normed_two, jnp.zeros((1, D), jnp.float32)], axis=0)
    slot_rows = padded[pair_table // TOPK].reshape(EXPERTS, CAP, D)
    gate_up = low_back(einsum_high('ecd,edf->ecf', slot_rows, w_gate_up))
    activated = low(jax.nn.silu(gate_up[..., :F]) * gate_up[..., F:])
    expert_out = low_back(einsum_high('ecf,efd->ecd', activated, w_down)).reshape(EXPERTS * CAP, D)
    expert_pad = jnp.concatenate([expert_out, jnp.zeros((1, D), jnp.float32)], axis=0)
    returned = expert_pad[target].reshape(length, TOPK, D)
    mixture = lax.optimization_barrier(jnp.sum(gates[:, :, None] * returned, axis=1))
    return middle + mixture

def reference(tokens, cotangent, gain_one, gain_two, w_qkv, w_out, w_router, w_gate_up, w_down, routes, slot_order):
    group = N_SHARD
    step_count = DEVICES // group
    params = (gain_one.astype(jnp.float32), gain_two.astype(jnp.float32), w_qkv.astype(jnp.float32), w_out.astype(jnp.float32), w_router.astype(jnp.float32), w_gate_up.astype(jnp.float32), w_down.astype(jnp.float32))
    inputs = tokens.astype(jnp.float32).reshape(step_count, group, TOK_DEV, D)
    route_blocks = routes.reshape(step_count, group, TOK_DEV, TOPK)
    order_blocks = slot_order.reshape(step_count, group, TOK_DEV * TOPK)

    def forward(param_list, layer_inputs):

        def step(carry, block):
            block_in, block_routes, block_order = block

            def single(seq_in, seq_routes, seq_order):
                return layer(seq_in, *param_list, seq_routes, seq_order)
            return (carry, jax.vmap(single)(block_in, block_routes, block_order))
        unused, outputs = lax.scan(jax.checkpoint(step), jnp.zeros((), jnp.float32), (layer_inputs, route_blocks, order_blocks))
        return outputs
    outputs, pullback = jax.vjp(forward, params, inputs)
    grad_params, grad_inputs = pullback(cotangent.astype(jnp.float32).reshape(outputs.shape))
    return (outputs.reshape(TOKENS, D).astype(jnp.bfloat16), grad_inputs.reshape(TOKENS, D).astype(jnp.bfloat16), grad_params[0], grad_params[1], grad_params[2], grad_params[3], grad_params[4], grad_params[5], grad_params[6])
```

```python
import math

import jax
import jax.numpy as jnp
from jax import lax
from jax.sharding import Mesh
from jax.sharding import PartitionSpec as P

D = 1024
HEADS = 16
KV_HEADS = 8
HD = 64
F = 512
TOPK = 8
EXPERTS = 10
CAP = 144
TOK = 160
EPSILON = 1e-06
ROPE_BASE = 10000.0

AXES = ("zh", "core", "x", "zl", "y")
SIZES = (4, 2, 4, 2, 4)
BF = jnp.bfloat16
F32 = jnp.float32


def dot(a, b, ca=1, cb=0):
    return lax.dot_general(a, b, (((ca,), (cb,)), ((), ())), preferred_element_type=F32)


def take(v, axis, k):
    return lax.ppermute(v, axis, [((i + k) % 4, i) for i in range(4)])


def ring_gather(v, axis):
    return [v] + [take(v, axis, k) for k in (1, 2, 3)]


def ring_return(blocks, axis):
    return [blocks[0]] + [take(blocks[(4 - k) % 4], axis, k) for k in (1, 2, 3)]


def keep_plan(routes, order):
    pairs = TOK * TOPK
    expert_row = routes.reshape(1, pairs)
    place = (lax.broadcasted_iota(jnp.int32, (pairs, pairs), 0) == order).astype(BF)
    named = (lax.broadcasted_iota(jnp.int32, (16, pairs), 0) == expert_row).astype(BF)
    ordered = dot(named, place)
    before = (
        lax.broadcasted_iota(jnp.int32, (pairs, pairs), 0)
        < lax.broadcasted_iota(jnp.int32, (pairs, pairs), 1)
    ).astype(BF)
    earlier = dot(ordered.astype(BF), before)
    kept = jnp.where(earlier < CAP, ordered, 0.0).astype(BF)
    kept_pair = dot(kept, place, 1, 1).astype(BF)
    owner = (
        lax.broadcasted_iota(jnp.int32, (TOK, pairs), 1) // TOPK
        == lax.broadcasted_iota(jnp.int32, (TOK, pairs), 0)
    ).astype(BF)
    kept_token = dot(owner, kept_pair, 1, 1)
    lane = lax.broadcasted_iota(jnp.int32, (TOK, 16), 1)
    routed = jnp.zeros((TOK, 16), F32)
    for r in range(TOPK):
        routed = routed + (routes[:, r : r + 1] == lane).astype(F32)
    return routed, kept_token


def rope_tables():
    half = HD // 2
    position = jnp.arange(TOK).astype(F32)[:, None]
    frequency = ROPE_BASE ** (-jnp.arange(half).astype(F32) / half)
    angles = position * frequency[None, :]
    return jnp.cos(angles), jnp.sin(angles)


def rotate(values, cosine, sine, direction):
    rows, width = values.shape
    v = values.reshape(rows // TOK, TOK, width // HD, 2, HD // 2)
    a, b = v[:, :, :, 0], v[:, :, :, 1]
    c = cosine[None, :, None, :]
    s = direction * sine[None, :, None, :]
    return jnp.stack([a * c - b * s, b * c + a * s], axis=3).reshape(rows, width)


def rms(v):
    return lax.rsqrt(jnp.mean(v * v, axis=-1, keepdims=True) + EPSILON)


def attention_units():
    for seq in range(4):
        for kv in range(2):
            yield seq, kv


def softmax_of(q, k):
    scores = dot(q, k, 1, 1) * (1.0 / math.sqrt(HD))
    rows = lax.broadcasted_iota(jnp.int32, (TOK, TOK), 0)
    cols = lax.broadcasted_iota(jnp.int32, (TOK, TOK), 1)
    scores = jnp.where(rows >= cols, scores, -1e30)
    peak = jnp.max(scores, axis=-1, keepdims=True)
    e = jnp.exp(scores - peak)
    return e / jnp.sum(e, axis=-1, keepdims=True)


def attention_forward(tok_all, gain, w, cosine, sine):
    x = tok_all.astype(F32)
    h1 = (x * rms(x) * gain).astype(BF)
    qkv = dot(h1, w)
    qk = rotate(qkv[:, :384], cosine, sine, 1.0).astype(BF)
    vv = qkv[:, 384:].astype(BF)
    out = []
    for seq in range(4):
        rows = slice(seq * TOK, seq * TOK + TOK)
        cols = []
        for head in range(4):
            kv = head // 2
            q = qk[rows, head * HD : head * HD + HD]
            k = qk[rows, 256 + kv * HD : 256 + kv * HD + HD]
            v = vv[rows, kv * HD : kv * HD + HD]
            cols.append(dot(softmax_of(q, k).astype(BF), v))
        out.append(jnp.concatenate(cols, axis=1))
    return h1, qk, vv, jnp.concatenate(out, axis=0).astype(BF)


def attention_backward(qk, vv, d_att, cosine, sine):
    scale = 1.0 / math.sqrt(HD)
    dq_all, dk_all, dv_all = [], [], []
    for seq in range(4):
        rows = slice(seq * TOK, seq * TOK + TOK)
        dqs, dks, dvs = [], [0.0, 0.0], [0.0, 0.0]
        for head in range(4):
            kv = head // 2
            q = qk[rows, head * HD : head * HD + HD]
            k = qk[rows, 256 + kv * HD : 256 + kv * HD + HD]
            v = vv[rows, kv * HD : kv * HD + HD]
            da = d_att[rows, head * HD : head * HD + HD]
            p = softmax_of(q, k)
            dp = dot(da, v, 1, 1)
            dvs[kv] = dvs[kv] + dot(p.astype(BF), da, 0, 0)
            ds = (p * (dp - jnp.sum(p * dp, axis=-1, keepdims=True))).astype(BF)
            dqs.append(dot(ds, k) * scale)
            dks[kv] = dks[kv] + dot(ds, q, 0, 0) * scale
        dq_all.append(jnp.concatenate(dqs, axis=1))
        dk_all.append(jnp.concatenate(dks, axis=1))
        dv_all.append(jnp.concatenate(dvs, axis=1))
    dqk = jnp.concatenate([jnp.concatenate(dq_all, 0), jnp.concatenate(dk_all, 0)], axis=1)
    dqk = rotate(dqk, cosine, sine, -1.0)
    return jnp.concatenate([dqk, jnp.concatenate(dv_all, 0)], axis=1).astype(BF)


def post_attention(tok, att, w_out, gain, w_router_t, routed, kept):
    middle = tok.astype(F32)
    for k in range(4):
        middle = middle + dot(att[k], w_out[k])
    rstd = rms(middle)
    h2 = (middle * rstd * gain).astype(BF)
    logits = dot(h2, w_router_t, 1, 1)
    masked = jnp.where(routed > 0.5, logits, -1e30)
    e = jnp.where(routed > 0.5, jnp.exp(masked - jnp.max(masked, axis=-1, keepdims=True)), 0.0)
    gates = e / jnp.sum(e, axis=-1, keepdims=True)
    weight = gates * kept
    high = weight.astype(BF)
    low = (weight - high.astype(F32)).astype(BF)
    pad = jnp.zeros((TOK, 128 - 2 * 16), BF)
    return middle, rstd, gates, jnp.concatenate([h2, high, low, pad], axis=1)


def moe_inner(h2_all, weight, c_all, w_gu, w_dn):
    gu = dot(h2_all, w_gu).reshape(-1, EXPERTS, 2, 128)
    g, u = gu[:, :, 0], gu[:, :, 1]
    s = 1.0 / (1.0 + jnp.exp(-g))
    act = (g * s * u).astype(BF)
    cw = dot(c_all, w_dn, 1, 1).reshape(-1, EXPERTS, 128)
    d_gates = jnp.sum(act.astype(F32) * cw, axis=2)
    wt = weight[:, :EXPERTS, None]
    d_act = cw * wt
    d_g = d_act * u * s * (1.0 + g * (1.0 - s))
    d_u = d_act * (g * s)
    d_gu = jnp.stack([d_g, d_u], axis=2).astype(BF).reshape(-1, EXPERTS * 256)
    wact = (act.astype(F32) * wt).astype(BF).reshape(-1, EXPERTS * 128)
    d_h2 = dot(d_gu, w_gu, 1, 1)
    return d_h2, d_gates, d_gu, wact


def local(tokens, cotangent, gain_one, gain_two, w_qkv, w_out, w_router, w_gate_up, w_down, routes, slot_order):
    xi = lax.axis_index("x")
    yi = lax.axis_index("y")
    ci = lax.axis_index("core")
    tok_all = jnp.concatenate(ring_gather(tokens, "x"), axis=0)
    heads = w_qkv[:, : 1024].reshape(128, 4, 2, 128)
    q_tiles = lax.dynamic_index_in_dim(heads, xi, 1, False)
    kv_tiles = lax.dynamic_index_in_dim(w_qkv[:, 1024:].reshape(128, 2, 4, 128), xi, 2, False)
    tiles = jnp.concatenate([q_tiles, kv_tiles], axis=1)
    qkv_tile = lax.dynamic_index_in_dim(tiles, yi, 1, False)
    out_rows = lax.dynamic_slice(w_out, (xi * 256 + yi * 64, 0), (64, 128))
    misc = jnp.concatenate([gain_one[None], gain_two[None], w_router.T, jnp.zeros((4, 128), BF)], axis=0)
    small = jnp.concatenate([qkv_tile, out_rows, misc], axis=0)
    small_all = lax.all_gather(small, ("zh", "core", "y"), axis=0).reshape(4, 2, 4, 208, 128)
    w_att = small_all[:, :, :, :128].transpose(0, 1, 3, 2, 4).reshape(1024, 512)
    w_o0 = small_all[:, :, :, 128:192].transpose(2, 3, 0, 1, 4).reshape(256, 1024)
    misc_all = small_all[:, :, 0, 192:].transpose(2, 0, 1, 3).reshape(16, 1024)
    w_o = ring_gather(w_o0, "x")
    gain_a = misc_all[0:1].astype(F32)
    gain_b = misc_all[1:2].astype(F32)
    router_t = jnp.concatenate([misc_all[2:12], jnp.zeros((6, D), BF)], axis=0)
    gu_local = w_gate_up.reshape(10, 128, 2, 4, 128)
    gu_x = lax.dynamic_index_in_dim(gu_local, xi, 3, False).transpose(0, 2, 1, 3).reshape(4, 5 * 128, 128)
    gu_xy = lax.dynamic_index_in_dim(gu_x, yi, 0, False)
    dn_x = lax.dynamic_index_in_dim(w_down.reshape(10, 4, 4, 32, 128), xi, 1, False)
    dn_xy = lax.dynamic_index_in_dim(dn_x, yi, 1, False).reshape(320, 128)
    experts = jnp.concatenate([gu_xy, dn_xy], axis=0)
    experts_z = lax.all_gather(experts, "zh", axis=0)
    experts_all = lax.all_gather(experts_z, ("core", "y"), axis=0).reshape(2, 4, 4, 960, 128)
    w_gu = experts_all[:, :, :, :640].reshape(2, 4, 4, 5, 128, 128).transpose(2, 0, 4, 1, 3, 5).reshape(1024, 2560)
    w_dn = experts_all[:, :, :, 640:].reshape(2, 4, 4, 10, 32, 128).transpose(3, 1, 4, 2, 0, 5).reshape(1280, 1024)

    routed, kept = keep_plan(routes, slot_order)
    cosine, sine = rope_tables()
    h1_all, qk, vv, att_all = attention_forward(tok_all, gain_a, w_att, cosine, sine)
    att = ring_return(list(att_all.reshape(4, TOK, 256)), "x")
    middle, rstd_two, gates, h2_ext = post_attention(tokens, att, w_o, gain_b, router_t, routed, kept)
    ext_all = jnp.concatenate(ring_gather(h2_ext, "x"), axis=0)
    c_all = jnp.concatenate(ring_gather(cotangent, "x"), axis=0)
    h2_all = ext_all[:, :1024]
    weight = ext_all[:, 1024:1040].astype(F32) + ext_all[:, 1040:1056].astype(F32)
    d_h2_part, d_gates_part, d_gu, wact = moe_inner(h2_all, weight, c_all, w_gu, w_dn)
    high = d_gates_part.astype(BF)
    low = (d_gates_part - high.astype(F32)).astype(BF)
    zero6 = jnp.zeros((4 * TOK, 6), BF)
    payload = jnp.concatenate([d_h2_part.astype(BF), high, zero6, low, zero6, jnp.zeros((4 * TOK, 96), BF)], axis=1)
    back = ring_return(list(payload.reshape(4, TOK, 1152)), "x")
    back = sum(b.astype(F32) for b in back)
    mix_part = dot(wact, w_dn).astype(BF)
    mix = ring_return(list(mix_part.reshape(4, TOK, 1024)), "x")
    layer_out = (middle + sum(m.astype(F32) for m in mix)).astype(BF)
    g_gu = dot(h2_all, d_gu, 0, 0).astype(BF)
    g_dn = dot(wact, c_all, 0, 0).astype(BF)
    upstream = cotangent.astype(F32)
    h2 = h2_ext[:, :1024]
    d_gates = (back[:, 1024:1040] + back[:, 1040:1056]) * kept
    d_logits = (gates * (d_gates - jnp.sum(gates * d_gates, axis=1, keepdims=True))).astype(BF)
    g_router = dot(d_logits, h2, 0, 0)
    d_h2 = back[:, :1024] + dot(d_logits, router_t)
    norm_two = middle * rstd_two
    g_gain_two = jnp.sum(d_h2 * norm_two, axis=0, keepdims=True)
    u2 = d_h2 * gain_b
    d_middle = upstream + rstd_two * (u2 - norm_two * jnp.mean(u2 * norm_two, axis=-1, keepdims=True))
    d_mid_all = jnp.concatenate(ring_gather(d_middle.astype(BF), "x"), axis=0)
    d_att = dot(d_mid_all, w_o0, 1, 1).astype(BF)
    d_qkv = attention_backward(qk, vv, d_att, cosine, sine)
    g_qkv = dot(h1_all, d_qkv, 0, 0)
    g_out = dot(att_all, d_mid_all, 0, 0)
    d_h1_part = dot(d_qkv, w_att, 1, 1)
    tf = tok_all.astype(F32)
    g_gain_one = jnp.sum(d_h1_part * (tf * rms(tf)), axis=0, keepdims=True)
    d_h1 = ring_return(list(d_h1_part.astype(BF).reshape(4, TOK, 1024)), "x")
    d_h1 = sum(b.astype(F32) for b in d_h1)
    x = tokens.astype(F32)
    rstd_one = rms(x)
    norm_one = x * rstd_one
    u1 = d_h1 * gain_a
    grad_tokens = (d_middle + rstd_one * (u1 - norm_one * jnp.mean(u1 * norm_one, axis=-1, keepdims=True))).astype(BF)

    def fold(v, n):
        other = lax.ppermute(lax.dynamic_index_in_dim(v, 1 - ci, 0, False), "core", [(0, 1), (1, 0)])
        mine = lax.dynamic_index_in_dim(v, ci, 0, False)
        return (mine.astype(F32) + other.astype(F32)).astype(BF)

    def fold_z(v, n):
        v = jnp.broadcast_to(v[:, None], (4, 2, n, 128)).reshape(8, n, 128)
        v = lax.all_to_all(v, ("zh", "zl"), 0, 0, tiled=True)
        return jnp.sum(v.astype(F32), axis=0).astype(BF)

    e_gu = g_gu.reshape(4, 2, 128, 4, 5, 128).transpose(1, 3, 0, 4, 2, 5).reshape(2, 4, 4, 640, 128)
    e_dn = g_dn.reshape(10, 4, 32, 4, 2, 128).transpose(4, 1, 3, 0, 2, 5).reshape(2, 4, 4, 320, 128)
    e = fold(jnp.concatenate([e_gu, e_dn], axis=3), 960)
    e = lax.psum_scatter(e, "y", scatter_dimension=0, tiled=False)
    e = fold_z(e, 960)
    e = lax.all_gather(e, ("x", "y"), axis=0).reshape(4, 4, 960, 128)
    grad_gate_up = (
        e[:, :, :640].reshape(4, 10, 2, 128, 128).transpose(1, 3, 2, 0, 4).reshape(10, 128, 1024).astype(F32)
    )
    grad_down = e[:, :, 640:].reshape(4, 4, 10, 32, 128).transpose(2, 0, 1, 3, 4).reshape(10, 512, 128).astype(F32)

    a_qkv = g_qkv.astype(BF).reshape(4, 2, 128, 4, 128).transpose(1, 3, 0, 2, 4)
    a_out = g_out.astype(BF).reshape(4, 64, 4, 2, 128).transpose(3, 0, 2, 1, 4)
    g_misc = jnp.concatenate([g_gain_one, g_gain_two, g_router[:10], jnp.zeros((4, D), F32)], axis=0).astype(BF)
    a_misc = g_misc.reshape(16, 4, 2, 128).transpose(2, 1, 0, 3)[:, None]
    a_misc = jnp.concatenate([a_misc, jnp.zeros((2, 3, 4, 16, 128), BF)], axis=1)
    a = fold(jnp.concatenate([a_qkv, a_out, a_misc], axis=3), 208)
    a = lax.all_to_all(a, "y", 0, 0, tiled=True)
    a = jnp.sum(a.astype(F32), axis=0).astype(BF)
    a = fold_z(a, 208)
    a = lax.all_gather(a, ("x", "y"), axis=0).reshape(4, 4, 208, 128)
    q = a[:, :2, :128].transpose(2, 0, 1, 3).reshape(128, 1024)
    k = a[:, 2, :128].transpose(1, 0, 2).reshape(128, 512)
    v = a[:, 3, :128].transpose(1, 0, 2).reshape(128, 512)
    grad_qkv = jnp.concatenate([q, k, v], axis=1).astype(F32)
    grad_out = a[:, :, 128:192].reshape(1024, 128).astype(F32)
    m = jnp.sum(a[:, 0, 192:].astype(F32), axis=0)
    return (layer_out, grad_tokens, m[0], m[1], grad_qkv, grad_out, m[2:12].T, grad_gate_up, grad_down)


def solution(mesh):
    fine = Mesh(mesh.devices.reshape(SIZES), AXES)
    rows = P(AXES, None)
    shard = ("zh", "core")
    return jax.shard_map(
        local,
        mesh=fine,
        in_specs=(
            rows, rows, P(shard), P(shard), P(shard, None), P(None, shard), P(shard, None),
            P(None, shard, None), P(None, None, shard), rows, rows,
        ),
        out_specs=(
            rows, rows, P(shard), P(shard), P(shard, None), P(None, shard), P(shard, None),
            P(None, shard, None), P(None, None, shard),
        ),
        check_vma=False,
    )
```

```python
import math

import jax
import jax.numpy as jnp
import numpy as np
from jax import lax
from jax.experimental import pallas as pl
from jax.experimental.pallas import tpu as pltpu
from jax.sharding import Mesh
from jax.sharding import PartitionSpec as P

D = 1024
HD = 64
TOPK = 8
EXPERTS = 10
CAP = 144
TOK = 160
RING = 4 * TOK
EPSILON = 1e-06
ROPE_BASE = 10000.0
SCALE = 1.0 / math.sqrt(HD)

AXES = ("zh", "core", "x", "zl", "y")
SIZES = (4, 2, 4, 2, 4)
BF = jnp.bfloat16
F32 = jnp.float32
VMEM = pl.BlockSpec(memory_space=pltpu.VMEM)
SMEM = pl.BlockSpec(memory_space=pltpu.SMEM)
ANY = pl.BlockSpec(memory_space=pl.ANY)
SMALL = 208
HALF = 5


def sds(shape, dtype):
    return jax.ShapeDtypeStruct(shape, dtype)


def call(kernel, name, outs, args, in_specs=None, out_specs=None, scratch=(), flops=0, moved=0):
    return pl.pallas_call(
        kernel,
        out_shape=tuple(outs),
        in_specs=in_specs or [VMEM] * len(args),
        out_specs=tuple(out_specs or [VMEM] * len(outs)),
        scratch_shapes=list(scratch),
        compiler_params=pltpu.CompilerParams(vmem_limit_bytes=52 * 2**20),
        cost_estimate=pl.CostEstimate(flops=flops, bytes_accessed=moved, transcendentals=0),
        name=name,
    )(*args)


def dot(a, b, ca=1, cb=0):
    return lax.dot_general(a, b, (((ca,), (cb,)), ((), ())), preferred_element_type=F32)


def take(v, axis, k):
    return lax.ppermute(v, axis, [((i + k) % 4, i) for i in range(4)])


def ring_gather(v, axis):
    return [v] + [take(v, axis, k) for k in (1, 3, 2)]


def ring_return(blocks, axis):
    return [blocks[0], take(blocks[2], axis, 1), take(blocks[1], axis, 3), take(blocks[3], axis, 2)]


def iota(shape, dim):
    return lax.broadcasted_iota(jnp.int32, shape, dim)


def rms(v):
    return lax.rsqrt(jnp.mean(v * v, axis=-1, keepdims=True) + EPSILON)


def rope_tables():
    half = HD // 2
    frequency = (ROPE_BASE ** (-np.arange(half, dtype=np.float32) / np.float32(half))).astype(np.float32)
    angles = np.arange(TOK, dtype=np.float32)[:, None] * frequency[None, :]
    cosine = np.cos(angles).astype(np.float32)
    sine = np.sin(angles).astype(np.float32)
    return np.tile(np.concatenate([cosine, cosine], 1), (1, 6)), np.tile(np.concatenate([-sine, sine], 1), (1, 6))


def rotate(v, cosine, sine):
    width = v.shape[1]
    first = (iota(v.shape, 1) % HD) < HD // 2
    other = jnp.where(first, pltpu.roll(v, width - HD // 2, 1), pltpu.roll(v, HD // 2, 1))
    return v * cosine + other * sine


def run_copies(copies, sem):
    started = [pltpu.make_async_copy(a, b, sem.at[n]) for n, (a, b) in enumerate(copies)]
    for c in started:
        c.start()
    for c in started:
        c.wait()


def pick_kernel(at, qkv, out, misc, small, sem):
    x = at[0]
    copies = [(misc, small.at[512:528]), (out.at[pl.ds(pl.multiple_of(x * 256, 256), 256), :], small.at[528:784])]
    for k, col in enumerate((x * 256, x * 256 + 128, 1024 + x * 128, 1536 + x * 128)):
        copies.append((qkv.at[:, pl.ds(pl.multiple_of(col, 128), 128)], small.at[k * 128 : k * 128 + 128]))
    run_copies(copies, sem)


def pick_experts_kernel(at, gu, dn, keep, send, sem):
    x, y, me = at[0], at[1], at[2]
    copies = []
    for half, to in ((me, keep), (1 - me, send)):
        some, rows = pl.ds(half * HALF, HALF), pl.ds(pl.multiple_of(y * 32, 32), 32)
        copies.append((gu.at[some, rows, pl.ds(pl.multiple_of(x * 128, 128), 128)], to.at[:, 0:32]))
        copies.append((gu.at[some, rows, pl.ds(pl.multiple_of(512 + x * 128, 128), 128)], to.at[:, 32:64]))
        copies.append((dn.at[some, pl.ds(pl.multiple_of(x * 128 + y * 32, 32), 32), :], to.at[:, 64:96]))
    run_copies(copies, sem)


def plan_kernel(routes, expert_row, order, routed_ref, kept_ref):
    pairs = TOK * TOPK
    place = jnp.where(iota((pairs, pairs), 0) == order[...], 1.0, 0.0).astype(BF)
    named = jnp.where(iota((16, pairs), 0) == expert_row[...], 1.0, 0.0).astype(BF)
    ordered = dot(named, place)
    before = jnp.where(iota((pairs, pairs), 0) < iota((pairs, pairs), 1), 1.0, 0.0).astype(BF)
    earlier = dot(ordered.astype(BF), before)
    kept = jnp.where(earlier < CAP, ordered, 0.0).astype(BF)
    kept_pair = dot(kept, place, 1, 1).astype(BF)
    token = iota((TOK, pairs), 0) * TOPK
    pair = iota((TOK, pairs), 1)
    owner = jnp.where((pair >= token) & (pair < token + TOPK), 1.0, 0.0).astype(BF)
    kept_ref[...] = dot(owner, kept_pair, 1, 1)
    lane = iota((TOK, 16), 1)
    routed = jnp.zeros((TOK, 16), F32)
    for r in range(TOPK):
        routed = routed + jnp.where(routes[:, r : r + 1] == lane, 1.0, 0.0)
    routed_ref[...] = routed


def place_of(at, k, r):
    return k * 2 + (at[2] + r) % 2


def load_misc(at, own, oth, scr):
    for r, ref in ((0, own), (1, oth)):
        for k in range(4):
            scr[place_of(at, k, r)] = ref[k, 512:528, :]
    return jnp.concatenate([scr[s] for s in range(8)], axis=1)


def load_w_att(at, own, oth, scr):
    for r, ref in ((0, own), (1, oth)):
        for k in range(4):
            row = pl.multiple_of(place_of(at, k, r) * 128, 128)
            for t in range(4):
                scr[pl.ds(row, 128), t * 128 : t * 128 + 128] = ref[k, t * 128 : t * 128 + 128, :]


def load_w_out(at, own, oth, scr):
    for r, piece in ((0, own), (1, oth)):
        for k in range(4):
            col = pl.multiple_of(place_of(at, k, r) * 128, 128)
            scr[:, pl.ds(col, 128)] = piece(k)


def softmax_of(q, k):
    scores = dot(q, k, 1, 1) * SCALE
    n = q.shape[0]
    row = iota((n, TOK), 0)
    row = jnp.where(row >= TOK, row - TOK, row)
    scores = jnp.where(row >= iota((n, TOK), 1), scores, -1e30)
    e = jnp.exp(scores - jnp.max(scores, axis=-1, keepdims=True))
    return e / jnp.sum(e, axis=-1, keepdims=True)


def pair_of(v, kv):
    return jnp.concatenate([v[:, kv * 128 : kv * 128 + HD], v[:, kv * 128 + HD : kv * 128 + 128]], axis=0)


def unpair(v):
    return jnp.concatenate([v[:TOK], v[TOK:]], axis=1)


def attention_kernel(at, t0, t1, t2, t3, own, oth, cosine, sine, h1, qk, vv, a0, a1, a2, a3, c_all, w, misc_scr):
    load_w_att(at, own, oth, w)
    gain = load_misc(at, own, oth, misc_scr)[10:11].astype(F32)
    for s, t in enumerate((t0, t1, t2, t3)):
        x = t[0].astype(F32)
        h1[s * TOK : s * TOK + TOK] = (x * rms(x) * gain).astype(BF)
        c_all[s * TOK : s * TOK + TOK] = t[1]
    for s, a in enumerate((a0, a1, a2, a3)):
        rows = slice(s * TOK, s * TOK + TOK)
        qkv = dot(h1[rows], w[...])
        turned = rotate(qkv[:, :384], cosine[...], sine[...]).astype(BF)
        values = qkv[:, 384:].astype(BF)
        qk[rows] = turned
        vv[rows] = values
        heads = []
        for kv in range(2):
            k = turned[:, 256 + kv * HD : 256 + kv * HD + HD]
            v = values[:, kv * HD : kv * HD + HD]
            probs = softmax_of(pair_of(turned, kv), k).astype(BF)
            heads.append(unpair(dot(probs, v)))
        a[...] = jnp.concatenate(heads, axis=1).astype(BF)


def middle_kernel(
    at, tok, a0, a1, a2, a3, o0, o1, o2, o3, v, own, oth, routed, kept, middle, ext, gates_ref, w, misc_scr
):
    misc = load_misc(at, own, oth, misc_scr)
    m = tok[...].astype(F32)
    for n, (a, o) in enumerate(((a0, o0), (a1, o1), (a2, o2), (a3, o3))):
        load_w_out(at, lambda k: o[k], (lambda k: oth[k, 528:784]) if n == 0 else (lambda k: v[n - 1, k]), w)
        m = m + dot(a[...], w[...])
    middle[...] = m
    h2 = (m * rms(m) * misc[11:12].astype(F32)).astype(BF)
    ext[:, :D] = h2
    logits = dot(h2, misc, 1, 1)
    named = routed[...] > 0.5
    e = jnp.where(named, logits, -1e30)
    e = jnp.where(named, jnp.exp(e - jnp.max(e, axis=-1, keepdims=True)), 0.0)
    gates = e / jnp.sum(e, axis=-1, keepdims=True)
    gates_ref[...] = gates
    weight = gates * kept[...]
    high = weight.astype(BF).astype(F32)
    ext[:, D:] = jnp.concatenate([high, weight - high, jnp.zeros((TOK, 96), F32)], axis=1).astype(BF)


def load_w_gu(at, ex, w):
    for r in range(2):
        core = (at[2] + r) % 2
        for zh in range(4):
            for y in range(4):
                row = pl.multiple_of((zh * 2 + core) * 128 + y * 32, 32)
                for e in range(HALF):
                    w[pl.ds(row, 32), e * 256 : e * 256 + 128] = ex[zh, y, r, e, 0:32, :]
                    w[pl.ds(row, 32), e * 256 + 128 : e * 256 + 256] = ex[zh, y, r, e, 32:64, :]


def load_w_dn(at, ex, w):
    for r in range(2):
        core = (at[2] + r) % 2
        for zh in range(4):
            col = pl.multiple_of((zh * 2 + core) * 128, 128)
            for y in range(4):
                for e in range(HALF):
                    w[e * 128 + y * 32 : e * 128 + y * 32 + 32, pl.ds(col, 128)] = ex[zh, y, r, e, 64:96, :]


def column(v, lane, e):
    return jnp.sum(jnp.where(lane == e, v, 0.0), axis=1, keepdims=True)


def experts_kernel(at, e0, e1, e2, e3, c, ex, pay, mix, d_gu, wact, h2, wg, wd):
    load_w_gu(at, ex, wg)
    load_w_dn(at, ex, wd)
    weight = []
    for s, e in enumerate((e0, e1, e2, e3)):
        h2[s * TOK : s * TOK + TOK] = e[:, :D]
        extra = e[:, D:].astype(F32)
        weight.append(extra[:, :16] + extra[:, 16:32])
    weight = jnp.concatenate(weight, axis=0)
    lane = iota((RING, 16), 1)
    dg = jnp.zeros((RING, 16), F32)
    for e in range(HALF):
        gu = dot(h2[...], wg[:, e * 256 : e * 256 + 256])
        cw = dot(c[...], wd[e * 128 : e * 128 + 128], 1, 1)
        g, u = gu[:, :128], gu[:, 128:]
        sig = 1.0 / (1.0 + jnp.exp(-g))
        silu = g * sig
        act = (silu * u).astype(BF).astype(F32)
        wt = column(weight, lane, at[2] * HALF + e)
        d_act = cw * wt
        d_gu[:, e * 256 : e * 256 + 128] = (d_act * u * sig * (1.0 + g * (1.0 - sig))).astype(BF)
        d_gu[:, e * 256 + 128 : e * 256 + 256] = (d_act * silu).astype(BF)
        wact[:, e * 128 : e * 128 + 128] = (act * wt).astype(BF)
        dg = dg + jnp.where(lane == at[2] * HALF + e, jnp.sum(act * cw, axis=1, keepdims=True), 0.0)
    pay[:, :D] = dot(d_gu[...], wg[...], 1, 1).astype(BF)
    high = dg.astype(BF).astype(F32)
    pay[:, D:] = jnp.concatenate([high, dg - high, jnp.zeros((RING, 96), F32)], axis=1).astype(BF)
    mix[...] = dot(wact[...], wd[...]).astype(BF)


def add_kernel(a, b, *outs):
    for s, o in enumerate(outs):
        rows = slice(s * TOK, s * TOK + TOK)
        o[...] = (a[rows].astype(F32) + b[rows].astype(F32)).astype(BF)


def expert_grads_kernel(
    e0, e1, e2, e3, e4, e5, e6, e7, c, c_oth, d_gu, d_gu_oth, wact, wact_oth, after, grads, h2, cc, dg, wa
):
    for s, e in enumerate((e0, e1, e2, e3, e4, e5, e6, e7)):
        h2[s * TOK : s * TOK + TOK] = e[:, :D]
    for s, (cs, ds, ws) in enumerate(((c, d_gu, wact), (c_oth, d_gu_oth, wact_oth))):
        rows = slice(s * RING, s * RING + RING)
        cc[rows] = cs[...]
        dg[rows] = ds[...]
        wa[rows] = ws[...]
    for e in range(HALF):
        g = dot(h2[...], dg[:, e * 256 : e * 256 + 256], 0, 0).astype(BF)
        for zh in range(4):
            for core in range(2):
                for y in range(4):
                    s = (zh * 2 + core) * 128 + y * 32
                    grads[core, y, zh, e, 0:32, :] = g[s : s + 32, 0:128]
                    grads[core, y, zh, e, 32:64, :] = g[s : s + 32, 128:256]
        g = dot(wa[:, e * 128 : e * 128 + 128], cc[...], 0, 0).astype(BF)
        for zh in range(4):
            for core in range(2):
                s = (zh * 2 + core) * 128
                for y in range(4):
                    grads[core, y, zh, e, 64:96, :] = g[y * 32 : y * 32 + 32, s : s + 128]


def hold_kernel(v, *rest):
    rest[-1][...] = v[...]


def stack_out_kernel(o1, o2, o3, after, out):
    for k, o in enumerate((o1, o2, o3)):
        out[k] = o[...]


def sum_of(v):
    total = v[0].astype(F32)
    for k in range(1, v.shape[0]):
        total = total + v[k].astype(F32)
    return total


def add_small_kernel(a, b, out):
    out[...] = (a[...].astype(F32) + b[...].astype(F32)).astype(BF)


def sum_twice_kernel(v, after, out):
    total = sum_of(v).astype(BF)
    for zh in range(4):
        out[2 * zh] = total[zh]
        out[2 * zh + 1] = total[zh]


def sum_spread_kernel(v, out):
    total = sum_of(v).astype(BF)
    for k in range(16):
        out[k] = total


def middle_back_kernel(at, b0, b1, b2, b3, middle, ext, gates_ref, kept, cot, own, oth, after, d_middle, d_low, g_misc, misc_scr):
    misc = load_misc(at, own, oth, misc_scr)
    lane = iota((16, D), 0)
    back = b0[...].astype(F32) + b1[...].astype(F32) + b2[...].astype(F32) + b3[...].astype(F32)
    gates = gates_ref[...]
    d_gates = (back[:, D : D + 16] + back[:, D + 16 : D + 32]) * kept[...]
    d_logits = (gates * (d_gates - jnp.sum(gates * d_gates, axis=1, keepdims=True))).astype(BF)
    g_router = dot(d_logits, ext[:, :D], 0, 0)
    d_h2 = back[:, :D] + dot(d_logits, misc)
    m = middle[...]
    rstd = rms(m)
    norm = m * rstd
    g_gain = jnp.sum(d_h2 * norm, axis=0, keepdims=True)
    g_misc[...] = jnp.where(lane == 11, g_gain, g_router)
    u = d_h2 * misc[11:12].astype(F32)
    d = cot[...].astype(F32) + rstd * (u - norm * jnp.mean(u * norm, axis=-1, keepdims=True))
    d_middle[...] = d
    d_low[...] = d.astype(BF)


def attention_back_kernel(
    at, m0, m1, m2, m3, t0, t1, t2, t3, a0, a1, a2, a3, h1, qk, vv, own, oth, cosine, sine, g_in, mix, mix_in,
    p0, p1, p2, p3, mine, send, w, wo, dm, att, dqkv, grads, sem,
):
    me = at[2]
    load_w_att(at, own, oth, w)
    load_w_out(at, lambda k: own[k, 528:784], lambda k: oth[k, 528:784], wo)
    for s, (m, a) in enumerate(((m0, a0), (m1, a1), (m2, a2), (m3, a3))):
        rows = slice(s * TOK, s * TOK + TOK)
        dm[rows] = m[...]
        att[rows] = a[...]
    for s in range(4):
        rows = slice(s * TOK, s * TOK + TOK)
        d_att = dot(dm[rows], wo[...], 1, 1).astype(BF)
        turned, values = qk[rows], vv[rows]
        dq, dk, dv = [], [], []
        for kv in range(2):
            k = turned[:, 256 + kv * HD : 256 + kv * HD + HD]
            v = values[:, kv * HD : kv * HD + HD]
            q = pair_of(turned, kv)
            da = pair_of(d_att, kv)
            p = softmax_of(q, k)
            dp = dot(da, v, 1, 1)
            dv.append(dot(p.astype(BF), da, 0, 0))
            ds = (p * (dp - jnp.sum(p * dp, axis=-1, keepdims=True))).astype(BF)
            dq.append(unpair(dot(ds, k)) * SCALE)
            dk.append(dot(ds, q, 0, 0) * SCALE)
        turned = rotate(jnp.concatenate(dq + dk, axis=1), cosine[...], -sine[...])
        dqkv[rows] = jnp.concatenate([turned] + dv, axis=1).astype(BF)
    g = dot(h1[...], dqkv[...], 0, 0).astype(BF)
    for y in range(4):
        for zh in range(4):
            for cc in range(2):
                s = (zh * 2 + cc) * 128
                grads[(cc + me) % 2, y, zh, 0:128, :] = g[s : s + 128, y * 128 : y * 128 + 128]
    g = dot(att[...], dm[...], 0, 0).astype(BF)
    for y in range(4):
        for zh in range(4):
            for cc in range(2):
                s = (zh * 2 + cc) * 128
                grads[(cc + me) % 2, y, zh, 128:192, :] = g[y * 64 : y * 64 + 64, s : s + 128]
    gain = jnp.zeros((1, D), F32)
    for s, (t, p) in enumerate(((t0, p0), (t1, p1), (t2, p2), (t3, p3))):
        d_h1 = dot(dqkv[s * TOK : s * TOK + TOK], w[...], 1, 1)
        x = t[0].astype(F32)
        gain = gain + jnp.sum(d_h1 * (x * rms(x)), axis=0, keepdims=True)
        p[:TOK] = d_h1.astype(BF)
        rows = slice(s * TOK, s * TOK + TOK)
        p[TOK:] = (mix[rows].astype(F32) + mix_in[rows].astype(F32)).astype(BF)
    g = jnp.where(iota((16, D), 0) == 10, gain, g_in[...]).astype(BF)
    for zh in range(4):
        for cc in range(2):
            s = (zh * 2 + cc) * 128
            grads[(cc + me) % 2, 0, zh, 192:SMALL, :] = g[:, s : s + 128]
            for y in range(1, 4):
                grads[(cc + me) % 2, y, zh, 192:SMALL, :] = jnp.zeros((16, 128), BF)
    to_mine = pltpu.make_async_copy(grads.at[0], mine, sem.at[0])
    to_send = pltpu.make_async_copy(grads.at[1], send, sem.at[1])
    to_mine.start()
    to_send.start()
    to_mine.wait()
    to_send.wait()


def tokens_kernel(at, b0, b1, b2, b3, tok, d_middle, middle, own, oth, after, out, layer, misc_scr):
    gain = load_misc(at, own, oth, misc_scr)[10:11].astype(F32)
    total = b0[...].astype(F32) + b1[...].astype(F32) + b2[...].astype(F32) + b3[...].astype(F32)
    layer[...] = (middle[...] + total[TOK:]).astype(BF)
    u = total[:TOK] * gain
    x = tok[...].astype(F32)
    rstd = rms(x)
    norm = x * rstd
    out[...] = (d_middle[...] + rstd * (u - norm * jnp.mean(u * norm, axis=-1, keepdims=True))).astype(BF)


def spread_kernel(first, e, gu, dn):
    for k in range(HALF):
        for x in range(4):
            for y in range(4):
                rows, row, col = slice(y * 32, y * 32 + 32), x * 128 + y * 32, x * 128
                gu[k, rows, col : col + 128] = e[x, y, 0, k, 0:32].astype(F32)
                gu[k, rows, 512 + col : 640 + col] = e[x, y, 0, k, 32:64].astype(F32)
                dn[k, row : row + 32] = e[x, y, 0, k, 64:96].astype(F32)


def spread(zl, e):
    return pl.pallas_call(
        spread_kernel,
        out_shape=(sds((EXPERTS, 128, 1024), F32), sds((EXPERTS, 512, 128), F32)),
        grid_spec=pltpu.PrefetchScalarGridSpec(
            num_scalar_prefetch=1,
            grid=(2,),
            in_specs=[pl.BlockSpec((4, 4, 1, HALF, 96, 128), lambda i, first: (0, 0, i, 0, 0, 0))],
            out_specs=(
                pl.BlockSpec((HALF, 128, 1024), lambda i, first: ((first[0] + i) % 2, 0, 0)),
                pl.BlockSpec((HALF, 512, 128), lambda i, first: ((first[0] + i) % 2, 0, 0)),
            ),
        ),
        compiler_params=pltpu.CompilerParams(vmem_limit_bytes=52 * 2**20),
        name="spread",
    )(zl, e)


def spread_small_kernel(a, qkv, out, misc):
    for x in range(4):
        for y in range(4):
            c = x * 256 + y * 128 if y < 2 else y * 512 + x * 128
            qkv[:, c : c + 128] = a[x, y, 0:128].astype(F32)
            out[x * 256 + y * 64 : x * 256 + y * 64 + 64] = a[x, y, 128:192].astype(F32)
    m = a[0, 0, 192:SMALL].astype(F32)
    for x in range(1, 4):
        m = m + a[x, 0, 192:SMALL].astype(F32)
    misc[...] = m


def local(tokens, cotangent, gain_one, gain_two, w_qkv, w_out, w_router, w_gate_up, w_down, routes, slot_order):
    at = jnp.stack([lax.axis_index(a) for a in ("x", "y", "core", "zh", "zl")]).astype(jnp.int32)
    swap = [(0, 1), (1, 0)]
    cosine, sine = (jnp.asarray(t) for t in rope_tables())

    misc = jnp.concatenate([w_router.T, gain_one[None], gain_two[None], jnp.zeros((4, 128), BF)], axis=0)
    (small,) = call(
        pick_kernel, "pick", [sds((784, 128), BF)], (at, w_qkv, w_out, misc),
        in_specs=[SMEM] + [ANY] * 3, scratch=[pltpu.SemaphoreType.DMA((6,))], moved=1 << 19,
    )
    keep, send = call(
        pick_experts_kernel, "pick_experts", [sds((HALF, 96, 128), BF)] * 2, (at, w_gate_up, w_down),
        in_specs=[SMEM] + [ANY] * 2, scratch=[pltpu.SemaphoreType.DMA((6,))], moved=1 << 19,
    )
    ex = jnp.stack([keep, lax.ppermute(send, "core", swap)])
    ex = lax.all_gather(ex, ("zh", "y"), axis=0).reshape(4, 4, 2, HALF, 96, 128)
    tok = ring_gather(jnp.stack([tokens, cotangent]), "x")
    own = lax.all_gather(small, "zh", axis=0)
    (own,) = call(hold_kernel, "stack", [sds((4, 784, 128), BF)], (own, *tok[1:]), in_specs=[VMEM] + [ANY] * 3, moved=2 << 20)
    oth = lax.ppermute(own, "core", swap)
    w_o = ring_gather(own[:, 528:], "x")

    routed, kept = call(
        plan_kernel, "plan", [sds((TOK, 16), F32)] * 2,
        (routes, routes.reshape(1, TOK * TOPK), slot_order), flops=2 * 1280 * 1280 * 64, moved=1 << 20,
    )
    misc_scr = pltpu.VMEM((8, 16, 128), BF)
    block = sds((TOK, D), BF)
    h1, qk, vv, *att, c_all = call(
        attention_kernel, "attention",
        [sds((RING, D), BF), sds((RING, 384), BF), sds((RING, 128), BF)] + [sds((TOK, 256), BF)] * 4 + [sds((RING, D), BF)],
        (at, *tok, own, oth, cosine, sine), in_specs=[SMEM] + [VMEM] * 8,
        scratch=[pltpu.VMEM((D, 512), BF), misc_scr], flops=2 * RING * D * 512 * 2, moved=10 << 20,
    )
    att_home = ring_return(att, "x")
    (w_o_oth,) = call(
        stack_out_kernel, "stack_out", [sds((3, 4, 256, 128), BF)], (*w_o[1:], h1), in_specs=[VMEM] * 3 + [ANY], moved=2 << 20,
    )
    w_o_oth = lax.ppermute(w_o_oth, "core", swap)
    c_oth = lax.ppermute(c_all, "core", swap)
    middle, ext, gates = call(
        middle_kernel, "middle", [sds((TOK, D), F32), sds((TOK, D + 128), BF), sds((TOK, 16), F32)],
        (at, tokens, *att_home, *w_o, w_o_oth, own, oth, routed, kept),
        in_specs=[SMEM] + [VMEM] * 14,
        scratch=[pltpu.VMEM((256, D), BF), misc_scr], flops=2 * TOK * D * D, moved=8 << 20,
    )
    exts = ring_gather(ext, "x")
    exts_oth = [lax.ppermute(e, "core", swap) for e in exts]

    def experts(pieces, c):
        return call(
            experts_kernel, "experts",
            [sds((RING, D + 128), BF), sds((RING, D), BF), sds((RING, HALF * 256), BF), sds((RING, HALF * 128), BF)],
            (at, *pieces, c, ex), in_specs=[SMEM] + [VMEM] * 6,
            scratch=[pltpu.VMEM((RING, D), BF), pltpu.VMEM((D, HALF * 256), BF), pltpu.VMEM((HALF * 128, D), BF)],
            flops=2 * RING * D * 128 * HALF * 6, moved=12 << 20,
        )

    pay_oth, mix_oth, d_gu_oth, wact_oth = experts(exts_oth, c_oth)
    pay_in = lax.ppermute(pay_oth, "core", swap)
    mix_in = lax.ppermute(mix_oth, "core", swap)
    pay, mix, d_gu, wact = experts(exts, c_all)
    part = call(add_kernel, "add_pay", [sds((TOK, D + 128), BF)] * 4, (pay, pay_in), moved=5 << 20)
    back = ring_return(part, "x")
    (grads,) = call(
        expert_grads_kernel, "expert_grads", [sds((2, 4, 4, HALF, 96, 128), BF)],
        (*exts, *exts_oth, c_all, c_oth, d_gu, d_gu_oth, wact, wact_oth, part[0]), in_specs=[VMEM] * 14 + [ANY],
        scratch=[
            pltpu.VMEM((2 * RING, D), BF), pltpu.VMEM((2 * RING, D), BF),
            pltpu.VMEM((2 * RING, HALF * 256), BF), pltpu.VMEM((2 * RING, HALF * 128), BF),
        ],
        flops=2 * RING * D * 128 * HALF * 6, moved=20 << 20,
    )
    d_middle, d_low, g_misc = call(
        middle_back_kernel, "middle_back", [sds((TOK, D), F32), block, sds((16, D), F32)],
        (at, *back, middle, ext, gates, kept, cotangent, own, oth, grads), in_specs=[SMEM] + [VMEM] * 11 + [ANY],
        scratch=[misc_scr], flops=100 * 10**9, moved=4 << 20,
    )
    d_mid = ring_gather(d_low, "x")
    e = lax.psum_scatter(grads.reshape(8, 4, HALF, 96, 128), ("zl", "y"), scatter_dimension=0, tiled=False)
    *part, a_mine, a_send = call(
        attention_back_kernel, "attention_back", [sds((2 * TOK, D), BF)] * 4 + [sds((4, 4, SMALL, 128), BF)] * 2,
        (at, *d_mid, *tok, *att, h1, qk, vv, own, oth, cosine, sine, g_misc, mix, mix_in),
        in_specs=[SMEM] + [VMEM] * 22, out_specs=[VMEM] * 4 + [ANY] * 2,
        scratch=[
            pltpu.VMEM((D, 512), BF), pltpu.VMEM((256, D), BF), pltpu.VMEM((RING, D), BF), pltpu.VMEM((RING, 256), BF),
            pltpu.VMEM((RING, 512), BF), pltpu.VMEM((2, 4, 4, SMALL, 128), BF), pltpu.SemaphoreType.DMA((2,)),
        ],
        flops=10 * 10**9, moved=12 << 20,
    )

    a = lax.ppermute(a_send, "core", swap)
    (a,) = call(add_small_kernel, "add_small", [sds((4, 4, SMALL, 128), BF)], (a_mine, a), moved=3 << 20)
    (e,) = call(hold_kernel, "hold", [sds((4, HALF, 96, 128), BF)], (e, a), in_specs=[VMEM, ANY], moved=1 << 20)
    e = lax.psum_scatter(e, "zh", scatter_dimension=0, tiled=False)
    a = lax.all_to_all(a, "y", 0, 0, tiled=True)
    back = ring_return(part, "x")
    (e,) = call(hold_kernel, "hold_last", [sds((HALF, 96, 128), BF)], (e, *(a, *back[1:])), in_specs=[VMEM] + [ANY] * len((a, *back[1:])), moved=1 << 18)
    pairs = [(a, b) for a in range(2) for b in range(2)]
    first = lax.ppermute(e, ("core", "zl"), [(a * 2 + b, b * 2 + a) for a, b in pairs])
    second = lax.ppermute(e, ("core", "zl"), [(a * 2 + b, b * 2 + 1 - a) for a, b in pairs])
    e_last = jnp.stack([first, second])
    e = lax.all_gather(e_last, ("x", "y"), axis=0).reshape(4, 4, 2, HALF, 96, 128)
    grad_tokens, layer_out = call(
        tokens_kernel, "tokens", [block] * 2, (at, *back, tokens, d_middle, middle, own, oth, e_last),
        in_specs=[SMEM] + [VMEM] * 9 + [ANY], scratch=[misc_scr], moved=6 << 20,
    )
    (a,) = call(
        sum_twice_kernel, "sum_twice", [sds((8, SMALL, 128), BF)], (a, grad_tokens), in_specs=[VMEM, ANY], moved=2 << 20
    )
    a = lax.all_to_all(a, ("zh", "zl"), 0, 0, tiled=True)
    (a,) = call(sum_spread_kernel, "sum_spread", [sds((16, SMALL, 128), BF)], (a,), moved=2 << 20)
    a = lax.all_to_all(a, ("x", "y"), 0, 0, tiled=True).reshape(4, 4, SMALL, 128)
    grad_qkv, grad_out, g_misc = call(
        spread_small_kernel, "spread_small",
        [sds((128, 2048), F32), sds((1024, 128), F32), sds((16, 128), F32)], (a,), moved=3 << 20,
    )
    grad_gate_up, grad_down = spread(at[4:5], e)
    return (
        layer_out, grad_tokens, g_misc[10], g_misc[11], grad_qkv, grad_out, g_misc[:10].T, grad_gate_up, grad_down,
    )


def solution(mesh):
    fine = Mesh(mesh.devices.reshape(SIZES), AXES)
    rows = P(AXES, None)
    s = ("zh", "core")
    return jax.shard_map(
        local,
        mesh=fine,
        in_specs=(
            rows, rows, P(s), P(s), P(s, None), P(None, s), P(s, None), P(None, s, None), P(None, None, s), rows, rows,
        ),
        out_specs=(rows, rows, P(s), P(s), P(s, None), P(None, s), P(s, None), P(None, s, None), P(None, None, s)),
        check_vma=False,
    )
```

```python
import math

import jax
import jax.numpy as jnp
import numpy as np
from jax import lax
from jax.experimental import pallas as pl
from jax.experimental.pallas import tpu as pltpu
from jax.sharding import Mesh
from jax.sharding import PartitionSpec as P

D = 1024
HD = 64
TOPK = 8
EXPERTS = 10
CAP = 144
TOK = 160
RING = 4 * TOK
EPSILON = 1e-06
ROPE_BASE = 10000.0
SCALE = 1.0 / math.sqrt(HD)

AXES = ("zh", "core", "x", "zl", "y")
SIZES = (4, 2, 4, 2, 4)
BF = jnp.bfloat16
F32 = jnp.float32
VMEM = pl.BlockSpec(memory_space=pltpu.VMEM)
SMEM = pl.BlockSpec(memory_space=pltpu.SMEM)
ANY = pl.BlockSpec(memory_space=pl.ANY)
HBM = pl.BlockSpec(memory_space=pltpu.HBM)
SMALL = 208
PIECE = 584
RING_ORDER = (0, 1, 3, 2)
TICK = jax.ShapeDtypeStruct((8, 128), jnp.float32)
HALF = 5


def sds(shape, dtype):
    return jax.ShapeDtypeStruct(shape, dtype)


def call(kernel, name, outs, args, in_specs=None, out_specs=None, scratch=(), flops=0, moved=0, vmem=12):
    return pl.pallas_call(
        kernel,
        out_shape=tuple(outs),
        in_specs=in_specs or [VMEM] * len(args),
        out_specs=tuple(out_specs or [VMEM] * len(outs)),
        scratch_shapes=list(scratch),
        compiler_params=pltpu.CompilerParams(vmem_limit_bytes=vmem * 2**20),
        cost_estimate=pl.CostEstimate(flops=flops, bytes_accessed=moved, transcendentals=0),
        name=name,
    )(*args)


def mark(tick):
    tick[...] = jnp.zeros_like(tick)


def dot(a, b, ca=1, cb=0):
    return lax.dot_general(a, b, (((ca,), (cb,)), ((), ())), preferred_element_type=F32)


def take(v, axis, k):
    return lax.ppermute(v, axis, [((i + k) % 4, i) for i in range(4)])


def ring_gather(v, axis):
    return [v] + [take(v, axis, k) for k in (1, 3, 2)]


def ring_return(blocks, axis):
    return [blocks[0], take(blocks[2], axis, 1), take(blocks[1], axis, 3), take(blocks[3], axis, 2)]


def iota(shape, dim):
    return lax.broadcasted_iota(jnp.int32, shape, dim)


def rms(v):
    return lax.rsqrt(jnp.mean(v * v, axis=-1, keepdims=True) + EPSILON)


def rope_tables():
    half = HD // 2
    frequency = (ROPE_BASE ** (-np.arange(half, dtype=np.float32) / np.float32(half))).astype(np.float32)
    angles = np.arange(TOK, dtype=np.float32)[:, None] * frequency[None, :]
    cosine = np.cos(angles).astype(np.float32)
    sine = np.sin(angles).astype(np.float32)
    return np.tile(np.concatenate([cosine, cosine], 1), (1, 6)), np.tile(np.concatenate([-sine, sine], 1), (1, 6))


def rotate(v, cosine, sine):
    width = v.shape[1]
    first = (iota(v.shape, 1) % HD) < HD // 2
    other = jnp.where(first, pltpu.roll(v, width - HD // 2, 1), pltpu.roll(v, HD // 2, 1))
    return v * cosine + other * sine


def run_copies(copies, sem):
    started = [pltpu.make_async_copy(a, b, sem.at[n]) for n, (a, b) in enumerate(copies)]
    for c in started:
        c.start()
    for c in started:
        c.wait()


def pick_kernel(at, qkv, out, misc, small, sem):
    x = at[0]
    copies = [(misc, small.at[512:528]), (out.at[pl.ds(pl.multiple_of(x * 256, 256), 256), :], small.at[528:784])]
    for k, col in enumerate((x * 256, x * 256 + 128, 1024 + x * 128, 1536 + x * 128)):
        copies.append((qkv.at[:, pl.ds(pl.multiple_of(col, 128), 128)], small.at[k * 128 : k * 128 + 128]))
    run_copies(copies, sem)


def pick_experts_kernel(at, gu, dn, keep, send, sem):
    x, y, me = at[0], at[1], at[2]
    copies = []
    for half, to in ((me, keep), (1 - me, send)):
        some, rows = pl.ds(half * HALF, HALF), pl.ds(pl.multiple_of(y * 32, 32), 32)
        copies.append((gu.at[some, rows, pl.ds(pl.multiple_of(x * 128, 128), 128)], to.at[:, 0:32]))
        copies.append((gu.at[some, rows, pl.ds(pl.multiple_of(512 + x * 128, 128), 128)], to.at[:, 32:64]))
        copies.append((dn.at[some, pl.ds(pl.multiple_of(x * 128 + y * 32, 32), 32), :], to.at[:, 64:96]))
    run_copies(copies, sem)


def plan_kernel(routes, expert_row, order, routed_ref, kept_ref):
    pairs = TOK * TOPK
    place = jnp.where(iota((pairs, pairs), 0) == order[...], 1.0, 0.0).astype(BF)
    named = jnp.where(iota((16, pairs), 0) == expert_row[...], 1.0, 0.0).astype(BF)
    ordered = dot(named, place)
    before = jnp.where(iota((pairs, pairs), 0) < iota((pairs, pairs), 1), 1.0, 0.0).astype(BF)
    earlier = dot(ordered.astype(BF), before)
    kept = jnp.where(earlier < CAP, ordered, 0.0).astype(BF)
    kept_pair = dot(kept, place, 1, 1).astype(BF)
    token = iota((TOK, pairs), 0) * TOPK
    pair = iota((TOK, pairs), 1)
    owner = jnp.where((pair >= token) & (pair < token + TOPK), 1.0, 0.0).astype(BF)
    kept_ref[...] = dot(owner, kept_pair, 1, 1)
    lane = iota((TOK, 16), 1)
    routed = jnp.zeros((TOK, 16), F32)
    for r in range(TOPK):
        routed = routed + jnp.where(routes[:, r : r + 1] == lane, 1.0, 0.0)
    routed_ref[...] = routed


def place_of(at, k, r):
    return k * 2 + (at[2] + r) % 2


def load_misc(at, own, oth, scr):
    for r, ref in ((0, own), (1, oth)):
        for k in range(4):
            scr[place_of(at, k, r)] = ref[k, 512:528, :]
    return jnp.concatenate([scr[s] for s in range(8)], axis=1)


def load_w_att(at, own, oth, scr):
    for r, ref in ((0, own), (1, oth)):
        for k in range(4):
            row = pl.multiple_of(place_of(at, k, r) * 128, 128)
            for t in range(4):
                scr[pl.ds(row, 128), t * 128 : t * 128 + 128] = ref[k, t * 128 : t * 128 + 128, :]


def load_w_out(at, own, oth, scr):
    for r, piece in ((0, own), (1, oth)):
        for k in range(4):
            col = pl.multiple_of(place_of(at, k, r) * 128, 128)
            scr[:, pl.ds(col, 128)] = piece(k)


def softmax_of(q, k):
    scores = dot(q, k, 1, 1) * SCALE
    n = q.shape[0]
    row = iota((n, TOK), 0)
    row = jnp.where(row >= TOK, row - TOK, row)
    scores = jnp.where(row >= iota((n, TOK), 1), scores, -1e30)
    e = jnp.exp(scores - jnp.max(scores, axis=-1, keepdims=True))
    return e / jnp.sum(e, axis=-1, keepdims=True)


def pair_of(v, kv):
    return jnp.concatenate([v[:, kv * 128 : kv * 128 + HD], v[:, kv * 128 + HD : kv * 128 + 128]], axis=0)


def unpair(v):
    return jnp.concatenate([v[:TOK], v[TOK:]], axis=1)


def attention_kernel(at, t0, t1, t2, t3, own, oth, cosine, sine, h1, qk, vv, a0, a1, a2, a3, c_all, tick, w, misc_scr):
    mark(tick)
    load_w_att(at, own, oth, w)
    gain = load_misc(at, own, oth, misc_scr)[10:11].astype(F32)
    for s, t in enumerate((t0, t1, t2, t3)):
        x = t[0].astype(F32)
        h1[s * TOK : s * TOK + TOK] = (x * rms(x) * gain).astype(BF)
        c_all[s * TOK : s * TOK + TOK] = t[1]
    for s, a in enumerate((a0, a1, a2, a3)):
        rows = slice(s * TOK, s * TOK + TOK)
        qkv = dot(h1[rows], w[...])
        turned = rotate(qkv[:, :384], cosine[...], sine[...]).astype(BF)
        values = qkv[:, 384:].astype(BF)
        qk[rows] = turned
        vv[rows] = values
        heads = []
        for kv in range(2):
            k = turned[:, 256 + kv * HD : 256 + kv * HD + HD]
            v = values[:, kv * HD : kv * HD + HD]
            probs = softmax_of(pair_of(turned, kv), k).astype(BF)
            heads.append(unpair(dot(probs, v)))
        a[...] = jnp.concatenate(heads, axis=1).astype(BF)


def middle_kernel(
    at, tok, a0, a1, a2, a3, o0, o1, o2, o3, v, own, oth, routed, kept, middle, ext, gates_ref, w, misc_scr
):
    misc = load_misc(at, own, oth, misc_scr)
    m = tok[...].astype(F32)
    for n, (a, o) in enumerate(((a0, o0), (a1, o1), (a2, o2), (a3, o3))):
        load_w_out(at, lambda k: o[k], (lambda k: oth[k, 528:784]) if n == 0 else (lambda k: v[n - 1, k]), w)
        m = m + dot(a[...], w[...])
    middle[...] = m
    h2 = (m * rms(m) * misc[11:12].astype(F32)).astype(BF)
    ext[:, :D] = h2
    logits = dot(h2, misc, 1, 1)
    named = routed[...] > 0.5
    e = jnp.where(named, logits, -1e30)
    e = jnp.where(named, jnp.exp(e - jnp.max(e, axis=-1, keepdims=True)), 0.0)
    gates = e / jnp.sum(e, axis=-1, keepdims=True)
    gates_ref[...] = gates
    weight = gates * kept[...]
    high = weight.astype(BF).astype(F32)
    ext[:, D:] = jnp.concatenate([high, weight - high, jnp.zeros((TOK, 96), F32)], axis=1).astype(BF)


def load_w_gu(at, ex, w):
    for r in range(2):
        core = (at[2] + r) % 2
        for zh in range(4):
            for y in range(4):
                row = pl.multiple_of((zh * 2 + core) * 128 + y * 32, 32)
                for e in range(HALF):
                    w[pl.ds(row, 32), e * 256 : e * 256 + 128] = ex[zh, y, r, e, 0:32, :]
                    w[pl.ds(row, 32), e * 256 + 128 : e * 256 + 256] = ex[zh, y, r, e, 32:64, :]


def load_w_dn(at, ex, w):
    for r in range(2):
        core = (at[2] + r) % 2
        for zh in range(4):
            col = pl.multiple_of((zh * 2 + core) * 128, 128)
            for y in range(4):
                for e in range(HALF):
                    w[e * 128 + y * 32 : e * 128 + y * 32 + 32, pl.ds(col, 128)] = ex[zh, y, r, e, 64:96, :]


def column(v, lane, e):
    return jnp.sum(jnp.where(lane == e, v, 0.0), axis=1, keepdims=True)


def assemble_kernel(at, ex, wg, wd):
    load_w_gu(at, ex, wg)
    load_w_dn(at, ex, wd)


def experts_kernel(at, e0, e1, e2, e3, c, wg, wd, pay, mix, d_gu, wact, h2):
    weight = []
    for s, e in enumerate((e0, e1, e2, e3)):
        h2[s * TOK : s * TOK + TOK] = e[:, :D]
        extra = e[:, D:].astype(F32)
        weight.append(extra[:, :16] + extra[:, 16:32])
    weight = jnp.concatenate(weight, axis=0)
    lane = iota((RING, 16), 1)
    dg = jnp.zeros((RING, 16), F32)
    for e in range(HALF):
        gu = dot(h2[...], wg[:, e * 256 : e * 256 + 256])
        cw = dot(c[...], wd[e * 128 : e * 128 + 128], 1, 1)
        g, u = gu[:, :128], gu[:, 128:]
        sig = 1.0 / (1.0 + jnp.exp(-g))
        silu = g * sig
        act = (silu * u).astype(BF).astype(F32)
        wt = column(weight, lane, at[2] * HALF + e)
        d_act = cw * wt
        d_gu[:, e * 256 : e * 256 + 128] = (d_act * u * sig * (1.0 + g * (1.0 - sig))).astype(BF)
        d_gu[:, e * 256 + 128 : e * 256 + 256] = (d_act * silu).astype(BF)
        wact[:, e * 128 : e * 128 + 128] = (act * wt).astype(BF)
        dg = dg + jnp.where(lane == at[2] * HALF + e, jnp.sum(act * cw, axis=1, keepdims=True), 0.0)
    pay[:, :D] = dot(d_gu[...], wg[...], 1, 1).astype(BF)
    high = dg.astype(BF).astype(F32)
    pay[:, D:] = jnp.concatenate([high, dg - high, jnp.zeros((RING, 96), F32)], axis=1).astype(BF)
    mix[...] = dot(wact[...], wd[...]).astype(BF)


def add_kernel(a, b, *outs):
    mark(outs[-1])
    for s, o in enumerate(outs[:-1]):
        rows = slice(s * TOK, s * TOK + TOK)
        o[...] = (a[rows].astype(F32) + b[rows].astype(F32)).astype(BF)


def expert_grads_kernel(h2, h2_oth, c, c_oth, d_gu, d_gu_oth, wact, wact_oth, after, grads, tick):
    mark(tick)
    for e in range(HALF):
        cols = slice(e * 256, e * 256 + 256)
        g = (dot(h2[...], d_gu[:, cols], 0, 0) + dot(h2_oth[...], d_gu_oth[:, cols], 0, 0)).astype(BF)
        for zh in range(4):
            for core in range(2):
                for y in range(4):
                    s = (zh * 2 + core) * 128 + y * 32
                    grads[core, y, zh, e, 0:32, :] = g[s : s + 32, 0:128]
                    grads[core, y, zh, e, 32:64, :] = g[s : s + 32, 128:256]
        cols = slice(e * 128, e * 128 + 128)
        g = (dot(wact[:, cols], c[...], 0, 0) + dot(wact_oth[:, cols], c_oth[...], 0, 0)).astype(BF)
        for zh in range(4):
            for core in range(2):
                s = (zh * 2 + core) * 128
                for y in range(4):
                    grads[core, y, zh, e, 64:96, :] = g[y * 32 : y * 32 + 32, s : s + 128]


def hold_mark_kernel(v, after, out, tick):
    mark(tick)
    out[...] = v[...]


def hold_kernel(v, *rest):
    rest[-1][...] = v[...]


def stack_out_kernel(o1, o2, o3, after, out):
    for k, o in enumerate((o1, o2, o3)):
        out[k] = o[...]


def sum_of(v):
    total = v[0].astype(F32)
    for k in range(1, v.shape[0]):
        total = total + v[k].astype(F32)
    return total


def add_small_kernel(a, b, out, tick):
    mark(tick)
    out[...] = (a[...].astype(F32) + b[...].astype(F32)).astype(BF)


def sum_twice_kernel(v, after_one, after_two, after_three, out):
    total = sum_of(v).astype(BF)
    for zh in range(4):
        out[2 * zh] = total[zh]
        out[2 * zh + 1] = total[zh]


def middle_back_kernel(at, b0, b1, b2, b3, middle, ext, gates_ref, kept, cot, own, oth, after, d_middle, d_low, g_misc, misc_scr):
    misc = load_misc(at, own, oth, misc_scr)
    lane = iota((16, D), 0)
    back = b0[...].astype(F32) + b1[...].astype(F32) + b2[...].astype(F32) + b3[...].astype(F32)
    gates = gates_ref[...]
    d_gates = (back[:, D : D + 16] + back[:, D + 16 : D + 32]) * kept[...]
    d_logits = (gates * (d_gates - jnp.sum(gates * d_gates, axis=1, keepdims=True))).astype(BF)
    g_router = dot(d_logits, ext[:, :D], 0, 0)
    d_h2 = back[:, :D] + dot(d_logits, misc)
    m = middle[...]
    rstd = rms(m)
    norm = m * rstd
    g_gain = jnp.sum(d_h2 * norm, axis=0, keepdims=True)
    g_misc[...] = jnp.where(lane == 11, g_gain, g_router)
    u = d_h2 * misc[11:12].astype(F32)
    d = cot[...].astype(F32) + rstd * (u - norm * jnp.mean(u * norm, axis=-1, keepdims=True))
    d_middle[...] = d
    d_low[...] = d.astype(BF)


def attention_back_kernel(
    at, m0, m1, m2, m3, t0, t1, t2, t3, a0, a1, a2, a3, h1, qk, vv, own, oth, cosine, sine, g_in, mix, mix_in,
    p0, p1, p2, p3, mine, send, w, wo, dm, att, dqkv, grads, sem,
):
    me = at[2]
    load_w_att(at, own, oth, w)
    load_w_out(at, lambda k: own[k, 528:784], lambda k: oth[k, 528:784], wo)
    for s, (m, a) in enumerate(((m0, a0), (m1, a1), (m2, a2), (m3, a3))):
        rows = slice(s * TOK, s * TOK + TOK)
        dm[rows] = m[...]
        att[rows] = a[...]
    for s in range(4):
        rows = slice(s * TOK, s * TOK + TOK)
        d_att = dot(dm[rows], wo[...], 1, 1).astype(BF)
        turned, values = qk[rows], vv[rows]
        dq, dk, dv = [], [], []
        for kv in range(2):
            k = turned[:, 256 + kv * HD : 256 + kv * HD + HD]
            v = values[:, kv * HD : kv * HD + HD]
            q = pair_of(turned, kv)
            da = pair_of(d_att, kv)
            p = softmax_of(q, k)
            dp = dot(da, v, 1, 1)
            dv.append(dot(p.astype(BF), da, 0, 0))
            ds = (p * (dp - jnp.sum(p * dp, axis=-1, keepdims=True))).astype(BF)
            dq.append(unpair(dot(ds, k)) * SCALE)
            dk.append(dot(ds, q, 0, 0) * SCALE)
        turned = rotate(jnp.concatenate(dq + dk, axis=1), cosine[...], -sine[...])
        dqkv[rows] = jnp.concatenate([turned] + dv, axis=1).astype(BF)
    g = dot(h1[...], dqkv[...], 0, 0).astype(BF)
    for y in range(4):
        for zh in range(4):
            for cc in range(2):
                s = (zh * 2 + cc) * 128
                grads[(cc + me) % 2, y, zh, 0:128, :] = g[s : s + 128, y * 128 : y * 128 + 128]
    g = dot(att[...], dm[...], 0, 0).astype(BF)
    for y in range(4):
        for zh in range(4):
            for cc in range(2):
                s = (zh * 2 + cc) * 128
                grads[(cc + me) % 2, y, zh, 128:192, :] = g[y * 64 : y * 64 + 64, s : s + 128]
    gain = jnp.zeros((1, D), F32)
    for s, (t, p) in enumerate(((t0, p0), (t1, p1), (t2, p2), (t3, p3))):
        d_h1 = dot(dqkv[s * TOK : s * TOK + TOK], w[...], 1, 1)
        x = t[0].astype(F32)
        gain = gain + jnp.sum(d_h1 * (x * rms(x)), axis=0, keepdims=True)
        p[:TOK] = d_h1.astype(BF)
        rows = slice(s * TOK, s * TOK + TOK)
        p[TOK:] = (mix[rows].astype(F32) + mix_in[rows].astype(F32)).astype(BF)
    g = jnp.where(iota((16, D), 0) == 10, gain, g_in[...]).astype(BF)
    for zh in range(4):
        for cc in range(2):
            s = (zh * 2 + cc) * 128
            grads[(cc + me) % 2, 0, zh, 192:SMALL, :] = g[:, s : s + 128]
            for y in range(1, 4):
                grads[(cc + me) % 2, y, zh, 192:SMALL, :] = jnp.zeros((16, 128), BF)
    to_mine = pltpu.make_async_copy(grads.at[0], mine, sem.at[0])
    to_send = pltpu.make_async_copy(grads.at[1], send, sem.at[1])
    to_mine.start()
    to_send.start()
    to_mine.wait()
    to_send.wait()


def tokens_kernel(at, b0, b1, b2, b3, tok, d_middle, middle, own, oth, out, layer, tick, misc_scr):
    mark(tick)
    gain = load_misc(at, own, oth, misc_scr)[10:11].astype(F32)
    total = b0[...].astype(F32) + b1[...].astype(F32) + b2[...].astype(F32) + b3[...].astype(F32)
    layer[...] = (middle[...] + total[TOK:]).astype(BF)
    u = total[:TOK] * gain
    x = tok[...].astype(F32)
    rstd = rms(x)
    norm = x * rstd
    out[...] = (d_middle[...] + rstd * (u - norm * jnp.mean(u * norm, axis=-1, keepdims=True))).astype(BF)


def pack_kernel(first, second, a, one, two):
    total = sum_of(a).astype(BF)
    for half, v, out in ((0, first, one), (1, second, two)):
        for k in range(HALF):
            out[k * 96 : k * 96 + 96] = v[k]
        out[480:PIECE] = total[half * 104 : half * 104 + 104]


def stack_two_kernel(a0, a1, a2, a3, b0, b1, b2, b3, one, two):
    for k, (a, b) in enumerate(((a0, b0), (a1, b1), (a2, b2), (a3, b3))):
        one[k] = a[...]
        two[k] = b[...]


def expert_places(at, s, t):
    for k in range(4):
        for n in range(4):
            far, near = RING_ORDER[k], RING_ORDER[n]
            yield 0, s[k], n, (at[0] + near) % 4, (at[1] + far) % 4
            yield 1, t[k], n, (at[0] + far) % 4, (at[1] + near) % 4


def spread_kernel(at, s0, s1, s2, s3, t0, t1, t2, t3, gu_out, dn_out, gu, dn, sem):
    outward = []
    for half in range(2):
        for r, v, n, x, y in expert_places(at, (s0, s1, s2, s3), (t0, t1, t2, t3)):
            if r != half:
                continue
            rows = pl.ds(pl.multiple_of(y * 32, 32), 32)
            row = pl.ds(pl.multiple_of(x * 128 + y * 32, 32), 32)
            for k in range(HALF):
                gu[r, k, rows, pl.ds(pl.multiple_of(x * 128, 128), 128)] = v[n, k * 96 : k * 96 + 32].astype(F32)
                gu[r, k, rows, pl.ds(pl.multiple_of(512 + x * 128, 128), 128)] = v[n, k * 96 + 32 : k * 96 + 64].astype(F32)
                dn[r, k, row] = v[n, k * 96 + 64 : k * 96 + 96].astype(F32)
        some = pl.ds(((at[4] + half) % 2) * HALF, HALF)
        outward.append(pltpu.make_async_copy(gu.at[half], gu_out.at[some], sem.at[2 * half]))
        outward.append(pltpu.make_async_copy(dn.at[half], dn_out.at[some], sem.at[2 * half + 1]))
        outward[-2].start()
        outward[-1].start()
    for copy in outward:
        copy.wait()


def spread_small_kernel(at, s0, s1, s2, s3, t0, t1, t2, t3, qkv, out, misc, whole):
    for r, v, n, x, y in expert_places(at, (s0, s1, s2, s3), (t0, t1, t2, t3)):
        whole[x * 4 + y, r * 104 : r * 104 + 104] = v[n, 480:PIECE]
    for x in range(4):
        for y in range(4):
            c = x * 256 + y * 128 if y < 2 else y * 512 + x * 128
            qkv[:, c : c + 128] = whole[x * 4 + y, 0:128].astype(F32)
            out[x * 256 + y * 64 : x * 256 + y * 64 + 64] = whole[x * 4 + y, 128:192].astype(F32)
    m = whole[0, 192:SMALL].astype(F32)
    for x in range(1, 4):
        m = m + whole[x * 4, 192:SMALL].astype(F32)
    misc[...] = m


def local(tokens, cotangent, gain_one, gain_two, w_qkv, w_out, w_router, w_gate_up, w_down, routes, slot_order):
    at = jnp.stack([lax.axis_index(a) for a in ("x", "y", "core", "zh", "zl")]).astype(jnp.int32)
    swap = [(0, 1), (1, 0)]
    cosine, sine = (jnp.asarray(t) for t in rope_tables())

    misc = jnp.concatenate([w_router.T, gain_one[None], gain_two[None], jnp.zeros((4, 128), BF)], axis=0)
    (small,) = call(
        pick_kernel, "pick", [sds((784, 128), BF)], (at, w_qkv, w_out, misc),
        in_specs=[SMEM] + [ANY] * 3, scratch=[pltpu.SemaphoreType.DMA((6,))], moved=1 << 19,
    )
    keep, send = call(
        pick_experts_kernel, "pick_experts", [sds((HALF, 96, 128), BF)] * 2, (at, w_gate_up, w_down),
        in_specs=[SMEM] + [ANY] * 2, scratch=[pltpu.SemaphoreType.DMA((6,))], moved=1 << 19,
    )
    ex = jnp.stack([keep, lax.ppermute(send, "core", swap)])
    ex = lax.all_gather(ex, ("zh", "y"), axis=0).reshape(4, 4, 2, HALF, 96, 128)
    tok = ring_gather(jnp.stack([tokens, cotangent]), "x")
    own = lax.all_gather(small, "zh", axis=0)
    (own,) = call(hold_kernel, "stack", [sds((4, 784, 128), BF)], (own, *tok[1:]), in_specs=[VMEM] + [ANY] * 3, moved=2 << 20)
    oth = lax.ppermute(own, "core", swap)
    w_o = ring_gather(own[:, 528:], "x")

    routed, kept = call(
        plan_kernel, "plan", [sds((TOK, 16), F32)] * 2,
        (routes, routes.reshape(1, TOK * TOPK), slot_order), flops=2 * 1280 * 1280 * 64, moved=1 << 20, vmem=32,
    )
    misc_scr = pltpu.VMEM((8, 16, 128), BF)
    block = sds((TOK, D), BF)
    h1, qk, vv, *att, c_all, tick = call(
        attention_kernel, "attention",
        [sds((RING, D), BF), sds((RING, 384), BF), sds((RING, 128), BF)] + [sds((TOK, 256), BF)] * 4 + [sds((RING, D), BF), TICK],
        (at, *tok, own, oth, cosine, sine), in_specs=[SMEM] + [VMEM] * 8,
        scratch=[pltpu.VMEM((D, 512), BF), misc_scr], flops=2 * RING * D * 512 * 2, moved=10 << 20, vmem=16,
    )
    att_home = ring_return(att, "x")
    (w_o_oth,) = call(
        stack_out_kernel, "stack_out", [sds((3, 4, 256, 128), BF)], (*w_o[1:], tick), in_specs=[VMEM] * 3 + [ANY], moved=2 << 20,
    )
    w_o_oth = lax.ppermute(w_o_oth, "core", swap)
    c_oth = lax.ppermute(c_all, "core", swap)
    middle, ext, gates = call(
        middle_kernel, "middle", [sds((TOK, D), F32), sds((TOK, D + 128), BF), sds((TOK, 16), F32)],
        (at, tokens, *att_home, *w_o, w_o_oth, own, oth, routed, kept),
        in_specs=[SMEM] + [VMEM] * 14,
        scratch=[pltpu.VMEM((256, D), BF), misc_scr], flops=2 * TOK * D * D, moved=8 << 20,
    )
    exts = ring_gather(ext, "x")
    exts_oth = [lax.ppermute(e, "core", swap) for e in exts]

    wg, wd = call(
        assemble_kernel, "assemble", [sds((D, HALF * 256), BF), sds((HALF * 128, D), BF)], (at, ex), in_specs=[SMEM, VMEM],
        flops=30 * 10**9, moved=8 << 20,
    )

    def experts(pieces, c):
        return call(
            experts_kernel, "experts",
            [
                sds((RING, D + 128), BF), sds((RING, D), BF), sds((RING, HALF * 256), BF), sds((RING, HALF * 128), BF),
                sds((RING, D), BF),
            ],
            (at, *pieces, c, wg, wd), in_specs=[SMEM] + [VMEM] * 7,
            flops=2 * RING * D * 128 * HALF * 6, moved=12 << 20, vmem=20,
        )

    pay_oth, mix_oth, d_gu_oth, wact_oth, h2_oth = experts(exts_oth, c_oth)
    pay_in = lax.ppermute(pay_oth, "core", swap)
    mix_in = lax.ppermute(mix_oth, "core", swap)
    pay, mix, d_gu, wact, h2 = experts(exts, c_all)
    *part, tick = call(add_kernel, "add_pay", [sds((TOK, D + 128), BF)] * 4 + [TICK], (pay, pay_in), moved=5 << 20)
    back = ring_return(part, "x")
    grads, tick = call(
        expert_grads_kernel, "expert_grads", [sds((2, 4, 4, HALF, 96, 128), BF), TICK],
        (h2, h2_oth, c_all, c_oth, d_gu, d_gu_oth, wact, wact_oth, tick), in_specs=[VMEM] * 8 + [ANY],
        flops=2 * RING * D * 128 * HALF * 6, moved=20 << 20, vmem=20,
    )
    d_middle, d_low, g_misc = call(
        middle_back_kernel, "middle_back", [sds((TOK, D), F32), block, sds((16, D), F32)],
        (at, *back, middle, ext, gates, kept, cotangent, own, oth, tick), in_specs=[SMEM] + [VMEM] * 11 + [ANY],
        scratch=[misc_scr], flops=100 * 10**9, moved=4 << 20,
    )
    d_mid = ring_gather(d_low, "x")
    e = lax.psum_scatter(grads.reshape(8, 4, HALF, 96, 128), ("zl", "y"), scatter_dimension=0, tiled=False)
    *part, a_mine, a_send = call(
        attention_back_kernel, "attention_back", [sds((2 * TOK, D), BF)] * 4 + [sds((4, 4, SMALL, 128), BF)] * 2,
        (at, *d_mid, *tok, *att, h1, qk, vv, own, oth, cosine, sine, g_misc, mix, mix_in),
        in_specs=[SMEM] + [VMEM] * 22, out_specs=[VMEM] * 4 + [ANY] * 2,
        scratch=[
            pltpu.VMEM((D, 512), BF), pltpu.VMEM((256, D), BF), pltpu.VMEM((RING, D), BF), pltpu.VMEM((RING, 256), BF),
            pltpu.VMEM((RING, 512), BF), pltpu.VMEM((2, 4, 4, SMALL, 128), BF), pltpu.SemaphoreType.DMA((2,)),
        ],
        flops=10 * 10**9, moved=12 << 20, vmem=26,
    )

    back = ring_return(part, "x")
    a = lax.ppermute(a_send, "core", swap)
    a, tick = call(add_small_kernel, "add_small", [sds((4, 4, SMALL, 128), BF), TICK], (a_mine, a), moved=3 << 20)
    a = lax.all_to_all(a, "y", 0, 0, tiled=True)
    e, tick = call(
        hold_mark_kernel, "hold", [sds((4, HALF, 96, 128), BF), TICK], (e, tick), in_specs=[VMEM, ANY], moved=1 << 20
    )
    e = lax.psum_scatter(e, "zh", scatter_dimension=0, tiled=False)
    (a,) = call(
        sum_twice_kernel, "sum_twice", [sds((8, SMALL, 128), BF)], (a, back[1], back[2], tick), in_specs=[VMEM] + [ANY] * 3,
        moved=2 << 20,
    )
    a = lax.all_to_all(a, ("zh", "zl"), 0, 0, tiled=True)
    grad_tokens, layer_out, tick = call(
        tokens_kernel, "tokens", [block, block, TICK], (at, *back, tokens, d_middle, middle, own, oth),
        in_specs=[SMEM] + [VMEM] * 9, scratch=[misc_scr], moved=6 << 20,
    )
    (e,) = call(hold_kernel, "hold_last", [sds((HALF, 96, 128), BF)], (e, tick), in_specs=[VMEM, ANY], moved=1 << 18)
    pairs = [(a, b) for a in range(2) for b in range(2)]
    first = lax.ppermute(e, ("core", "zl"), [(a * 2 + b, b * 2 + a) for a, b in pairs])
    second = lax.ppermute(e, ("core", "zl"), [(a * 2 + b, b * 2 + 1 - a) for a, b in pairs])
    piece = sds((PIECE, 128), BF)
    one, two = call(pack_kernel, "pack", [piece] * 2, (first, second, a), moved=1 << 20)
    one, two = ring_gather(one, "x"), ring_gather(two, "y")
    one, two = call(stack_two_kernel, "stack_two", [sds((4, PIECE, 128), BF)] * 2, (*one, *two), moved=2 << 20)
    spread = (*ring_gather(one, "y"), *ring_gather(two, "x"))
    grad_qkv, grad_out, g_misc = call(
        spread_small_kernel, "spread_small", [sds((128, 2048), F32), sds((1024, 128), F32), sds((16, 128), F32)], (at, *spread),
        in_specs=[SMEM] + [VMEM] * 8, scratch=[pltpu.VMEM((16, SMALL, 128), BF)], moved=3 << 20,
    )
    grad_gate_up, grad_down = call(
        spread_kernel, "spread", [sds((EXPERTS, 128, 1024), F32), sds((EXPERTS, 512, 128), F32)], (at, *spread),
        in_specs=[SMEM] + [VMEM] * 8, out_specs=[ANY] * 2,
        scratch=[pltpu.VMEM((2, HALF, 128, 1024), F32), pltpu.VMEM((2, HALF, 512, 128), F32), pltpu.SemaphoreType.DMA((4,))],
        moved=12 << 20, vmem=18,
    )
    return (
        layer_out, grad_tokens, g_misc[10], g_misc[11], grad_qkv, grad_out, g_misc[:10].T, grad_gate_up, grad_down,
    )


def solution(mesh):
    fine = Mesh(mesh.devices.reshape(SIZES), AXES)
    rows = P(AXES, None)
    s = ("zh", "core")
    return jax.shard_map(
        local,
        mesh=fine,
        in_specs=(
            rows, rows, P(s), P(s), P(s, None), P(None, s), P(s, None), P(None, s, None), P(None, None, s), rows, rows,
        ),
        out_specs=(rows, rows, P(s), P(s), P(s, None), P(None, s), P(s, None), P(None, s, None), P(None, None, s)),
        check_vma=False,
    )
```

```python
import math

import jax
import jax.numpy as jnp
import numpy as np
from jax import lax
from jax.experimental import pallas as pl
from jax.experimental.pallas import tpu as pltpu
from jax.sharding import Mesh
from jax.sharding import PartitionSpec as P

D = 1024
HD = 64
TOPK = 8
EXPERTS = 10
CAP = 144
TOK = 160
RING = 4 * TOK
EPSILON = 1e-06
ROPE_BASE = 10000.0
SCALE = 1.0 / math.sqrt(HD)

AXES = ("zh", "core", "x", "zl", "y")
SIZES = (4, 2, 4, 2, 4)
BF = jnp.bfloat16
F32 = jnp.float32
VMEM = pl.BlockSpec(memory_space=pltpu.VMEM)
SMEM = pl.BlockSpec(memory_space=pltpu.SMEM)
ANY = pl.BlockSpec(memory_space=pl.ANY)
HBM = pl.BlockSpec(memory_space=pltpu.HBM)
SMALL = 224
SMALL_HALF = 112
PIECE = 592
RING_ORDER = (0, 1, 3, 2)
TICK = jax.ShapeDtypeStruct((8, 128), jnp.float32)
HALF = 5


def sds(shape, dtype):
    return jax.ShapeDtypeStruct(shape, dtype)


def call(kernel, name, outs, args, in_specs=None, out_specs=None, scratch=(), flops=0, moved=0, vmem=12):
    return pl.pallas_call(
        kernel,
        out_shape=tuple(outs),
        in_specs=in_specs or [VMEM] * len(args),
        out_specs=tuple(out_specs or [VMEM] * len(outs)),
        scratch_shapes=list(scratch),
        compiler_params=pltpu.CompilerParams(vmem_limit_bytes=vmem * 2**20),
        cost_estimate=pl.CostEstimate(flops=flops, bytes_accessed=moved, transcendentals=0),
        name=name,
    )(*args)


def mark(tick):
    tick[...] = jnp.zeros_like(tick)


def dot(a, b, ca=1, cb=0):
    return lax.dot_general(a, b, (((ca,), (cb,)), ((), ())), preferred_element_type=F32)


def take(v, axis, k):
    return lax.ppermute(v, axis, [((i + k) % 4, i) for i in range(4)])


def ring_gather(v, axis):
    return [v] + [take(v, axis, k) for k in (1, 3, 2)]


def ring_return(blocks, axis):
    return [blocks[0], take(blocks[2], axis, 1), take(blocks[1], axis, 3), take(blocks[3], axis, 2)]


def iota(shape, dim):
    return lax.broadcasted_iota(jnp.int32, shape, dim)


def rms(v):
    return lax.rsqrt(jnp.mean(v * v, axis=-1, keepdims=True) + EPSILON)


def rope_tables():
    half = HD // 2
    frequency = (ROPE_BASE ** (-np.arange(half, dtype=np.float32) / np.float32(half))).astype(np.float32)
    angles = np.arange(TOK, dtype=np.float32)[:, None] * frequency[None, :]
    cosine = np.cos(angles).astype(np.float32)
    sine = np.sin(angles).astype(np.float32)
    return np.tile(np.concatenate([cosine, cosine], 1), (1, 6)), np.tile(np.concatenate([-sine, sine], 1), (1, 6))


def rotate(v, cosine, sine):
    width = v.shape[1]
    first = (iota(v.shape, 1) % HD) < HD // 2
    other = jnp.where(first, pltpu.roll(v, width - HD // 2, 1), pltpu.roll(v, HD // 2, 1))
    return v * cosine + other * sine


def run_copies(copies, sem):
    started = [pltpu.make_async_copy(a, b, sem.at[n]) for n, (a, b) in enumerate(copies)]
    for c in started:
        c.start()
    for c in started:
        c.wait()


def pick_kernel(at, qkv, out, misc, small, sem):
    x = at[0]
    copies = [(misc, small.at[512:528]), (out.at[pl.ds(pl.multiple_of(x * 256, 256), 256), :], small.at[528:784])]
    for k, col in enumerate((x * 256, x * 256 + 128, 1024 + x * 128, 1536 + x * 128)):
        copies.append((qkv.at[:, pl.ds(pl.multiple_of(col, 128), 128)], small.at[k * 128 : k * 128 + 128]))
    run_copies(copies, sem)


def pick_experts_kernel(at, gu, dn, keep, send, sem):
    x, y, me = at[0], at[1], at[2]
    copies = []
    for half, to in ((me, keep), (1 - me, send)):
        some, rows = pl.ds(half * HALF, HALF), pl.ds(pl.multiple_of(y * 32, 32), 32)
        copies.append((gu.at[some, rows, pl.ds(pl.multiple_of(x * 128, 128), 128)], to.at[:, 0:32]))
        copies.append((gu.at[some, rows, pl.ds(pl.multiple_of(512 + x * 128, 128), 128)], to.at[:, 32:64]))
        copies.append((dn.at[some, pl.ds(pl.multiple_of(x * 128 + y * 32, 32), 32), :], to.at[:, 64:96]))
    run_copies(copies, sem)


def plan_kernel(routes, expert_row, order, routed_ref, kept_ref):
    pairs = TOK * TOPK
    place = jnp.where(iota((pairs, pairs), 0) == order[...], 1.0, 0.0).astype(BF)
    named = jnp.where(iota((16, pairs), 0) == expert_row[...], 1.0, 0.0).astype(BF)
    ordered = dot(named, place)
    before = jnp.where(iota((pairs, pairs), 0) < iota((pairs, pairs), 1), 1.0, 0.0).astype(BF)
    earlier = dot(ordered.astype(BF), before)
    kept = jnp.where(earlier < CAP, ordered, 0.0).astype(BF)
    kept_pair = dot(kept, place, 1, 1).astype(BF)
    token = iota((TOK, pairs), 0) * TOPK
    pair = iota((TOK, pairs), 1)
    owner = jnp.where((pair >= token) & (pair < token + TOPK), 1.0, 0.0).astype(BF)
    kept_ref[...] = dot(owner, kept_pair, 1, 1)
    lane = iota((TOK, 16), 1)
    routed = jnp.zeros((TOK, 16), F32)
    for r in range(TOPK):
        routed = routed + jnp.where(routes[:, r : r + 1] == lane, 1.0, 0.0)
    routed_ref[...] = routed


def place_of(at, k, r):
    return k * 2 + (at[2] + r) % 2


def load_misc(at, own, oth, scr):
    for r, ref in ((0, own), (1, oth)):
        for k in range(4):
            scr[place_of(at, k, r)] = ref[k, 512:528, :]
    return jnp.concatenate([scr[s] for s in range(8)], axis=1)


def load_w_att(at, own, oth, scr):
    for r, ref in ((0, own), (1, oth)):
        for k in range(4):
            row = pl.multiple_of(place_of(at, k, r) * 128, 128)
            for t in range(4):
                scr[pl.ds(row, 128), t * 128 : t * 128 + 128] = ref[k, t * 128 : t * 128 + 128, :]


def load_w_out(at, own, oth, scr):
    for r, piece in ((0, own), (1, oth)):
        for k in range(4):
            col = pl.multiple_of(place_of(at, k, r) * 128, 128)
            scr[:, pl.ds(col, 128)] = piece(k)


def softmax_of(q, k):
    scores = dot(q, k, 1, 1) * SCALE
    n = q.shape[0]
    row = iota((n, TOK), 0)
    row = jnp.where(row >= TOK, row - TOK, row)
    scores = jnp.where(row >= iota((n, TOK), 1), scores, -1e30)
    e = jnp.exp(scores - jnp.max(scores, axis=-1, keepdims=True))
    return e / jnp.sum(e, axis=-1, keepdims=True)


def pair_of(v, kv):
    return jnp.concatenate([v[:, kv * 128 : kv * 128 + HD], v[:, kv * 128 + HD : kv * 128 + 128]], axis=0)


def unpair(v):
    return jnp.concatenate([v[:TOK], v[TOK:]], axis=1)


def attention_kernel(at, t0, t1, t2, t3, own, oth, cosine, sine, h1, qk, vv, a0, a1, a2, a3, c_all, tick, w, misc_scr):
    mark(tick)
    load_w_att(at, own, oth, w)
    gain = load_misc(at, own, oth, misc_scr)[10:11].astype(F32)
    for s, t in enumerate((t0, t1, t2, t3)):
        x = t[0].astype(F32)
        h1[s * TOK : s * TOK + TOK] = (x * rms(x) * gain).astype(BF)
        c_all[s * TOK : s * TOK + TOK] = t[1]
    for s, a in enumerate((a0, a1, a2, a3)):
        rows = slice(s * TOK, s * TOK + TOK)
        qkv = dot(h1[rows], w[...])
        turned = rotate(qkv[:, :384], cosine[...], sine[...]).astype(BF)
        values = qkv[:, 384:].astype(BF)
        qk[rows] = turned
        vv[rows] = values
        heads = []
        for kv in range(2):
            k = turned[:, 256 + kv * HD : 256 + kv * HD + HD]
            v = values[:, kv * HD : kv * HD + HD]
            probs = softmax_of(pair_of(turned, kv), k).astype(BF)
            heads.append(unpair(dot(probs, v)))
        a[...] = jnp.concatenate(heads, axis=1).astype(BF)


def middle_kernel(
    at, tok, a0, a1, a2, a3, o0, o1, o2, o3, v, own, oth, routed, kept, middle, ext, gates_ref, w, misc_scr
):
    misc = load_misc(at, own, oth, misc_scr)
    m = tok[...].astype(F32)
    for n, (a, o) in enumerate(((a0, o0), (a1, o1), (a2, o2), (a3, o3))):
        load_w_out(at, lambda k: o[k], (lambda k: oth[k, 528:784]) if n == 0 else (lambda k: v[n - 1, k]), w)
        m = m + dot(a[...], w[...])
    middle[...] = m
    h2 = (m * rms(m) * misc[11:12].astype(F32)).astype(BF)
    ext[:, :D] = h2
    logits = dot(h2, misc, 1, 1)
    named = routed[...] > 0.5
    e = jnp.where(named, logits, -1e30)
    e = jnp.where(named, jnp.exp(e - jnp.max(e, axis=-1, keepdims=True)), 0.0)
    gates = e / jnp.sum(e, axis=-1, keepdims=True)
    gates_ref[...] = gates
    weight = gates * kept[...]
    high = weight.astype(BF).astype(F32)
    ext[:, D:] = jnp.concatenate([high, weight - high, jnp.zeros((TOK, 96), F32)], axis=1).astype(BF)


def load_w_gu(at, ex, w):
    for r in range(2):
        core = (at[2] + r) % 2
        for zh in range(4):
            for y in range(4):
                row = pl.multiple_of((zh * 2 + core) * 128 + y * 32, 32)
                for e in range(HALF):
                    w[pl.ds(row, 32), e * 256 : e * 256 + 128] = ex[zh, y, r, e, 0:32, :]
                    w[pl.ds(row, 32), e * 256 + 128 : e * 256 + 256] = ex[zh, y, r, e, 32:64, :]


def load_w_dn(at, ex, w):
    for r in range(2):
        core = (at[2] + r) % 2
        for zh in range(4):
            col = pl.multiple_of((zh * 2 + core) * 128, 128)
            for y in range(4):
                for e in range(HALF):
                    w[e * 128 + y * 32 : e * 128 + y * 32 + 32, pl.ds(col, 128)] = ex[zh, y, r, e, 64:96, :]


def column(v, lane, e):
    return jnp.sum(jnp.where(lane == e, v, 0.0), axis=1, keepdims=True)


def assemble_kernel(at, ex, wg, wd):
    load_w_gu(at, ex, wg)
    load_w_dn(at, ex, wd)


def experts_kernel(at, e0, e1, e2, e3, c, wg, wd, pay, mix, d_gu, wact, h2):
    weight = []
    for s, e in enumerate((e0, e1, e2, e3)):
        h2[s * TOK : s * TOK + TOK] = e[:, :D]
        extra = e[:, D:].astype(F32)
        weight.append(extra[:, :16] + extra[:, 16:32])
    weight = jnp.concatenate(weight, axis=0)
    lane = iota((RING, 16), 1)
    dg = jnp.zeros((RING, 16), F32)
    for e in range(HALF):
        gu = dot(h2[...], wg[:, e * 256 : e * 256 + 256])
        cw = dot(c[...], wd[e * 128 : e * 128 + 128], 1, 1)
        g, u = gu[:, :128], gu[:, 128:]
        sig = 1.0 / (1.0 + jnp.exp(-g))
        silu = g * sig
        act = (silu * u).astype(BF).astype(F32)
        wt = column(weight, lane, at[2] * HALF + e)
        d_act = cw * wt
        d_gu[:, e * 256 : e * 256 + 128] = (d_act * u * sig * (1.0 + g * (1.0 - sig))).astype(BF)
        d_gu[:, e * 256 + 128 : e * 256 + 256] = (d_act * silu).astype(BF)
        wact[:, e * 128 : e * 128 + 128] = (act * wt).astype(BF)
        dg = dg + jnp.where(lane == at[2] * HALF + e, jnp.sum(act * cw, axis=1, keepdims=True), 0.0)
    pay[:, :D] = dot(d_gu[...], wg[...], 1, 1).astype(BF)
    high = dg.astype(BF).astype(F32)
    pay[:, D:] = jnp.concatenate([high, dg - high, jnp.zeros((RING, 96), F32)], axis=1).astype(BF)
    mix[...] = dot(wact[...], wd[...]).astype(BF)


def add_kernel(a, b, *outs):
    mark(outs[-1])
    for s, o in enumerate(outs[:-1]):
        rows = slice(s * TOK, s * TOK + TOK)
        o[...] = (a[rows].astype(F32) + b[rows].astype(F32)).astype(BF)


def expert_grads_kernel(h2, h2_oth, c, c_oth, d_gu, d_gu_oth, wact, wact_oth, after, grads, tick):
    mark(tick)
    for e in range(HALF):
        cols = slice(e * 256, e * 256 + 256)
        g = (dot(h2[...], d_gu[:, cols], 0, 0) + dot(h2_oth[...], d_gu_oth[:, cols], 0, 0)).astype(BF)
        for zh in range(4):
            for core in range(2):
                for y in range(4):
                    s = (zh * 2 + core) * 128 + y * 32
                    grads[core, y, zh, e, 0:32, :] = g[s : s + 32, 0:128]
                    grads[core, y, zh, e, 32:64, :] = g[s : s + 32, 128:256]
        cols = slice(e * 128, e * 128 + 128)
        g = (dot(wact[:, cols], c[...], 0, 0) + dot(wact_oth[:, cols], c_oth[...], 0, 0)).astype(BF)
        for zh in range(4):
            for core in range(2):
                s = (zh * 2 + core) * 128
                for y in range(4):
                    grads[core, y, zh, e, 64:96, :] = g[y * 32 : y * 32 + 32, s : s + 128]


def hold_kernel(v, *rest):
    rest[-1][...] = v[...]


def stack_out_kernel(o1, o2, o3, after, out):
    for k, o in enumerate((o1, o2, o3)):
        out[k] = o[...]


def sum_of(v):
    total = v[0].astype(F32)
    for k in range(1, v.shape[0]):
        total = total + v[k].astype(F32)
    return total


def add_small_kernel(a, b, out):
    out[...] = (a[...].astype(F32) + b[...].astype(F32)).astype(BF)


def sum_four_kernel(v0, v1, v2, v3, e, a):
    total = (v0[...].astype(F32) + v1[...].astype(F32) + v2[...].astype(F32) + v3[...].astype(F32)).astype(BF)
    e[...] = total[:480]
    a[...] = total[480:]


def split_kernel(at, e, a, *outs):
    for k, out in zip(RING_ORDER, outs):
        zh = (at[3] + k) % 4
        for n in range(HALF):
            out[n * 96 : n * 96 + 96] = e[zh, n]
        total = a[0, zh].astype(F32)
        for n in range(1, 8):
            total = total + a[n, zh].astype(F32)
        out[480:PIECE] = total.astype(BF)


def middle_back_kernel(at, b0, b1, b2, b3, middle, ext, gates_ref, kept, cot, own, oth, after, d_middle, d_low, g_misc, misc_scr):
    misc = load_misc(at, own, oth, misc_scr)
    lane = iota((16, D), 0)
    back = b0[...].astype(F32) + b1[...].astype(F32) + b2[...].astype(F32) + b3[...].astype(F32)
    gates = gates_ref[...]
    d_gates = (back[:, D : D + 16] + back[:, D + 16 : D + 32]) * kept[...]
    d_logits = (gates * (d_gates - jnp.sum(gates * d_gates, axis=1, keepdims=True))).astype(BF)
    g_router = dot(d_logits, ext[:, :D], 0, 0)
    d_h2 = back[:, :D] + dot(d_logits, misc)
    m = middle[...]
    rstd = rms(m)
    norm = m * rstd
    g_gain = jnp.sum(d_h2 * norm, axis=0, keepdims=True)
    g_misc[...] = jnp.where(lane == 11, g_gain, g_router)
    u = d_h2 * misc[11:12].astype(F32)
    d = cot[...].astype(F32) + rstd * (u - norm * jnp.mean(u * norm, axis=-1, keepdims=True))
    d_middle[...] = d
    d_low[...] = d.astype(BF)


def attention_back_kernel(
    at, m0, m1, m2, m3, t0, t1, t2, t3, a0, a1, a2, a3, h1, qk, vv, own, oth, cosine, sine, g_in, mix, mix_in,
    parts, mine, send, w, wo, dm, att, dqkv, grads, sem,
):
    me = at[2]
    load_w_att(at, own, oth, w)
    load_w_out(at, lambda k: own[k, 528:784], lambda k: oth[k, 528:784], wo)
    for s, (m, a) in enumerate(((m0, a0), (m1, a1), (m2, a2), (m3, a3))):
        rows = slice(s * TOK, s * TOK + TOK)
        dm[rows] = m[...]
        att[rows] = a[...]
    for s in range(4):
        rows = slice(s * TOK, s * TOK + TOK)
        d_att = dot(dm[rows], wo[...], 1, 1).astype(BF)
        turned, values = qk[rows], vv[rows]
        dq, dk, dv = [], [], []
        for kv in range(2):
            k = turned[:, 256 + kv * HD : 256 + kv * HD + HD]
            v = values[:, kv * HD : kv * HD + HD]
            q = pair_of(turned, kv)
            da = pair_of(d_att, kv)
            p = softmax_of(q, k)
            dp = dot(da, v, 1, 1)
            dv.append(dot(p.astype(BF), da, 0, 0))
            ds = (p * (dp - jnp.sum(p * dp, axis=-1, keepdims=True))).astype(BF)
            dq.append(unpair(dot(ds, k)) * SCALE)
            dk.append(dot(ds, q, 0, 0) * SCALE)
        turned = rotate(jnp.concatenate(dq + dk, axis=1), cosine[...], -sine[...])
        dqkv[rows] = jnp.concatenate([turned] + dv, axis=1).astype(BF)
    g = dot(h1[...], dqkv[...], 0, 0).astype(BF)
    g_out = dot(att[...], dm[...], 0, 0).astype(BF)
    for y in range(4):
        for zh in range(4):
            for cc in range(2):
                s, to = (zh * 2 + cc) * 128, (cc + me) % 2
                grads[to, 0, y, zh] = g[s : s + 112, y * 128 : y * 128 + 128]
                grads[to, 1, y, zh, 0:16, :] = g[s + 112 : s + 128, y * 128 : y * 128 + 128]
                grads[to, 1, y, zh, 16:80, :] = g_out[y * 64 : y * 64 + 64, s : s + 128]
                grads[to, 1, y, zh, 80:112, :] = jnp.zeros((32, 128), BF)
    gain = jnp.zeros((1, D), F32)
    for s, t in enumerate((t0, t1, t2, t3)):
        rows = slice(s * TOK, s * TOK + TOK)
        to = (at[0] + RING_ORDER[s]) % 4
        d_h1 = dot(dqkv[rows], w[...], 1, 1)
        x = t[0].astype(F32)
        gain = gain + jnp.sum(d_h1 * (x * rms(x)), axis=0, keepdims=True)
        parts[to, :TOK] = d_h1.astype(BF)
        parts[to, TOK:] = (mix[rows].astype(F32) + mix_in[rows].astype(F32)).astype(BF)
    g = jnp.where(iota((16, D), 0) == 10, gain, g_in[...]).astype(BF)
    for zh in range(4):
        for cc in range(2):
            s = (zh * 2 + cc) * 128
            grads[(cc + me) % 2, 1, 0, zh, 80:96, :] = g[:, s : s + 128]
    copies = []
    for r, out in ((0, mine), (1, send)):
        for zl in range(2):
            copies.append(pltpu.make_async_copy(grads.at[r, zl], out.at[4 * zl : 4 * zl + 4], sem.at[2 * r + zl]))
    for copy in copies:
        copy.start()
    for copy in copies:
        copy.wait()


def tokens_kernel(at, back, tok, d_middle, middle, own, oth, out, layer, tick, misc_scr):
    mark(tick)
    gain = load_misc(at, own, oth, misc_scr)[10:11].astype(F32)
    total = back[...].astype(F32)
    layer[...] = (middle[...] + total[TOK:]).astype(BF)
    u = total[:TOK] * gain
    x = tok[...].astype(F32)
    rstd = rms(x)
    norm = x * rstd
    out[...] = (d_middle[...] + rstd * (u - norm * jnp.mean(u * norm, axis=-1, keepdims=True))).astype(BF)


def pack_kernel(first, second, a, a_other, one, two):
    for v, rest, out in ((first, a, one), (second, a_other, two)):
        out[0:480] = v[...]
        out[480:PIECE] = rest[...]


def stack_two_kernel(a0, a1, a2, a3, b0, b1, b2, b3, one, two):
    for k, (a, b) in enumerate(((a0, b0), (a1, b1), (a2, b2), (a3, b3))):
        one[k] = a[...]
        two[k] = b[...]


def expert_places(at, s, t):
    for k in range(4):
        for n in range(4):
            far, near = RING_ORDER[k], RING_ORDER[n]
            yield 0, s[k], n, (at[0] + near) % 4, (at[1] + far) % 4
            yield 1, t[k], n, (at[0] + far) % 4, (at[1] + near) % 4


def spread_kernel(
    at, s0, s1, s2, s3, t0, t1, t2, t3, after, gu_out, dn_out, qkv_out, out_out, misc, gu, dn, whole, qkv, out, sem
):
    places = list(expert_places(at, (s0, s1, s2, s3), (t0, t1, t2, t3)))
    copies = []

    def send(source, target):
        copies.append(pltpu.make_async_copy(source, target, sem.at[len(copies)]))
        copies[-1].start()

    for r, v, n, x, y in places:
        whole[x * 4 + y, pl.ds(pl.multiple_of((at[4] + r) % 2 * SMALL_HALF, 16), SMALL_HALF)] = v[n, 480:PIECE]
    for x in range(4):
        for y in range(4):
            c = x * 256 + y * 128 if y < 2 else y * 512 + x * 128
            qkv[:, c : c + 128] = whole[x * 4 + y, 0:128].astype(F32)
            out[x * 256 + y * 64 : x * 256 + y * 64 + 64] = whole[x * 4 + y, 128:192].astype(F32)
    send(qkv, qkv_out)
    send(out, out_out)
    m = whole[0, 192:208].astype(F32)
    for x in range(1, 4):
        m = m + whole[x * 4, 192:208].astype(F32)
    misc[...] = m
    for half in range(2):
        for k in range(HALF):
            for r, v, n, x, y in places:
                if r == half:
                    rows = pl.ds(pl.multiple_of(y * 32, 32), 32)
                    row = pl.ds(pl.multiple_of(x * 128 + y * 32, 32), 32)
                    gu[r, k, rows, pl.ds(pl.multiple_of(x * 128, 128), 128)] = v[n, k * 96 : k * 96 + 32].astype(F32)
                    gu[r, k, rows, pl.ds(pl.multiple_of(512 + x * 128, 128), 128)] = v[n, k * 96 + 32 : k * 96 + 64].astype(F32)
                    dn[r, k, row] = v[n, k * 96 + 64 : k * 96 + 96].astype(F32)
            expert = ((at[4] + half) % 2) * HALF + k
            send(gu.at[half, k], gu_out.at[expert])
            send(dn.at[half, k], dn_out.at[expert])
    for copy in copies:
        copy.wait()


def local(tokens, cotangent, gain_one, gain_two, w_qkv, w_out, w_router, w_gate_up, w_down, routes, slot_order):
    at = jnp.stack([lax.axis_index(a) for a in ("x", "y", "core", "zh", "zl")]).astype(jnp.int32)
    swap = [(0, 1), (1, 0)]
    cosine, sine = (jnp.asarray(t) for t in rope_tables())

    misc = jnp.concatenate([w_router.T, gain_one[None], gain_two[None], jnp.zeros((4, 128), BF)], axis=0)
    (small,) = call(
        pick_kernel, "pick", [sds((784, 128), BF)], (at, w_qkv, w_out, misc),
        in_specs=[SMEM] + [ANY] * 3, scratch=[pltpu.SemaphoreType.DMA((6,))], moved=1 << 19,
    )
    keep, send = call(
        pick_experts_kernel, "pick_experts", [sds((HALF, 96, 128), BF)] * 2, (at, w_gate_up, w_down),
        in_specs=[SMEM] + [ANY] * 2, scratch=[pltpu.SemaphoreType.DMA((6,))], moved=1 << 19,
    )
    ex = jnp.stack([keep, lax.ppermute(send, "core", swap)])
    ex = lax.all_gather(ex, ("zh", "y"), axis=0).reshape(4, 4, 2, HALF, 96, 128)
    tok = ring_gather(jnp.stack([tokens, cotangent]), "x")
    own = lax.all_gather(small, "zh", axis=0)
    (own,) = call(hold_kernel, "stack", [sds((4, 784, 128), BF)], (own, *tok[1:]), in_specs=[VMEM] + [ANY] * 3, moved=2 << 20)
    oth = lax.ppermute(own, "core", swap)
    w_o = ring_gather(own[:, 528:], "x")

    routed, kept = call(
        plan_kernel, "plan", [sds((TOK, 16), F32)] * 2,
        (routes, routes.reshape(1, TOK * TOPK), slot_order), flops=2 * 1280 * 1280 * 64, moved=1 << 20, vmem=32,
    )
    misc_scr = pltpu.VMEM((8, 16, 128), BF)
    block = sds((TOK, D), BF)
    h1, qk, vv, *att, c_all, tick = call(
        attention_kernel, "attention",
        [sds((RING, D), BF), sds((RING, 384), BF), sds((RING, 128), BF)] + [sds((TOK, 256), BF)] * 4 + [sds((RING, D), BF), TICK],
        (at, *tok, own, oth, cosine, sine), in_specs=[SMEM] + [VMEM] * 8,
        scratch=[pltpu.VMEM((D, 512), BF), misc_scr], flops=2 * RING * D * 512 * 2, moved=10 << 20, vmem=16,
    )
    att_home = ring_return(att, "x")
    (w_o_oth,) = call(
        stack_out_kernel, "stack_out", [sds((3, 4, 256, 128), BF)], (*w_o[1:], tick), in_specs=[VMEM] * 3 + [ANY], moved=2 << 20,
    )
    w_o_oth = lax.ppermute(w_o_oth, "core", swap)
    c_oth = lax.ppermute(c_all, "core", swap)
    middle, ext, gates = call(
        middle_kernel, "middle", [sds((TOK, D), F32), sds((TOK, D + 128), BF), sds((TOK, 16), F32)],
        (at, tokens, *att_home, *w_o, w_o_oth, own, oth, routed, kept),
        in_specs=[SMEM] + [VMEM] * 14,
        scratch=[pltpu.VMEM((256, D), BF), misc_scr], flops=2 * TOK * D * D, moved=8 << 20,
    )
    exts = ring_gather(ext, "x")
    exts_oth = [lax.ppermute(e, "core", swap) for e in exts]

    wg, wd = call(
        assemble_kernel, "assemble", [sds((D, HALF * 256), BF), sds((HALF * 128, D), BF)], (at, ex), in_specs=[SMEM, VMEM],
        flops=30 * 10**9, moved=8 << 20,
    )

    def experts(pieces, c):
        return call(
            experts_kernel, "experts",
            [
                sds((RING, D + 128), BF), sds((RING, D), BF), sds((RING, HALF * 256), BF), sds((RING, HALF * 128), BF),
                sds((RING, D), BF),
            ],
            (at, *pieces, c, wg, wd), in_specs=[SMEM] + [VMEM] * 7,
            flops=2 * RING * D * 128 * HALF * 6, moved=12 << 20, vmem=20,
        )

    pay_oth, mix_oth, d_gu_oth, wact_oth, h2_oth = experts(exts_oth, c_oth)
    pay_in = lax.ppermute(pay_oth, "core", swap)
    mix_in = lax.ppermute(mix_oth, "core", swap)
    pay, mix, d_gu, wact, h2 = experts(exts, c_all)
    *part, tick = call(add_kernel, "add_pay", [sds((TOK, D + 128), BF)] * 4 + [TICK], (pay, pay_in), moved=5 << 20)
    back = ring_return(part, "x")
    grads, tick = call(
        expert_grads_kernel, "expert_grads", [sds((2, 4, 4, HALF, 96, 128), BF), TICK],
        (h2, h2_oth, c_all, c_oth, d_gu, d_gu_oth, wact, wact_oth, tick), in_specs=[VMEM] * 8 + [ANY],
        flops=2 * RING * D * 128 * HALF * 6, moved=20 << 20, vmem=20,
    )
    d_middle, d_low, g_misc = call(
        middle_back_kernel, "middle_back", [sds((TOK, D), F32), block, sds((16, D), F32)],
        (at, *back, middle, ext, gates, kept, cotangent, own, oth, tick), in_specs=[SMEM] + [VMEM] * 11 + [ANY],
        scratch=[misc_scr], flops=100 * 10**9, moved=4 << 20,
    )
    d_mid = ring_gather(d_low, "x")
    e = lax.psum_scatter(grads.reshape(8, 4, HALF, 96, 128), ("zl", "y"), scatter_dimension=0, tiled=False)
    part, a_mine, a_send = call(
        attention_back_kernel, "attention_back", [sds((4, 2 * TOK, D), BF)] + [sds((8, 4, SMALL_HALF, 128), BF)] * 2,
        (at, *d_mid, *tok, *att, h1, qk, vv, own, oth, cosine, sine, g_misc, mix, mix_in),
        in_specs=[SMEM] + [VMEM] * 22, out_specs=[VMEM] + [ANY] * 2,
        scratch=[
            pltpu.VMEM((D, 512), BF), pltpu.VMEM((256, D), BF), pltpu.VMEM((RING, D), BF), pltpu.VMEM((RING, 256), BF),
            pltpu.VMEM((RING, 512), BF), pltpu.VMEM((2, 2, 4, 4, SMALL_HALF, 128), BF), pltpu.SemaphoreType.DMA((4,)),
        ],
        flops=10 * 10**9, moved=12 << 20, vmem=26,
    )

    back = lax.psum_scatter(part, "x", scatter_dimension=0, tiled=False)
    a = lax.ppermute(a_send, "core", swap)
    (a,) = call(add_small_kernel, "add_small", [sds((8, 4, SMALL_HALF, 128), BF)], (a_mine, a), moved=3 << 20)
    a = lax.all_to_all(a, ("zl", "y"), 0, 0, tiled=True)
    e = call(split_kernel, "split", [sds((PIECE, 128), BF)] * 4, (at, e, a), in_specs=[SMEM] + [VMEM] * 2, moved=2 << 20)
    e = ring_return(e, "zh")
    grad_tokens, layer_out, last_tick = call(
        tokens_kernel, "tokens", [block, block, TICK], (at, back, tokens, d_middle, middle, own, oth),
        in_specs=[SMEM] + [VMEM] * 6, scratch=[misc_scr], moved=6 << 20,
    )
    e, a = call(sum_four_kernel, "sum_four", [sds((480, 128), BF), sds((SMALL_HALF, 128), BF)], e, moved=1 << 20)
    pairs = [(a, b) for a in range(2) for b in range(2)]
    first = lax.ppermute(e, ("core", "zl"), [(a * 2 + b, b * 2 + a) for a, b in pairs])
    second = lax.ppermute(e, ("core", "zl"), [(a * 2 + b, b * 2 + 1 - a) for a, b in pairs])
    a_other = lax.ppermute(a, "zl", swap)
    one, two = call(pack_kernel, "pack", [sds((PIECE, 128), BF)] * 2, (first, second, a, a_other), moved=1 << 20)
    one, two = ring_gather(one, "x"), ring_gather(two, "y")
    one, two = call(stack_two_kernel, "stack_two", [sds((4, PIECE, 128), BF)] * 2, (*one, *two), moved=2 << 20)
    spread = (*ring_gather(one, "y"), *ring_gather(two, "x"))
    grad_gate_up, grad_down, grad_qkv, grad_out, g_misc = call(
        spread_kernel, "spread",
        [
            sds((EXPERTS, 128, 1024), F32), sds((EXPERTS, 512, 128), F32), sds((128, 2048), F32), sds((1024, 128), F32),
            sds((16, 128), F32),
        ],
        (at, *spread, last_tick), in_specs=[SMEM] + [VMEM] * 8 + [ANY], out_specs=[ANY] * 4 + [VMEM],
        scratch=[
            pltpu.VMEM((2, HALF, 128, 1024), F32), pltpu.VMEM((2, HALF, 512, 128), F32), pltpu.VMEM((16, SMALL, 128), BF),
            pltpu.VMEM((128, 2048), F32), pltpu.VMEM((1024, 128), F32), pltpu.SemaphoreType.DMA((22,)),
        ],
        moved=14 << 20, vmem=20,
    )
    return (
        layer_out, grad_tokens, g_misc[10], g_misc[11], grad_qkv, grad_out, g_misc[:10].T, grad_gate_up, grad_down,
    )


def solution(mesh):
    fine = Mesh(mesh.devices.reshape(SIZES), AXES)
    rows = P(AXES, None)
    s = ("zh", "core")
    return jax.shard_map(
        local,
        mesh=fine,
        in_specs=(
            rows, rows, P(s), P(s), P(s, None), P(None, s), P(s, None), P(None, s, None), P(None, None, s), rows, rows,
        ),
        out_specs=(rows, rows, P(s), P(s), P(s, None), P(None, s), P(s, None), P(None, s, None), P(None, None, s)),
        check_vma=False,
    )
```

```python
import math

import jax
import jax.numpy as jnp
import numpy as np
from jax import lax
from jax.experimental import pallas as pl
from jax.experimental.pallas import tpu as pltpu
from jax.sharding import Mesh
from jax.sharding import PartitionSpec as P

D = 1024
HD = 64
TOPK = 8
EXPERTS = 10
CAP = 144
TOK = 160
RING = 4 * TOK
EPSILON = 1e-06
ROPE_BASE = 10000.0
SCALE = 1.0 / math.sqrt(HD)

AXES = ("zh", "core", "x", "zl", "y")
SIZES = (4, 2, 4, 2, 4)
BF = jnp.bfloat16
F32 = jnp.float32
VMEM = pl.BlockSpec(memory_space=pltpu.VMEM)
SMEM = pl.BlockSpec(memory_space=pltpu.SMEM)
ANY = pl.BlockSpec(memory_space=pl.ANY)
HBM = pl.BlockSpec(memory_space=pltpu.HBM)
SMALL = 224
SMALL_HALF = 112
PIECE = 592
RING_ORDER = (0, 1, 3, 2)
TICK = jax.ShapeDtypeStruct((8, 128), jnp.float32)
HALF = 5


def sds(shape, dtype):
    return jax.ShapeDtypeStruct(shape, dtype)


def call(kernel, name, outs, args, in_specs=None, out_specs=None, scratch=(), flops=0, moved=0, vmem=12):
    return pl.pallas_call(
        kernel,
        out_shape=tuple(outs),
        in_specs=in_specs or [VMEM] * len(args),
        out_specs=tuple(out_specs or [VMEM] * len(outs)),
        scratch_shapes=list(scratch),
        compiler_params=pltpu.CompilerParams(vmem_limit_bytes=vmem * 2**20),
        cost_estimate=pl.CostEstimate(flops=flops, bytes_accessed=moved, transcendentals=0),
        name=name,
    )(*args)


def mark(tick):
    tick[...] = jnp.zeros_like(tick)


def dot(a, b, ca=1, cb=0):
    return lax.dot_general(a, b, (((ca,), (cb,)), ((), ())), preferred_element_type=F32)


def take(v, axis, k):
    return lax.ppermute(v, axis, [((i + k) % 4, i) for i in range(4)])


def ring_gather(v, axis):
    return [v] + [take(v, axis, k) for k in (1, 3, 2)]


def ring_return(blocks, axis):
    return [blocks[0], take(blocks[2], axis, 1), take(blocks[1], axis, 3), take(blocks[3], axis, 2)]


def iota(shape, dim):
    return lax.broadcasted_iota(jnp.int32, shape, dim)


def rms(v):
    return lax.rsqrt(jnp.mean(v * v, axis=-1, keepdims=True) + EPSILON)


def rope_tables():
    half = HD // 2
    frequency = (ROPE_BASE ** (-np.arange(half, dtype=np.float32) / np.float32(half))).astype(np.float32)
    angles = np.arange(TOK, dtype=np.float32)[:, None] * frequency[None, :]
    cosine = np.cos(angles).astype(np.float32)
    sine = np.sin(angles).astype(np.float32)
    return np.tile(np.concatenate([cosine, cosine], 1), (1, 6)), np.tile(np.concatenate([-sine, sine], 1), (1, 6))


def rotate(v, cosine, sine):
    width = v.shape[1]
    first = (iota(v.shape, 1) % HD) < HD // 2
    other = jnp.where(first, pltpu.roll(v, width - HD // 2, 1), pltpu.roll(v, HD // 2, 1))
    return v * cosine + other * sine


def run_copies(copies, sem):
    started = [pltpu.make_async_copy(a, b, sem.at[n]) for n, (a, b) in enumerate(copies)]
    for c in started:
        c.start()
    for c in started:
        c.wait()


def pick_kernel(at, qkv, out, misc, small, sem):
    x = at[0]
    copies = [(misc, small.at[512:528]), (out.at[pl.ds(pl.multiple_of(x * 256, 256), 256), :], small.at[528:784])]
    for k, col in enumerate((x * 256, x * 256 + 128, 1024 + x * 128, 1536 + x * 128)):
        copies.append((qkv.at[:, pl.ds(pl.multiple_of(col, 128), 128)], small.at[k * 128 : k * 128 + 128]))
    run_copies(copies, sem)


def pick_experts_kernel(at, gu, dn, keep, send, sem):
    x, y, me = at[0], at[1], at[2]
    copies = []
    for half, to in ((me, keep), (1 - me, send)):
        some, rows = pl.ds(half * HALF, HALF), pl.ds(pl.multiple_of(y * 32, 32), 32)
        copies.append((gu.at[some, rows, pl.ds(pl.multiple_of(x * 128, 128), 128)], to.at[:, 0:32]))
        copies.append((gu.at[some, rows, pl.ds(pl.multiple_of(512 + x * 128, 128), 128)], to.at[:, 32:64]))
        copies.append((dn.at[some, pl.ds(pl.multiple_of(x * 128 + y * 32, 32), 32), :], to.at[:, 64:96]))
    run_copies(copies, sem)


def plan_kernel(routes, expert_row, order, routed_ref, kept_ref):
    pairs = TOK * TOPK
    place = jnp.where(iota((pairs, pairs), 0) == order[...], 1.0, 0.0).astype(BF)
    named = jnp.where(iota((16, pairs), 0) == expert_row[...], 1.0, 0.0).astype(BF)
    ordered = dot(named, place)
    before = jnp.where(iota((pairs, pairs), 0) < iota((pairs, pairs), 1), 1.0, 0.0).astype(BF)
    earlier = dot(ordered.astype(BF), before)
    kept = jnp.where(earlier < CAP, ordered, 0.0).astype(BF)
    kept_pair = dot(kept, place, 1, 1).astype(BF)
    token = iota((TOK, pairs), 0) * TOPK
    pair = iota((TOK, pairs), 1)
    owner = jnp.where((pair >= token) & (pair < token + TOPK), 1.0, 0.0).astype(BF)
    kept_ref[...] = dot(owner, kept_pair, 1, 1)
    lane = iota((TOK, 16), 1)
    routed = jnp.zeros((TOK, 16), F32)
    for r in range(TOPK):
        routed = routed + jnp.where(routes[:, r : r + 1] == lane, 1.0, 0.0)
    routed_ref[...] = routed


def place_of(at, k, r):
    return k * 2 + (at[2] + r) % 2


def load_misc(at, own, oth, scr):
    for r, ref in ((0, own), (1, oth)):
        for k in range(4):
            scr[place_of(at, k, r)] = ref[k, 512:528, :]
    return jnp.concatenate([scr[s] for s in range(8)], axis=1)


def load_w_att(at, own, oth, scr):
    for r, ref in ((0, own), (1, oth)):
        for k in range(4):
            row = pl.multiple_of(place_of(at, k, r) * 128, 128)
            for t in range(4):
                scr[pl.ds(row, 128), t * 128 : t * 128 + 128] = ref[k, t * 128 : t * 128 + 128, :]


def load_w_out(at, own, oth, scr):
    for r, piece in ((0, own), (1, oth)):
        for k in range(4):
            col = pl.multiple_of(place_of(at, k, r) * 128, 128)
            scr[:, pl.ds(col, 128)] = piece(k)


def softmax_of(q, k):
    scores = dot(q, k, 1, 1) * SCALE
    n = q.shape[0]
    row = iota((n, TOK), 0)
    row = jnp.where(row >= TOK, row - TOK, row)
    scores = jnp.where(row >= iota((n, TOK), 1), scores, -1e30)
    e = jnp.exp(scores - jnp.max(scores, axis=-1, keepdims=True))
    return e / jnp.sum(e, axis=-1, keepdims=True)


def pair_of(v, kv):
    return jnp.concatenate([v[:, kv * 128 : kv * 128 + HD], v[:, kv * 128 + HD : kv * 128 + 128]], axis=0)


def unpair(v):
    return jnp.concatenate([v[:TOK], v[TOK:]], axis=1)


def attention_kernel(at, t0, t1, t2, t3, own, oth, cosine, sine, h1, qk, vv, a0, a1, a2, a3, c_all, tick, w, misc_scr):
    mark(tick)
    load_w_att(at, own, oth, w)
    gain = load_misc(at, own, oth, misc_scr)[10:11].astype(F32)
    for s, t in enumerate((t0, t1, t2, t3)):
        x = t[0].astype(F32)
        h1[s * TOK : s * TOK + TOK] = (x * rms(x) * gain).astype(BF)
        c_all[s * TOK : s * TOK + TOK] = t[1]
    for s, a in enumerate((a0, a1, a2, a3)):
        rows = slice(s * TOK, s * TOK + TOK)
        qkv = dot(h1[rows], w[...])
        turned = rotate(qkv[:, :384], cosine[...], sine[...]).astype(BF)
        values = qkv[:, 384:].astype(BF)
        qk[rows] = turned
        vv[rows] = values
        heads = []
        for kv in range(2):
            k = turned[:, 256 + kv * HD : 256 + kv * HD + HD]
            v = values[:, kv * HD : kv * HD + HD]
            probs = softmax_of(pair_of(turned, kv), k).astype(BF)
            heads.append(unpair(dot(probs, v)))
        a[...] = jnp.concatenate(heads, axis=1).astype(BF)


def middle_kernel(
    at, tok, a0, a1, a2, a3, o0, o1, o2, o3, v, own, oth, routed, kept, middle, ext, gates_ref, w, misc_scr
):
    misc = load_misc(at, own, oth, misc_scr)
    m = tok[...].astype(F32)
    for n, (a, o) in enumerate(((a0, o0), (a1, o1), (a2, o2), (a3, o3))):
        load_w_out(at, lambda k: o[k], (lambda k: oth[k, 528:784]) if n == 0 else (lambda k: v[n - 1, k]), w)
        m = m + dot(a[...], w[...])
    middle[...] = m
    h2 = (m * rms(m) * misc[11:12].astype(F32)).astype(BF)
    ext[:, :D] = h2
    logits = dot(h2, misc, 1, 1)
    named = routed[...] > 0.5
    e = jnp.where(named, logits, -1e30)
    e = jnp.where(named, jnp.exp(e - jnp.max(e, axis=-1, keepdims=True)), 0.0)
    gates = e / jnp.sum(e, axis=-1, keepdims=True)
    gates_ref[...] = gates
    weight = gates * kept[...]
    high = weight.astype(BF).astype(F32)
    ext[:, D:] = jnp.concatenate([high, weight - high, jnp.zeros((TOK, 96), F32)], axis=1).astype(BF)


def load_w_gu(at, ex, w):
    for r in range(2):
        core = (at[2] + r) % 2
        for zh in range(4):
            for y in range(4):
                row = pl.multiple_of((zh * 2 + core) * 128 + y * 32, 32)
                for e in range(HALF):
                    w[pl.ds(row, 32), e * 256 : e * 256 + 128] = ex[zh, y, r, e, 0:32, :]
                    w[pl.ds(row, 32), e * 256 + 128 : e * 256 + 256] = ex[zh, y, r, e, 32:64, :]


def load_w_dn(at, ex, w):
    for r in range(2):
        core = (at[2] + r) % 2
        for zh in range(4):
            col = pl.multiple_of((zh * 2 + core) * 128, 128)
            for y in range(4):
                for e in range(HALF):
                    w[e * 128 + y * 32 : e * 128 + y * 32 + 32, pl.ds(col, 128)] = ex[zh, y, r, e, 64:96, :]


def column(v, lane, e):
    return jnp.sum(jnp.where(lane == e, v, 0.0), axis=1, keepdims=True)


def assemble_kernel(at, ex, wg, wd):
    load_w_gu(at, ex, wg)
    load_w_dn(at, ex, wd)


def experts_kernel(at, e0, e1, e2, e3, c, wg, wd, pay, mix, d_gu, wact, h2):
    weight = []
    for s, e in enumerate((e0, e1, e2, e3)):
        h2[s * TOK : s * TOK + TOK] = e[:, :D]
        extra = e[:, D:].astype(F32)
        weight.append(extra[:, :16] + extra[:, 16:32])
    weight = jnp.concatenate(weight, axis=0)
    lane = iota((RING, 16), 1)
    dg = jnp.zeros((RING, 16), F32)
    for e in range(HALF):
        gu = dot(h2[...], wg[:, e * 256 : e * 256 + 256])
        cw = dot(c[...], wd[e * 128 : e * 128 + 128], 1, 1)
        g, u = gu[:, :128], gu[:, 128:]
        sig = 1.0 / (1.0 + jnp.exp(-g))
        silu = g * sig
        act = (silu * u).astype(BF).astype(F32)
        wt = column(weight, lane, at[2] * HALF + e)
        d_act = cw * wt
        d_gu[:, e * 256 : e * 256 + 128] = (d_act * u * sig * (1.0 + g * (1.0 - sig))).astype(BF)
        d_gu[:, e * 256 + 128 : e * 256 + 256] = (d_act * silu).astype(BF)
        wact[:, e * 128 : e * 128 + 128] = (act * wt).astype(BF)
        dg = dg + jnp.where(lane == at[2] * HALF + e, jnp.sum(act * cw, axis=1, keepdims=True), 0.0)
    pay[:, :D] = dot(d_gu[...], wg[...], 1, 1).astype(BF)
    high = dg.astype(BF).astype(F32)
    pay[:, D:] = jnp.concatenate([high, dg - high, jnp.zeros((RING, 96), F32)], axis=1).astype(BF)
    mix[...] = dot(wact[...], wd[...]).astype(BF)


def add_kernel(a, b, *outs):
    mark(outs[-1])
    for s, o in enumerate(outs[:-1]):
        rows = slice(s * TOK, s * TOK + TOK)
        o[...] = (a[rows].astype(F32) + b[rows].astype(F32)).astype(BF)


def expert_grads_kernel(h2, h2_oth, c, c_oth, d_gu, d_gu_oth, wact, wact_oth, after, grads, tick):
    mark(tick)
    for e in range(HALF):
        cols = slice(e * 256, e * 256 + 256)
        g = (dot(h2[...], d_gu[:, cols], 0, 0) + dot(h2_oth[...], d_gu_oth[:, cols], 0, 0)).astype(BF)
        for zh in range(4):
            for core in range(2):
                for y in range(4):
                    s = (zh * 2 + core) * 128 + y * 32
                    grads[core, y, zh, e, 0:32, :] = g[s : s + 32, 0:128]
                    grads[core, y, zh, e, 32:64, :] = g[s : s + 32, 128:256]
        cols = slice(e * 128, e * 128 + 128)
        g = (dot(wact[:, cols], c[...], 0, 0) + dot(wact_oth[:, cols], c_oth[...], 0, 0)).astype(BF)
        for zh in range(4):
            for core in range(2):
                s = (zh * 2 + core) * 128
                for y in range(4):
                    grads[core, y, zh, e, 64:96, :] = g[y * 32 : y * 32 + 32, s : s + 128]


def hold_kernel(v, *rest):
    rest[-1][...] = v[...]


def stack_out_kernel(o1, o2, o3, after, out):
    for k, o in enumerate((o1, o2, o3)):
        out[k] = o[...]


def sum_of(v):
    total = v[0].astype(F32)
    for k in range(1, v.shape[0]):
        total = total + v[k].astype(F32)
    return total


def add_small_kernel(a, b, out):
    out[...] = (a[...].astype(F32) + b[...].astype(F32)).astype(BF)


def sum_four_kernel(v0, v1, v2, v3, out):
    out[...] = (v0[...].astype(F32) + v1[...].astype(F32) + v2[...].astype(F32) + v3[...].astype(F32)).astype(BF)


def sum_kernel(v, out):
    out[...] = sum_of(v).astype(BF)


def split_kernel(at, e, *outs):
    for k, out in zip(RING_ORDER, outs):
        zh = (at[3] + k) % 4
        for n in range(HALF):
            out[n * 96 : n * 96 + 96] = e[zh, n]


def middle_back_kernel(at, b0, b1, b2, b3, middle, ext, gates_ref, kept, cot, own, oth, after, d_middle, d_low, g_misc, misc_scr):
    misc = load_misc(at, own, oth, misc_scr)
    lane = iota((16, D), 0)
    back = b0[...].astype(F32) + b1[...].astype(F32) + b2[...].astype(F32) + b3[...].astype(F32)
    gates = gates_ref[...]
    d_gates = (back[:, D : D + 16] + back[:, D + 16 : D + 32]) * kept[...]
    d_logits = (gates * (d_gates - jnp.sum(gates * d_gates, axis=1, keepdims=True))).astype(BF)
    g_router = dot(d_logits, ext[:, :D], 0, 0)
    d_h2 = back[:, :D] + dot(d_logits, misc)
    m = middle[...]
    rstd = rms(m)
    norm = m * rstd
    g_gain = jnp.sum(d_h2 * norm, axis=0, keepdims=True)
    g_misc[...] = jnp.where(lane == 11, g_gain, g_router)
    u = d_h2 * misc[11:12].astype(F32)
    d = cot[...].astype(F32) + rstd * (u - norm * jnp.mean(u * norm, axis=-1, keepdims=True))
    d_middle[...] = d
    d_low[...] = d.astype(BF)


def attention_back_kernel(
    at, m0, m1, m2, m3, t0, t1, t2, t3, a0, a1, a2, a3, h1, qk, vv, own, oth, cosine, sine, g_in, mix, mix_in,
    parts, mine, send, w, wo, dm, att, dqkv, grads, sem,
):
    me = at[2]
    load_w_att(at, own, oth, w)
    load_w_out(at, lambda k: own[k, 528:784], lambda k: oth[k, 528:784], wo)
    for s, (m, a) in enumerate(((m0, a0), (m1, a1), (m2, a2), (m3, a3))):
        rows = slice(s * TOK, s * TOK + TOK)
        dm[rows] = m[...]
        att[rows] = a[...]
    for s in range(4):
        rows = slice(s * TOK, s * TOK + TOK)
        d_att = dot(dm[rows], wo[...], 1, 1).astype(BF)
        turned, values = qk[rows], vv[rows]
        dq, dk, dv = [], [], []
        for kv in range(2):
            k = turned[:, 256 + kv * HD : 256 + kv * HD + HD]
            v = values[:, kv * HD : kv * HD + HD]
            q = pair_of(turned, kv)
            da = pair_of(d_att, kv)
            p = softmax_of(q, k)
            dp = dot(da, v, 1, 1)
            dv.append(dot(p.astype(BF), da, 0, 0))
            ds = (p * (dp - jnp.sum(p * dp, axis=-1, keepdims=True))).astype(BF)
            dq.append(unpair(dot(ds, k)) * SCALE)
            dk.append(dot(ds, q, 0, 0) * SCALE)
        turned = rotate(jnp.concatenate(dq + dk, axis=1), cosine[...], -sine[...])
        dqkv[rows] = jnp.concatenate([turned] + dv, axis=1).astype(BF)
    g = dot(h1[...], dqkv[...], 0, 0).astype(BF)
    g_out = dot(att[...], dm[...], 0, 0).astype(BF)
    for y in range(4):
        for zh in range(4):
            for cc in range(2):
                s, to = (zh * 2 + cc) * 128, (cc + me) % 2
                grads[to, 0, y, zh] = g[s : s + 112, y * 128 : y * 128 + 128]
                grads[to, 1, y, zh, 0:16, :] = g[s + 112 : s + 128, y * 128 : y * 128 + 128]
                grads[to, 1, y, zh, 16:80, :] = g_out[y * 64 : y * 64 + 64, s : s + 128]
                grads[to, 1, y, zh, 80:112, :] = jnp.zeros((32, 128), BF)
    gain = jnp.zeros((1, D), F32)
    for s, t in enumerate((t0, t1, t2, t3)):
        rows = slice(s * TOK, s * TOK + TOK)
        to = (at[0] + RING_ORDER[s]) % 4
        d_h1 = dot(dqkv[rows], w[...], 1, 1)
        x = t[0].astype(F32)
        gain = gain + jnp.sum(d_h1 * (x * rms(x)), axis=0, keepdims=True)
        parts[to, :TOK] = d_h1.astype(BF)
        parts[to, TOK:] = (mix[rows].astype(F32) + mix_in[rows].astype(F32)).astype(BF)
    g = jnp.where(iota((16, D), 0) == 10, gain, g_in[...]).astype(BF)
    for zh in range(4):
        for cc in range(2):
            s = (zh * 2 + cc) * 128
            grads[(cc + me) % 2, 1, 0, zh, 80:96, :] = g[:, s : s + 128]
    copies = []
    for r, out in ((0, mine), (1, send)):
        for zl in range(2):
            copies.append(pltpu.make_async_copy(grads.at[r, zl], out.at[4 * zl : 4 * zl + 4], sem.at[2 * r + zl]))
    for copy in copies:
        copy.start()
    for copy in copies:
        copy.wait()


def tokens_kernel(at, back, tok, d_middle, middle, own, oth, out, layer, tick, misc_scr):
    mark(tick)
    gain = load_misc(at, own, oth, misc_scr)[10:11].astype(F32)
    total = back[...].astype(F32)
    layer[...] = (middle[...] + total[TOK:]).astype(BF)
    u = total[:TOK] * gain
    x = tok[...].astype(F32)
    rstd = rms(x)
    norm = x * rstd
    out[...] = (d_middle[...] + rstd * (u - norm * jnp.mean(u * norm, axis=-1, keepdims=True))).astype(BF)


def pack_kernel(first, second, a, a_other, one, two):
    for v, rest, out in ((first, a, one), (second, a_other, two)):
        out[0:480] = v[...]
        out[480:PIECE] = rest[...]


def stack_two_kernel(a0, a1, a2, a3, b0, b1, b2, b3, one, two):
    for k, (a, b) in enumerate(((a0, b0), (a1, b1), (a2, b2), (a3, b3))):
        one[k] = a[...]
        two[k] = b[...]


def expert_places(at, s, t):
    for k in range(4):
        for n in range(4):
            far, near = RING_ORDER[k], RING_ORDER[n]
            yield 0, s[k], n, (at[0] + near) % 4, (at[1] + far) % 4
            yield 1, t[k], n, (at[0] + far) % 4, (at[1] + near) % 4


def spread_kernel(
    at, s0, s1, s2, s3, t0, t1, t2, t3, after, gu_out, dn_out, qkv_out, out_out, misc, gu, dn, whole, qkv, out, sem
):
    places = list(expert_places(at, (s0, s1, s2, s3), (t0, t1, t2, t3)))
    copies = []

    def send(source, target):
        copies.append(pltpu.make_async_copy(source, target, sem.at[len(copies)]))
        copies[-1].start()

    for r, v, n, x, y in places:
        whole[x * 4 + y, pl.ds(pl.multiple_of((at[4] + r) % 2 * SMALL_HALF, 16), SMALL_HALF)] = v[n, 480:PIECE]
    for x in range(4):
        for y in range(4):
            c = x * 256 + y * 128 if y < 2 else y * 512 + x * 128
            qkv[:, c : c + 128] = whole[x * 4 + y, 0:128].astype(F32)
            out[x * 256 + y * 64 : x * 256 + y * 64 + 64] = whole[x * 4 + y, 128:192].astype(F32)
    send(qkv, qkv_out)
    send(out, out_out)
    m = whole[0, 192:208].astype(F32)
    for x in range(1, 4):
        m = m + whole[x * 4, 192:208].astype(F32)
    misc[...] = m
    for half in range(2):
        for k in range(HALF):
            for r, v, n, x, y in places:
                if r == half:
                    rows = pl.ds(pl.multiple_of(y * 32, 32), 32)
                    row = pl.ds(pl.multiple_of(x * 128 + y * 32, 32), 32)
                    gu[r, k, rows, pl.ds(pl.multiple_of(x * 128, 128), 128)] = v[n, k * 96 : k * 96 + 32].astype(F32)
                    gu[r, k, rows, pl.ds(pl.multiple_of(512 + x * 128, 128), 128)] = v[n, k * 96 + 32 : k * 96 + 64].astype(F32)
                    dn[r, k, row] = v[n, k * 96 + 64 : k * 96 + 96].astype(F32)
            expert = ((at[4] + half) % 2) * HALF + k
            send(gu.at[half, k], gu_out.at[expert])
            send(dn.at[half, k], dn_out.at[expert])
    for copy in copies:
        copy.wait()


def local(tokens, cotangent, gain_one, gain_two, w_qkv, w_out, w_router, w_gate_up, w_down, routes, slot_order):
    at = jnp.stack([lax.axis_index(a) for a in ("x", "y", "core", "zh", "zl")]).astype(jnp.int32)
    swap = [(0, 1), (1, 0)]
    cosine, sine = (jnp.asarray(t) for t in rope_tables())

    misc = jnp.concatenate([w_router.T, gain_one[None], gain_two[None], jnp.zeros((4, 128), BF)], axis=0)
    (small,) = call(
        pick_kernel, "pick", [sds((784, 128), BF)], (at, w_qkv, w_out, misc),
        in_specs=[SMEM] + [ANY] * 3, scratch=[pltpu.SemaphoreType.DMA((6,))], moved=1 << 19,
    )
    keep, send = call(
        pick_experts_kernel, "pick_experts", [sds((HALF, 96, 128), BF)] * 2, (at, w_gate_up, w_down),
        in_specs=[SMEM] + [ANY] * 2, scratch=[pltpu.SemaphoreType.DMA((6,))], moved=1 << 19,
    )
    ex = jnp.stack([keep, lax.ppermute(send, "core", swap)])
    ex = lax.all_gather(ex, ("zh", "y"), axis=0).reshape(4, 4, 2, HALF, 96, 128)
    tok = ring_gather(jnp.stack([tokens, cotangent]), "x")
    own = lax.all_gather(small, "zh", axis=0)
    (own,) = call(hold_kernel, "stack", [sds((4, 784, 128), BF)], (own, *tok[1:]), in_specs=[VMEM] + [ANY] * 3, moved=2 << 20)
    oth = lax.ppermute(own, "core", swap)
    w_o = ring_gather(own[:, 528:], "x")

    routed, kept = call(
        plan_kernel, "plan", [sds((TOK, 16), F32)] * 2,
        (routes, routes.reshape(1, TOK * TOPK), slot_order), flops=2 * 1280 * 1280 * 64, moved=1 << 20, vmem=32,
    )
    misc_scr = pltpu.VMEM((8, 16, 128), BF)
    block = sds((TOK, D), BF)
    h1, qk, vv, *att, c_all, tick = call(
        attention_kernel, "attention",
        [sds((RING, D), BF), sds((RING, 384), BF), sds((RING, 128), BF)] + [sds((TOK, 256), BF)] * 4 + [sds((RING, D), BF), TICK],
        (at, *tok, own, oth, cosine, sine), in_specs=[SMEM] + [VMEM] * 8,
        scratch=[pltpu.VMEM((D, 512), BF), misc_scr], flops=2 * RING * D * 512 * 2, moved=10 << 20, vmem=16,
    )
    att_home = ring_return(att, "x")
    (w_o_oth,) = call(
        stack_out_kernel, "stack_out", [sds((3, 4, 256, 128), BF)], (*w_o[1:], tick), in_specs=[VMEM] * 3 + [ANY], moved=2 << 20,
    )
    w_o_oth = lax.ppermute(w_o_oth, "core", swap)
    c_oth = lax.ppermute(c_all, "core", swap)
    middle, ext, gates = call(
        middle_kernel, "middle", [sds((TOK, D), F32), sds((TOK, D + 128), BF), sds((TOK, 16), F32)],
        (at, tokens, *att_home, *w_o, w_o_oth, own, oth, routed, kept),
        in_specs=[SMEM] + [VMEM] * 14,
        scratch=[pltpu.VMEM((256, D), BF), misc_scr], flops=2 * TOK * D * D, moved=8 << 20,
    )
    exts = ring_gather(ext, "x")
    exts_oth = [lax.ppermute(e, "core", swap) for e in exts]

    wg, wd = call(
        assemble_kernel, "assemble", [sds((D, HALF * 256), BF), sds((HALF * 128, D), BF)], (at, ex), in_specs=[SMEM, VMEM],
        flops=30 * 10**9, moved=8 << 20,
    )

    def experts(pieces, c):
        return call(
            experts_kernel, "experts",
            [
                sds((RING, D + 128), BF), sds((RING, D), BF), sds((RING, HALF * 256), BF), sds((RING, HALF * 128), BF),
                sds((RING, D), BF),
            ],
            (at, *pieces, c, wg, wd), in_specs=[SMEM] + [VMEM] * 7,
            flops=2 * RING * D * 128 * HALF * 6, moved=12 << 20, vmem=20,
        )

    pay_oth, mix_oth, d_gu_oth, wact_oth, h2_oth = experts(exts_oth, c_oth)
    pay_in = lax.ppermute(pay_oth, "core", swap)
    mix_in = lax.ppermute(mix_oth, "core", swap)
    pay, mix, d_gu, wact, h2 = experts(exts, c_all)
    *part, tick = call(add_kernel, "add_pay", [sds((TOK, D + 128), BF)] * 4 + [TICK], (pay, pay_in), moved=5 << 20)
    back = ring_return(part, "x")
    grads, tick = call(
        expert_grads_kernel, "expert_grads", [sds((2, 4, 4, HALF, 96, 128), BF), TICK],
        (h2, h2_oth, c_all, c_oth, d_gu, d_gu_oth, wact, wact_oth, tick), in_specs=[VMEM] * 8 + [ANY],
        flops=2 * RING * D * 128 * HALF * 6, moved=20 << 20, vmem=20,
    )
    d_middle, d_low, g_misc = call(
        middle_back_kernel, "middle_back", [sds((TOK, D), F32), block, sds((16, D), F32)],
        (at, *back, middle, ext, gates, kept, cotangent, own, oth, tick), in_specs=[SMEM] + [VMEM] * 11 + [ANY],
        scratch=[misc_scr], flops=100 * 10**9, moved=4 << 20,
    )
    d_mid = ring_gather(d_low, "x")
    e = lax.psum_scatter(grads.reshape(8, 4, HALF, 96, 128), ("zl", "y"), scatter_dimension=0, tiled=False)
    part, a_mine, a_send = call(
        attention_back_kernel, "attention_back", [sds((4, 2 * TOK, D), BF)] + [sds((8, 4, SMALL_HALF, 128), BF)] * 2,
        (at, *d_mid, *tok, *att, h1, qk, vv, own, oth, cosine, sine, g_misc, mix, mix_in),
        in_specs=[SMEM] + [VMEM] * 22, out_specs=[VMEM] + [ANY] * 2,
        scratch=[
            pltpu.VMEM((D, 512), BF), pltpu.VMEM((256, D), BF), pltpu.VMEM((RING, D), BF), pltpu.VMEM((RING, 256), BF),
            pltpu.VMEM((RING, 512), BF), pltpu.VMEM((2, 2, 4, 4, SMALL_HALF, 128), BF), pltpu.SemaphoreType.DMA((4,)),
        ],
        flops=10 * 10**9, moved=12 << 20, vmem=26,
    )

    back = lax.psum_scatter(part, "x", scatter_dimension=0, tiled=False)
    a = lax.ppermute(a_send, "core", swap)
    (a,) = call(add_small_kernel, "add_small", [sds((8, 4, SMALL_HALF, 128), BF)], (a_mine, a), moved=3 << 20)
    a = lax.all_to_all(a, ("zl", "y"), 0, 0, tiled=True)
    e_piece = sds((480, 128), BF)
    e = call(split_kernel, "split", [e_piece] * 4, (at, e), in_specs=[SMEM, VMEM], moved=2 << 20)
    e = ring_return(e, "zh")
    grad_tokens, layer_out, last_tick = call(
        tokens_kernel, "tokens", [block, block, TICK], (at, back, tokens, d_middle, middle, own, oth),
        in_specs=[SMEM] + [VMEM] * 6, scratch=[misc_scr], moved=6 << 20,
    )
    (e,) = call(sum_four_kernel, "sum_four", [e_piece], e, moved=1 << 20)
    (a,) = call(sum_kernel, "sum_eight", [sds((4, SMALL_HALF, 128), BF)], (a,), moved=1 << 20)
    a = lax.all_to_all(a, "zh", 0, 0, tiled=True)
    (a,) = call(sum_kernel, "sum_last", [sds((SMALL_HALF, 128), BF)], (a,), moved=1 << 18)
    pairs = [(a, b) for a in range(2) for b in range(2)]
    first = lax.ppermute(e, ("core", "zl"), [(a * 2 + b, b * 2 + a) for a, b in pairs])
    second = lax.ppermute(e, ("core", "zl"), [(a * 2 + b, b * 2 + 1 - a) for a, b in pairs])
    a_other = lax.ppermute(a, "zl", swap)
    one, two = call(pack_kernel, "pack", [sds((PIECE, 128), BF)] * 2, (first, second, a, a_other), moved=1 << 20)
    one, two = ring_gather(one, "x"), ring_gather(two, "y")
    one, two = call(stack_two_kernel, "stack_two", [sds((4, PIECE, 128), BF)] * 2, (*one, *two), moved=2 << 20)
    spread = (*ring_gather(one, "y"), *ring_gather(two, "x"))
    grad_gate_up, grad_down, grad_qkv, grad_out, g_misc = call(
        spread_kernel, "spread",
        [
            sds((EXPERTS, 128, 1024), F32), sds((EXPERTS, 512, 128), F32), sds((128, 2048), F32), sds((1024, 128), F32),
            sds((16, 128), F32),
        ],
        (at, *spread, last_tick), in_specs=[SMEM] + [VMEM] * 8 + [ANY], out_specs=[ANY] * 4 + [VMEM],
        scratch=[
            pltpu.VMEM((2, HALF, 128, 1024), F32), pltpu.VMEM((2, HALF, 512, 128), F32), pltpu.VMEM((16, SMALL, 128), BF),
            pltpu.VMEM((128, 2048), F32), pltpu.VMEM((1024, 128), F32), pltpu.SemaphoreType.DMA((22,)),
        ],
        moved=14 << 20, vmem=20,
    )
    return (
        layer_out, grad_tokens, g_misc[10], g_misc[11], grad_qkv, grad_out, g_misc[:10].T, grad_gate_up, grad_down,
    )


def solution(mesh):
    fine = Mesh(mesh.devices.reshape(SIZES), AXES)
    rows = P(AXES, None)
    s = ("zh", "core")
    return jax.shard_map(
        local,
        mesh=fine,
        in_specs=(
            rows, rows, P(s), P(s), P(s, None), P(None, s), P(s, None), P(None, s, None), P(None, None, s), rows, rows,
        ),
        out_specs=(rows, rows, P(s), P(s), P(s, None), P(None, s), P(s, None), P(None, s, None), P(None, None, s)),
        check_vma=False,
    )
```

```python
import math

import jax
import jax.numpy as jnp
import numpy as np
from jax import lax
from jax.experimental import pallas as pl
from jax.experimental.pallas import tpu as pltpu
from jax.sharding import Mesh
from jax.sharding import PartitionSpec as P

D = 1024
HD = 64
TOPK = 8
EXPERTS = 10
CAP = 144
TOK = 160
RING = 4 * TOK
EPSILON = 1e-06
ROPE_BASE = 10000.0
SCALE = 1.0 / math.sqrt(HD)

AXES = ("zh", "core", "x", "zl", "y")
SIZES = (4, 2, 4, 2, 4)
BF = jnp.bfloat16
F32 = jnp.float32
VMEM = pl.BlockSpec(memory_space=pltpu.VMEM)
SMEM = pl.BlockSpec(memory_space=pltpu.SMEM)
ANY = pl.BlockSpec(memory_space=pl.ANY)
HBM = pl.BlockSpec(memory_space=pltpu.HBM)
SMALL = 224
SMALL_HALF = 112
PIECE = 592
RING_ORDER = (0, 1, 3, 2)
TICK = jax.ShapeDtypeStruct((8, 128), jnp.float32)
HALF = 5


def sds(shape, dtype):
    return jax.ShapeDtypeStruct(shape, dtype)


def call(kernel, name, outs, args, in_specs=None, out_specs=None, scratch=(), flops=0, moved=0, vmem=12):
    return pl.pallas_call(
        kernel,
        out_shape=tuple(outs),
        in_specs=in_specs or [VMEM] * len(args),
        out_specs=tuple(out_specs or [VMEM] * len(outs)),
        scratch_shapes=list(scratch),
        compiler_params=pltpu.CompilerParams(vmem_limit_bytes=vmem * 2**20),
        cost_estimate=pl.CostEstimate(flops=flops, bytes_accessed=moved, transcendentals=0),
        name=name,
    )(*args)


def mark(tick):
    tick[...] = jnp.zeros_like(tick)


def dot(a, b, ca=1, cb=0):
    return lax.dot_general(a, b, (((ca,), (cb,)), ((), ())), preferred_element_type=F32)


def take(v, axis, k):
    return lax.ppermute(v, axis, [((i + k) % 4, i) for i in range(4)])


def ring_gather(v, axis):
    return [v] + [take(v, axis, k) for k in (1, 3, 2)]


def ring_return(blocks, axis):
    return [blocks[0], take(blocks[2], axis, 1), take(blocks[1], axis, 3), take(blocks[3], axis, 2)]


def iota(shape, dim):
    return lax.broadcasted_iota(jnp.int32, shape, dim)


def rms(v):
    return lax.rsqrt(jnp.mean(v * v, axis=-1, keepdims=True) + EPSILON)


def rope_tables():
    half = HD // 2
    frequency = (ROPE_BASE ** (-np.arange(half, dtype=np.float32) / np.float32(half))).astype(np.float32)
    angles = np.arange(TOK, dtype=np.float32)[:, None] * frequency[None, :]
    cosine = np.cos(angles).astype(np.float32)
    sine = np.sin(angles).astype(np.float32)
    return np.tile(np.concatenate([cosine, cosine], 1), (1, 6)), np.tile(np.concatenate([-sine, sine], 1), (1, 6))


def rotate(v, cosine, sine):
    width = v.shape[1]
    first = (iota(v.shape, 1) % HD) < HD // 2
    other = jnp.where(first, pltpu.roll(v, width - HD // 2, 1), pltpu.roll(v, HD // 2, 1))
    return v * cosine + other * sine


def run_copies(copies, sem):
    started = [pltpu.make_async_copy(a, b, sem.at[n]) for n, (a, b) in enumerate(copies)]
    for c in started:
        c.start()
    for c in started:
        c.wait()


def pick_kernel(at, qkv, out, misc, small, sem):
    x = at[0]
    copies = [(misc, small.at[512:528]), (out.at[pl.ds(pl.multiple_of(x * 256, 256), 256), :], small.at[528:784])]
    for k, col in enumerate((x * 256, x * 256 + 128, 1024 + x * 128, 1536 + x * 128)):
        copies.append((qkv.at[:, pl.ds(pl.multiple_of(col, 128), 128)], small.at[k * 128 : k * 128 + 128]))
    run_copies(copies, sem)


def pick_experts_kernel(at, gu, dn, keep, send, sem):
    x, y, me = at[0], at[1], at[2]
    copies = []
    for half, to in ((me, keep), (1 - me, send)):
        some, rows = pl.ds(half * HALF, HALF), pl.ds(pl.multiple_of(y * 32, 32), 32)
        copies.append((gu.at[some, rows, pl.ds(pl.multiple_of(x * 128, 128), 128)], to.at[:, 0:32]))
        copies.append((gu.at[some, rows, pl.ds(pl.multiple_of(512 + x * 128, 128), 128)], to.at[:, 32:64]))
        copies.append((dn.at[some, pl.ds(pl.multiple_of(x * 128 + y * 32, 32), 32), :], to.at[:, 64:96]))
    run_copies(copies, sem)


def plan_kernel(routes, expert_row, order, routed_ref, kept_ref):
    pairs = TOK * TOPK
    place = jnp.where(iota((pairs, pairs), 0) == order[...], 1.0, 0.0).astype(BF)
    named = jnp.where(iota((16, pairs), 0) == expert_row[...], 1.0, 0.0).astype(BF)
    ordered = dot(named, place)
    before = jnp.where(iota((pairs, pairs), 0) < iota((pairs, pairs), 1), 1.0, 0.0).astype(BF)
    earlier = dot(ordered.astype(BF), before)
    kept = jnp.where(earlier < CAP, ordered, 0.0).astype(BF)
    kept_pair = dot(kept, place, 1, 1).astype(BF)
    token = iota((TOK, pairs), 0) * TOPK
    pair = iota((TOK, pairs), 1)
    owner = jnp.where((pair >= token) & (pair < token + TOPK), 1.0, 0.0).astype(BF)
    kept_ref[...] = dot(owner, kept_pair, 1, 1)
    lane = iota((TOK, 16), 1)
    routed = jnp.zeros((TOK, 16), F32)
    for r in range(TOPK):
        routed = routed + jnp.where(routes[:, r : r + 1] == lane, 1.0, 0.0)
    routed_ref[...] = routed


def place_of(at, k, r):
    return k * 2 + (at[2] + r) % 2


def load_misc(at, own, oth, scr):
    for r, ref in ((0, own), (1, oth)):
        for k in range(4):
            scr[place_of(at, k, r)] = ref[k, 512:528, :]
    return jnp.concatenate([scr[s] for s in range(8)], axis=1)


def load_w_att(at, own, oth, scr):
    for r, ref in ((0, own), (1, oth)):
        for k in range(4):
            row = pl.multiple_of(place_of(at, k, r) * 128, 128)
            for t in range(4):
                scr[pl.ds(row, 128), t * 128 : t * 128 + 128] = ref[k, t * 128 : t * 128 + 128, :]


def load_w_out(at, own, oth, scr):
    for r, piece in ((0, own), (1, oth)):
        for k in range(4):
            col = pl.multiple_of(place_of(at, k, r) * 128, 128)
            scr[:, pl.ds(col, 128)] = piece(k)


def softmax_of(q, k):
    scores = dot(q, k, 1, 1) * SCALE
    n = q.shape[0]
    row = iota((n, TOK), 0)
    row = jnp.where(row >= TOK, row - TOK, row)
    scores = jnp.where(row >= iota((n, TOK), 1), scores, -1e30)
    e = jnp.exp(scores - jnp.max(scores, axis=-1, keepdims=True))
    return e / jnp.sum(e, axis=-1, keepdims=True)


def pair_of(v, kv):
    return jnp.concatenate([v[:, kv * 128 : kv * 128 + HD], v[:, kv * 128 + HD : kv * 128 + 128]], axis=0)


def unpair(v):
    return jnp.concatenate([v[:TOK], v[TOK:]], axis=1)


def attention_kernel(at, t0, t1, t2, t3, own, oth, cosine, sine, h1, qk, vv, a0, a1, a2, a3, c_all, tick, w, misc_scr):
    mark(tick)
    load_w_att(at, own, oth, w)
    gain = load_misc(at, own, oth, misc_scr)[10:11].astype(F32)
    for s, t in enumerate((t0, t1, t2, t3)):
        x = t[0].astype(F32)
        h1[s * TOK : s * TOK + TOK] = (x * rms(x) * gain).astype(BF)
        c_all[s * TOK : s * TOK + TOK] = t[1]
    for s, a in enumerate((a0, a1, a2, a3)):
        rows = slice(s * TOK, s * TOK + TOK)
        qkv = dot(h1[rows], w[...])
        turned = rotate(qkv[:, :384], cosine[...], sine[...]).astype(BF)
        values = qkv[:, 384:].astype(BF)
        qk[rows] = turned
        vv[rows] = values
        heads = []
        for kv in range(2):
            k = turned[:, 256 + kv * HD : 256 + kv * HD + HD]
            v = values[:, kv * HD : kv * HD + HD]
            probs = softmax_of(pair_of(turned, kv), k).astype(BF)
            heads.append(unpair(dot(probs, v)))
        a[...] = jnp.concatenate(heads, axis=1).astype(BF)


def middle_kernel(
    at, tok, a0, a1, a2, a3, o0, o1, o2, o3, v, own, oth, routed, kept, middle, ext, gates_ref, w, misc_scr
):
    misc = load_misc(at, own, oth, misc_scr)
    m = tok[...].astype(F32)
    for n, (a, o) in enumerate(((a0, o0), (a1, o1), (a2, o2), (a3, o3))):
        load_w_out(at, lambda k: o[k], (lambda k: oth[k, 528:784]) if n == 0 else (lambda k: v[n - 1, k]), w)
        m = m + dot(a[...], w[...])
    middle[...] = m
    h2 = (m * rms(m) * misc[11:12].astype(F32)).astype(BF)
    ext[:, :D] = h2
    logits = dot(h2, misc, 1, 1)
    named = routed[...] > 0.5
    e = jnp.where(named, logits, -1e30)
    e = jnp.where(named, jnp.exp(e - jnp.max(e, axis=-1, keepdims=True)), 0.0)
    gates = e / jnp.sum(e, axis=-1, keepdims=True)
    gates_ref[...] = gates
    weight = gates * kept[...]
    high = weight.astype(BF).astype(F32)
    ext[:, D:] = jnp.concatenate([high, weight - high, jnp.zeros((TOK, 96), F32)], axis=1).astype(BF)


def load_w_gu(at, ex, w):
    for r in range(2):
        core = (at[2] + r) % 2
        for zh in range(4):
            for y in range(4):
                row = pl.multiple_of((zh * 2 + core) * 128 + y * 32, 32)
                for e in range(HALF):
                    w[pl.ds(row, 32), e * 256 : e * 256 + 128] = ex[zh, y, r, e, 0:32, :]
                    w[pl.ds(row, 32), e * 256 + 128 : e * 256 + 256] = ex[zh, y, r, e, 32:64, :]


def load_w_dn(at, ex, w):
    for r in range(2):
        core = (at[2] + r) % 2
        for zh in range(4):
            col = pl.multiple_of((zh * 2 + core) * 128, 128)
            for y in range(4):
                for e in range(HALF):
                    w[e * 128 + y * 32 : e * 128 + y * 32 + 32, pl.ds(col, 128)] = ex[zh, y, r, e, 64:96, :]


def column(v, lane, e):
    return jnp.sum(jnp.where(lane == e, v, 0.0), axis=1, keepdims=True)


def assemble_kernel(at, ex, wg, wd):
    load_w_gu(at, ex, wg)
    load_w_dn(at, ex, wd)


def experts_kernel(at, e0, e1, e2, e3, c, wg, wd, pay, mix, d_gu, wact, h2):
    weight = []
    for s, e in enumerate((e0, e1, e2, e3)):
        h2[s * TOK : s * TOK + TOK] = e[:, :D]
        extra = e[:, D:].astype(F32)
        weight.append(extra[:, :16] + extra[:, 16:32])
    weight = jnp.concatenate(weight, axis=0)
    lane = iota((RING, 16), 1)
    dg = jnp.zeros((RING, 16), F32)
    for e in range(HALF):
        gu = dot(h2[...], wg[:, e * 256 : e * 256 + 256])
        cw = dot(c[...], wd[e * 128 : e * 128 + 128], 1, 1)
        g, u = gu[:, :128], gu[:, 128:]
        sig = 1.0 / (1.0 + jnp.exp(-g))
        silu = g * sig
        act = (silu * u).astype(BF).astype(F32)
        wt = column(weight, lane, at[2] * HALF + e)
        d_act = cw * wt
        d_gu[:, e * 256 : e * 256 + 128] = (d_act * u * sig * (1.0 + g * (1.0 - sig))).astype(BF)
        d_gu[:, e * 256 + 128 : e * 256 + 256] = (d_act * silu).astype(BF)
        wact[:, e * 128 : e * 128 + 128] = (act * wt).astype(BF)
        dg = dg + jnp.where(lane == at[2] * HALF + e, jnp.sum(act * cw, axis=1, keepdims=True), 0.0)
    pay[:, :D] = dot(d_gu[...], wg[...], 1, 1).astype(BF)
    high = dg.astype(BF).astype(F32)
    pay[:, D:] = jnp.concatenate([high, dg - high, jnp.zeros((RING, 96), F32)], axis=1).astype(BF)
    mix[...] = dot(wact[...], wd[...]).astype(BF)


def add_kernel(a, b, *outs):
    mark(outs[-1])
    for s, o in enumerate(outs[:-1]):
        rows = slice(s * TOK, s * TOK + TOK)
        o[...] = (a[rows].astype(F32) + b[rows].astype(F32)).astype(BF)


def expert_grads_kernel(h2, h2_oth, c, c_oth, d_gu, d_gu_oth, wact, wact_oth, after, grads, tick):
    mark(tick)
    for e in range(HALF):
        cols = slice(e * 256, e * 256 + 256)
        g = (dot(h2[...], d_gu[:, cols], 0, 0) + dot(h2_oth[...], d_gu_oth[:, cols], 0, 0)).astype(BF)
        for zh in range(4):
            for core in range(2):
                for y in range(4):
                    s = (zh * 2 + core) * 128 + y * 32
                    grads[core, y, zh, e, 0:32, :] = g[s : s + 32, 0:128]
                    grads[core, y, zh, e, 32:64, :] = g[s : s + 32, 128:256]
        cols = slice(e * 128, e * 128 + 128)
        g = (dot(wact[:, cols], c[...], 0, 0) + dot(wact_oth[:, cols], c_oth[...], 0, 0)).astype(BF)
        for zh in range(4):
            for core in range(2):
                s = (zh * 2 + core) * 128
                for y in range(4):
                    grads[core, y, zh, e, 64:96, :] = g[y * 32 : y * 32 + 32, s : s + 128]


def hold_kernel(v, *rest):
    rest[-1][...] = v[...]


def stack_out_kernel(o1, o2, o3, after, out):
    for k, o in enumerate((o1, o2, o3)):
        out[k] = o[...]


def sum_of(v):
    total = v[0].astype(F32)
    for k in range(1, v.shape[0]):
        total = total + v[k].astype(F32)
    return total


def add_small_kernel(a, b, out):
    out[...] = (a[...].astype(F32) + b[...].astype(F32)).astype(BF)


def sum_four_kernel(v0, v1, v2, v3, out):
    out[...] = (v0[...].astype(F32) + v1[...].astype(F32) + v2[...].astype(F32) + v3[...].astype(F32)).astype(BF)


def sum_kernel(v, out):
    out[...] = sum_of(v).astype(BF)


def split_kernel(at, e, *outs):
    for k, out in zip(RING_ORDER, outs):
        zh = (at[3] + k) % 4
        for n in range(HALF):
            out[n * 96 : n * 96 + 96] = e[zh, n]


def middle_back_kernel(at, b0, b1, b2, b3, middle, ext, gates_ref, kept, cot, own, oth, after, d_middle, d_low, g_misc, misc_scr):
    misc = load_misc(at, own, oth, misc_scr)
    lane = iota((16, D), 0)
    back = b0[...].astype(F32) + b1[...].astype(F32) + b2[...].astype(F32) + b3[...].astype(F32)
    gates = gates_ref[...]
    d_gates = (back[:, D : D + 16] + back[:, D + 16 : D + 32]) * kept[...]
    d_logits = (gates * (d_gates - jnp.sum(gates * d_gates, axis=1, keepdims=True))).astype(BF)
    g_router = dot(d_logits, ext[:, :D], 0, 0)
    d_h2 = back[:, :D] + dot(d_logits, misc)
    m = middle[...]
    rstd = rms(m)
    norm = m * rstd
    g_gain = jnp.sum(d_h2 * norm, axis=0, keepdims=True)
    g_misc[...] = jnp.where(lane == 11, g_gain, g_router)
    u = d_h2 * misc[11:12].astype(F32)
    d = cot[...].astype(F32) + rstd * (u - norm * jnp.mean(u * norm, axis=-1, keepdims=True))
    d_middle[...] = d
    d_low[...] = d.astype(BF)


def prepare_kernel(at, qk, own, oth, mix, mix_in, after, probs, w, wo, mix_out):
    mix_out[...] = (mix[...].astype(F32) + mix_in[...].astype(F32)).astype(BF)
    load_w_att(at, own, oth, w)
    load_w_out(at, lambda k: own[k, 528:784], lambda k: oth[k, 528:784], wo)
    for s in range(4):
        turned = qk[s * TOK : s * TOK + TOK]
        for kv in range(2):
            probs[2 * s + kv] = softmax_of(pair_of(turned, kv), turned[:, 256 + kv * HD : 256 + kv * HD + HD])


def attention_back_kernel(
    at, m0, m1, m2, m3, t0, t1, t2, t3, a0, a1, a2, a3, h1, qk, vv, probs, w, wo, mix, cosine, sine, g_in,
    parts, mine, send, dm, att, dqkv, grads, sem,
):
    me = at[2]
    for s, (m, a) in enumerate(((m0, a0), (m1, a1), (m2, a2), (m3, a3))):
        rows = slice(s * TOK, s * TOK + TOK)
        dm[rows] = m[...]
        att[rows] = a[...]
    for s in range(4):
        rows = slice(s * TOK, s * TOK + TOK)
        d_att = dot(dm[rows], wo[...], 1, 1).astype(BF)
        turned, values = qk[rows], vv[rows]
        dq, dk, dv = [], [], []
        for kv in range(2):
            k = turned[:, 256 + kv * HD : 256 + kv * HD + HD]
            v = values[:, kv * HD : kv * HD + HD]
            q = pair_of(turned, kv)
            da = pair_of(d_att, kv)
            p = probs[2 * s + kv]
            dp = dot(da, v, 1, 1)
            dv.append(dot(p.astype(BF), da, 0, 0))
            ds = (p * (dp - jnp.sum(p * dp, axis=-1, keepdims=True))).astype(BF)
            dq.append(unpair(dot(ds, k)) * SCALE)
            dk.append(dot(ds, q, 0, 0) * SCALE)
        turned = rotate(jnp.concatenate(dq + dk, axis=1), cosine[...], -sine[...])
        dqkv[rows] = jnp.concatenate([turned] + dv, axis=1).astype(BF)
    g = dot(h1[...], dqkv[...], 0, 0).astype(BF)
    g_out = dot(att[...], dm[...], 0, 0).astype(BF)
    for y in range(4):
        for zh in range(4):
            for cc in range(2):
                s, to = (zh * 2 + cc) * 128, (cc + me) % 2
                grads[to, 0, y, zh] = g[s : s + 112, y * 128 : y * 128 + 128]
                grads[to, 1, y, zh, 0:16, :] = g[s + 112 : s + 128, y * 128 : y * 128 + 128]
                grads[to, 1, y, zh, 16:80, :] = g_out[y * 64 : y * 64 + 64, s : s + 128]
                grads[to, 1, y, zh, 80:112, :] = jnp.zeros((32, 128), BF)
    gain = jnp.zeros((1, D), F32)
    for s, t in enumerate((t0, t1, t2, t3)):
        rows = slice(s * TOK, s * TOK + TOK)
        to = (at[0] + RING_ORDER[s]) % 4
        d_h1 = dot(dqkv[rows], w[...], 1, 1)
        x = t[0].astype(F32)
        gain = gain + jnp.sum(d_h1 * (x * rms(x)), axis=0, keepdims=True)
        parts[to, :TOK] = d_h1.astype(BF)
        parts[to, TOK:] = mix[rows]
    g = jnp.where(iota((16, D), 0) == 10, gain, g_in[...]).astype(BF)
    for zh in range(4):
        for cc in range(2):
            s = (zh * 2 + cc) * 128
            grads[(cc + me) % 2, 1, 0, zh, 80:96, :] = g[:, s : s + 128]
    copies = []
    for r, out in ((0, mine), (1, send)):
        for zl in range(2):
            copies.append(pltpu.make_async_copy(grads.at[r, zl], out.at[4 * zl : 4 * zl + 4], sem.at[2 * r + zl]))
    for copy in copies:
        copy.start()
    for copy in copies:
        copy.wait()


def tokens_kernel(at, back, tok, d_middle, middle, own, oth, out, layer, tick, misc_scr):
    mark(tick)
    gain = load_misc(at, own, oth, misc_scr)[10:11].astype(F32)
    total = back[...].astype(F32)
    layer[...] = (middle[...] + total[TOK:]).astype(BF)
    u = total[:TOK] * gain
    x = tok[...].astype(F32)
    rstd = rms(x)
    norm = x * rstd
    out[...] = (d_middle[...] + rstd * (u - norm * jnp.mean(u * norm, axis=-1, keepdims=True))).astype(BF)


def pack_kernel(first, second, a, a_other, one, two):
    for v, rest, out in ((first, a, one), (second, a_other, two)):
        out[0:480] = v[...]
        out[480:PIECE] = rest[...]


def stack_two_kernel(a0, a1, a2, a3, b0, b1, b2, b3, one, two):
    for k, (a, b) in enumerate(((a0, b0), (a1, b1), (a2, b2), (a3, b3))):
        one[k] = a[...]
        two[k] = b[...]


def expert_places(at, s, t):
    for k in range(4):
        for n in range(4):
            far, near = RING_ORDER[k], RING_ORDER[n]
            yield 0, s[k], n, (at[0] + near) % 4, (at[1] + far) % 4
            yield 1, t[k], n, (at[0] + far) % 4, (at[1] + near) % 4


def spread_kernel(
    at, s0, s1, s2, s3, t0, t1, t2, t3, after, gu_out, dn_out, qkv_out, out_out, misc, gu, dn, whole, qkv, out, sem
):
    places = list(expert_places(at, (s0, s1, s2, s3), (t0, t1, t2, t3)))
    copies = []

    def send(source, target):
        copies.append(pltpu.make_async_copy(source, target, sem.at[len(copies)]))
        copies[-1].start()

    for r, v, n, x, y in places:
        whole[x * 4 + y, pl.ds(pl.multiple_of((at[4] + r) % 2 * SMALL_HALF, 16), SMALL_HALF)] = v[n, 480:PIECE]
    for x in range(4):
        for y in range(4):
            c = x * 256 + y * 128 if y < 2 else y * 512 + x * 128
            qkv[:, c : c + 128] = whole[x * 4 + y, 0:128].astype(F32)
            out[x * 256 + y * 64 : x * 256 + y * 64 + 64] = whole[x * 4 + y, 128:192].astype(F32)
    send(qkv, qkv_out)
    send(out, out_out)
    m = whole[0, 192:208].astype(F32)
    for x in range(1, 4):
        m = m + whole[x * 4, 192:208].astype(F32)
    misc[...] = m
    for half in range(2):
        for k in range(HALF):
            for r, v, n, x, y in places:
                if r == half:
                    rows = pl.ds(pl.multiple_of(y * 32, 32), 32)
                    row = pl.ds(pl.multiple_of(x * 128 + y * 32, 32), 32)
                    gu[r, k, rows, pl.ds(pl.multiple_of(x * 128, 128), 128)] = v[n, k * 96 : k * 96 + 32].astype(F32)
                    gu[r, k, rows, pl.ds(pl.multiple_of(512 + x * 128, 128), 128)] = v[n, k * 96 + 32 : k * 96 + 64].astype(F32)
                    dn[r, k, row] = v[n, k * 96 + 64 : k * 96 + 96].astype(F32)
            expert = ((at[4] + half) % 2) * HALF + k
            send(gu.at[half, k], gu_out.at[expert])
            send(dn.at[half, k], dn_out.at[expert])
    for copy in copies:
        copy.wait()


def local(tokens, cotangent, gain_one, gain_two, w_qkv, w_out, w_router, w_gate_up, w_down, routes, slot_order):
    at = jnp.stack([lax.axis_index(a) for a in ("x", "y", "core", "zh", "zl")]).astype(jnp.int32)
    swap = [(0, 1), (1, 0)]
    cosine, sine = (jnp.asarray(t) for t in rope_tables())

    misc = jnp.concatenate([w_router.T, gain_one[None], gain_two[None], jnp.zeros((4, 128), BF)], axis=0)
    (small,) = call(
        pick_kernel, "pick", [sds((784, 128), BF)], (at, w_qkv, w_out, misc),
        in_specs=[SMEM] + [ANY] * 3, scratch=[pltpu.SemaphoreType.DMA((6,))], moved=1 << 19,
    )
    keep, send = call(
        pick_experts_kernel, "pick_experts", [sds((HALF, 96, 128), BF)] * 2, (at, w_gate_up, w_down),
        in_specs=[SMEM] + [ANY] * 2, scratch=[pltpu.SemaphoreType.DMA((6,))], moved=1 << 19,
    )
    ex = jnp.stack([keep, lax.ppermute(send, "core", swap)])
    ex = lax.all_gather(ex, ("zh", "y"), axis=0).reshape(4, 4, 2, HALF, 96, 128)
    tok = ring_gather(jnp.stack([tokens, cotangent]), "x")
    own = lax.all_gather(small, "zh", axis=0)
    (own,) = call(hold_kernel, "stack", [sds((4, 784, 128), BF)], (own, *tok[1:]), in_specs=[VMEM] + [ANY] * 3, moved=2 << 20)
    oth = lax.ppermute(own, "core", swap)
    w_o = ring_gather(own[:, 528:], "x")

    routed, kept = call(
        plan_kernel, "plan", [sds((TOK, 16), F32)] * 2,
        (routes, routes.reshape(1, TOK * TOPK), slot_order), flops=2 * 1280 * 1280 * 64, moved=1 << 20, vmem=32,
    )
    misc_scr = pltpu.VMEM((8, 16, 128), BF)
    block = sds((TOK, D), BF)
    h1, qk, vv, *att, c_all, tick = call(
        attention_kernel, "attention",
        [sds((RING, D), BF), sds((RING, 384), BF), sds((RING, 128), BF)] + [sds((TOK, 256), BF)] * 4 + [sds((RING, D), BF), TICK],
        (at, *tok, own, oth, cosine, sine), in_specs=[SMEM] + [VMEM] * 8,
        scratch=[pltpu.VMEM((D, 512), BF), misc_scr], flops=2 * RING * D * 512 * 2, moved=10 << 20, vmem=16,
    )
    att_home = ring_return(att, "x")
    (w_o_oth,) = call(
        stack_out_kernel, "stack_out", [sds((3, 4, 256, 128), BF)], (*w_o[1:], tick), in_specs=[VMEM] * 3 + [ANY], moved=2 << 20,
    )
    w_o_oth = lax.ppermute(w_o_oth, "core", swap)
    c_oth = lax.ppermute(c_all, "core", swap)
    middle, ext, gates = call(
        middle_kernel, "middle", [sds((TOK, D), F32), sds((TOK, D + 128), BF), sds((TOK, 16), F32)],
        (at, tokens, *att_home, *w_o, w_o_oth, own, oth, routed, kept),
        in_specs=[SMEM] + [VMEM] * 14,
        scratch=[pltpu.VMEM((256, D), BF), misc_scr], flops=2 * TOK * D * D, moved=8 << 20,
    )
    exts = ring_gather(ext, "x")
    exts_oth = [lax.ppermute(e, "core", swap) for e in exts]

    wg, wd = call(
        assemble_kernel, "assemble", [sds((D, HALF * 256), BF), sds((HALF * 128, D), BF)], (at, ex), in_specs=[SMEM, VMEM],
        flops=30 * 10**9, moved=8 << 20,
    )

    def experts(pieces, c):
        return call(
            experts_kernel, "experts",
            [
                sds((RING, D + 128), BF), sds((RING, D), BF), sds((RING, HALF * 256), BF), sds((RING, HALF * 128), BF),
                sds((RING, D), BF),
            ],
            (at, *pieces, c, wg, wd), in_specs=[SMEM] + [VMEM] * 7,
            flops=2 * RING * D * 128 * HALF * 6, moved=12 << 20, vmem=20,
        )

    pay_oth, mix_oth, d_gu_oth, wact_oth, h2_oth = experts(exts_oth, c_oth)
    pay_in = lax.ppermute(pay_oth, "core", swap)
    mix_in = lax.ppermute(mix_oth, "core", swap)
    pay, mix, d_gu, wact, h2 = experts(exts, c_all)
    *part, tick = call(add_kernel, "add_pay", [sds((TOK, D + 128), BF)] * 4 + [TICK], (pay, pay_in), moved=5 << 20)
    back = ring_return(part, "x")
    grads, tick = call(
        expert_grads_kernel, "expert_grads", [sds((2, 4, 4, HALF, 96, 128), BF), TICK],
        (h2, h2_oth, c_all, c_oth, d_gu, d_gu_oth, wact, wact_oth, tick), in_specs=[VMEM] * 8 + [ANY],
        flops=2 * RING * D * 128 * HALF * 6, moved=20 << 20, vmem=20,
    )
    d_middle, d_low, g_misc = call(
        middle_back_kernel, "middle_back", [sds((TOK, D), F32), block, sds((16, D), F32)],
        (at, *back, middle, ext, gates, kept, cotangent, own, oth, tick), in_specs=[SMEM] + [VMEM] * 11 + [ANY],
        scratch=[misc_scr], flops=100 * 10**9, moved=4 << 20,
    )
    d_mid = ring_gather(d_low, "x")
    e = lax.psum_scatter(grads.reshape(8, 4, HALF, 96, 128), ("zl", "y"), scatter_dimension=0, tiled=False)
    prepared = call(
        prepare_kernel, "prepare", [sds((8, 2 * TOK, TOK), F32), sds((D, 512), BF), sds((256, D), BF), sds((RING, D), BF)],
        (at, qk, own, oth, mix, mix_in, g_misc), in_specs=[SMEM] + [VMEM] * 5 + [ANY], flops=10**10, moved=8 << 20, vmem=16,
    )
    part, a_mine, a_send = call(
        attention_back_kernel, "attention_back", [sds((4, 2 * TOK, D), BF)] + [sds((8, 4, SMALL_HALF, 128), BF)] * 2,
        (at, *d_mid, *tok, *att, h1, qk, vv, *prepared, cosine, sine, g_misc),
        in_specs=[SMEM] + [VMEM] * 22, out_specs=[VMEM] + [ANY] * 2,
        scratch=[
            pltpu.VMEM((RING, D), BF), pltpu.VMEM((RING, 256), BF),
            pltpu.VMEM((RING, 512), BF), pltpu.VMEM((2, 2, 4, 4, SMALL_HALF, 128), BF), pltpu.SemaphoreType.DMA((4,)),
        ],
        flops=10 * 10**9, moved=12 << 20, vmem=26,
    )

    back = lax.psum_scatter(part, "x", scatter_dimension=0, tiled=False)
    a = lax.ppermute(a_send, "core", swap)
    (a,) = call(add_small_kernel, "add_small", [sds((8, 4, SMALL_HALF, 128), BF)], (a_mine, a), moved=3 << 20)
    a = lax.all_to_all(a, ("zl", "y"), 0, 0, tiled=True)
    e_piece = sds((480, 128), BF)
    e = call(split_kernel, "split", [e_piece] * 4, (at, e), in_specs=[SMEM, VMEM], moved=2 << 20)
    e = ring_return(e, "zh")
    grad_tokens, layer_out, last_tick = call(
        tokens_kernel, "tokens", [block, block, TICK], (at, back, tokens, d_middle, middle, own, oth),
        in_specs=[SMEM] + [VMEM] * 6, scratch=[misc_scr], moved=6 << 20,
    )
    (e,) = call(sum_four_kernel, "sum_four", [e_piece], e, moved=1 << 20)
    (a,) = call(sum_kernel, "sum_eight", [sds((4, SMALL_HALF, 128), BF)], (a,), moved=1 << 20)
    a = lax.all_to_all(a, "zh", 0, 0, tiled=True)
    (a,) = call(sum_kernel, "sum_last", [sds((SMALL_HALF, 128), BF)], (a,), moved=1 << 18)
    pairs = [(a, b) for a in range(2) for b in range(2)]
    first = lax.ppermute(e, ("core", "zl"), [(a * 2 + b, b * 2 + a) for a, b in pairs])
    second = lax.ppermute(e, ("core", "zl"), [(a * 2 + b, b * 2 + 1 - a) for a, b in pairs])
    a_other = lax.ppermute(a, "zl", swap)
    one, two = call(pack_kernel, "pack", [sds((PIECE, 128), BF)] * 2, (first, second, a, a_other), moved=1 << 20)
    one, two = ring_gather(one, "x"), ring_gather(two, "y")
    one, two = call(stack_two_kernel, "stack_two", [sds((4, PIECE, 128), BF)] * 2, (*one, *two), moved=2 << 20)
    spread = (*ring_gather(one, "y"), *ring_gather(two, "x"))
    grad_gate_up, grad_down, grad_qkv, grad_out, g_misc = call(
        spread_kernel, "spread",
        [
            sds((EXPERTS, 128, 1024), F32), sds((EXPERTS, 512, 128), F32), sds((128, 2048), F32), sds((1024, 128), F32),
            sds((16, 128), F32),
        ],
        (at, *spread, last_tick), in_specs=[SMEM] + [VMEM] * 8 + [ANY], out_specs=[ANY] * 4 + [VMEM],
        scratch=[
            pltpu.VMEM((2, HALF, 128, 1024), F32), pltpu.VMEM((2, HALF, 512, 128), F32), pltpu.VMEM((16, SMALL, 128), BF),
            pltpu.VMEM((128, 2048), F32), pltpu.VMEM((1024, 128), F32), pltpu.SemaphoreType.DMA((22,)),
        ],
        moved=14 << 20, vmem=20,
    )
    return (
        layer_out, grad_tokens, g_misc[10], g_misc[11], grad_qkv, grad_out, g_misc[:10].T, grad_gate_up, grad_down,
    )


def solution(mesh):
    fine = Mesh(mesh.devices.reshape(SIZES), AXES)
    rows = P(AXES, None)
    s = ("zh", "core")
    return jax.shard_map(
        local,
        mesh=fine,
        in_specs=(
            rows, rows, P(s), P(s), P(s, None), P(None, s), P(s, None), P(None, s, None), P(None, None, s), rows, rows,
        ),
        out_specs=(rows, rows, P(s), P(s), P(s, None), P(None, s), P(s, None), P(None, s, None), P(None, None, s)),
        check_vma=False,
    )
```

```python
import math

import jax
import jax.numpy as jnp
import numpy as np
from jax import lax
from jax.experimental import pallas as pl
from jax.experimental.pallas import tpu as pltpu
from jax.sharding import Mesh
from jax.sharding import PartitionSpec as P

D = 1024
HD = 64
TOPK = 8
EXPERTS = 10
CAP = 144
TOK = 160
RING = 4 * TOK
EPSILON = 1e-06
ROPE_BASE = 10000.0
SCALE = 1.0 / math.sqrt(HD)

AXES = ("zh", "core", "x", "zl", "y")
SIZES = (4, 2, 4, 2, 4)
BF = jnp.bfloat16
F32 = jnp.float32
VMEM = pl.BlockSpec(memory_space=pltpu.VMEM)
SMEM = pl.BlockSpec(memory_space=pltpu.SMEM)
ANY = pl.BlockSpec(memory_space=pl.ANY)
HBM = pl.BlockSpec(memory_space=pltpu.HBM)
SMALL = 224
SMALL_HALF = 112
PIECE = 592
RING_ORDER = (0, 1, 3, 2)
ORDER_ONE = (0, 2, 1, 3)
ORDER_TWO = (0, 1, 2, 3)
TICK = jax.ShapeDtypeStruct((8, 128), jnp.float32)
HALF = 5


def sds(shape, dtype):
    return jax.ShapeDtypeStruct(shape, dtype)


def call(kernel, name, outs, args, in_specs=None, out_specs=None, scratch=(), flops=0, moved=0, vmem=12):
    return pl.pallas_call(
        kernel,
        out_shape=tuple(outs),
        in_specs=in_specs or [VMEM] * len(args),
        out_specs=tuple(out_specs or [VMEM] * len(outs)),
        scratch_shapes=list(scratch),
        compiler_params=pltpu.CompilerParams(vmem_limit_bytes=vmem * 2**20),
        cost_estimate=pl.CostEstimate(flops=flops, bytes_accessed=moved, transcendentals=0),
        name=name,
    )(*args)


def mark(tick):
    tick[...] = jnp.zeros_like(tick)


def dot(a, b, ca=1, cb=0):
    return lax.dot_general(a, b, (((ca,), (cb,)), ((), ())), preferred_element_type=F32)


def take(v, axis, k):
    return lax.ppermute(v, axis, [((i + k) % 4, i) for i in range(4)])


def ring_gather(v, axis, order=(0, 1, 3, 2)):
    return [v] + [take(v, axis, k) for k in order[1:]]


def ring_return(blocks, axis):
    return [blocks[0], take(blocks[2], axis, 1), take(blocks[1], axis, 3), take(blocks[3], axis, 2)]


def iota(shape, dim):
    return lax.broadcasted_iota(jnp.int32, shape, dim)


def rms(v):
    return lax.rsqrt(jnp.mean(v * v, axis=-1, keepdims=True) + EPSILON)


def rope_tables():
    half = HD // 2
    frequency = (ROPE_BASE ** (-np.arange(half, dtype=np.float32) / np.float32(half))).astype(np.float32)
    angles = np.arange(TOK, dtype=np.float32)[:, None] * frequency[None, :]
    cosine = np.cos(angles).astype(np.float32)
    sine = np.sin(angles).astype(np.float32)
    return np.tile(np.concatenate([cosine, cosine], 1), (1, 6)), np.tile(np.concatenate([-sine, sine], 1), (1, 6))


def rotate(v, cosine, sine):
    width = v.shape[1]
    first = (iota(v.shape, 1) % HD) < HD // 2
    other = jnp.where(first, pltpu.roll(v, width - HD // 2, 1), pltpu.roll(v, HD // 2, 1))
    return v * cosine + other * sine


def run_copies(copies, sem):
    started = [pltpu.make_async_copy(a, b, sem.at[n]) for n, (a, b) in enumerate(copies)]
    for c in started:
        c.start()
    for c in started:
        c.wait()


def pick_kernel(at, qkv, out, misc, small, sem):
    x = at[0]
    copies = [(misc, small.at[512:528]), (out.at[pl.ds(pl.multiple_of(x * 256, 256), 256), :], small.at[528:784])]
    for k, col in enumerate((x * 256, x * 256 + 128, 1024 + x * 128, 1536 + x * 128)):
        copies.append((qkv.at[:, pl.ds(pl.multiple_of(col, 128), 128)], small.at[k * 128 : k * 128 + 128]))
    run_copies(copies, sem)


def pick_experts_kernel(at, gu, dn, keep, send, sem):
    x, y, me = at[0], at[1], at[2]
    copies = []
    for half, to in ((me, keep), (1 - me, send)):
        some, rows = pl.ds(half * HALF, HALF), pl.ds(pl.multiple_of(y * 32, 32), 32)
        copies.append((gu.at[some, rows, pl.ds(pl.multiple_of(x * 128, 128), 128)], to.at[:, 0:32]))
        copies.append((gu.at[some, rows, pl.ds(pl.multiple_of(512 + x * 128, 128), 128)], to.at[:, 32:64]))
        copies.append((dn.at[some, pl.ds(pl.multiple_of(x * 128 + y * 32, 32), 32), :], to.at[:, 64:96]))
    run_copies(copies, sem)


def plan_kernel(routes, expert_row, order, routed_ref, kept_ref):
    pairs = TOK * TOPK
    place = jnp.where(iota((pairs, pairs), 0) == order[...], 1.0, 0.0).astype(BF)
    named = jnp.where(iota((16, pairs), 0) == expert_row[...], 1.0, 0.0).astype(BF)
    ordered = dot(named, place)
    before = jnp.where(iota((pairs, pairs), 0) < iota((pairs, pairs), 1), 1.0, 0.0).astype(BF)
    earlier = dot(ordered.astype(BF), before)
    kept = jnp.where(earlier < CAP, ordered, 0.0).astype(BF)
    kept_pair = dot(kept, place, 1, 1).astype(BF)
    token = iota((TOK, pairs), 0) * TOPK
    pair = iota((TOK, pairs), 1)
    owner = jnp.where((pair >= token) & (pair < token + TOPK), 1.0, 0.0).astype(BF)
    kept_ref[...] = dot(owner, kept_pair, 1, 1)
    lane = iota((TOK, 16), 1)
    routed = jnp.zeros((TOK, 16), F32)
    for r in range(TOPK):
        routed = routed + jnp.where(routes[:, r : r + 1] == lane, 1.0, 0.0)
    routed_ref[...] = routed


def place_of(at, k, r):
    return k * 2 + (at[2] + r) % 2


def load_misc(at, own, oth, scr):
    for r, ref in ((0, own), (1, oth)):
        for k in range(4):
            scr[place_of(at, k, r)] = ref[k, 512:528, :]
    return jnp.concatenate([scr[s] for s in range(8)], axis=1)


def load_w_att(at, own, oth, scr):
    for r, ref in ((0, own), (1, oth)):
        for k in range(4):
            row = pl.multiple_of(place_of(at, k, r) * 128, 128)
            for t in range(4):
                scr[pl.ds(row, 128), t * 128 : t * 128 + 128] = ref[k, t * 128 : t * 128 + 128, :]


def load_w_out(at, own, oth, scr):
    for r, piece in ((0, own), (1, oth)):
        for k in range(4):
            col = pl.multiple_of(place_of(at, k, r) * 128, 128)
            scr[:, pl.ds(col, 128)] = piece(k)


def softmax_of(q, k):
    scores = dot(q, k, 1, 1) * SCALE
    n = q.shape[0]
    row = iota((n, TOK), 0)
    row = jnp.where(row >= TOK, row - TOK, row)
    scores = jnp.where(row >= iota((n, TOK), 1), scores, -1e30)
    e = jnp.exp(scores - jnp.max(scores, axis=-1, keepdims=True))
    return e / jnp.sum(e, axis=-1, keepdims=True)


def pair_of(v, kv):
    return jnp.concatenate([v[:, kv * 128 : kv * 128 + HD], v[:, kv * 128 + HD : kv * 128 + 128]], axis=0)


def unpair(v):
    return jnp.concatenate([v[:TOK], v[TOK:]], axis=1)


def attention_kernel(at, t0, t1, t2, t3, own, oth, cosine, sine, h1, qk, vv, a0, a1, a2, a3, c_all, tick, w, misc_scr):
    mark(tick)
    load_w_att(at, own, oth, w)
    gain = load_misc(at, own, oth, misc_scr)[10:11].astype(F32)
    for s, t in enumerate((t0, t1, t2, t3)):
        x = t[0].astype(F32)
        h1[s * TOK : s * TOK + TOK] = (x * rms(x) * gain).astype(BF)
        c_all[s * TOK : s * TOK + TOK] = t[1]
    for s, a in enumerate((a0, a1, a2, a3)):
        rows = slice(s * TOK, s * TOK + TOK)
        qkv = dot(h1[rows], w[...])
        turned = rotate(qkv[:, :384], cosine[...], sine[...]).astype(BF)
        values = qkv[:, 384:].astype(BF)
        qk[rows] = turned
        vv[rows] = values
        heads = []
        for kv in range(2):
            k = turned[:, 256 + kv * HD : 256 + kv * HD + HD]
            v = values[:, kv * HD : kv * HD + HD]
            probs = softmax_of(pair_of(turned, kv), k).astype(BF)
            heads.append(unpair(dot(probs, v)))
        a[...] = jnp.concatenate(heads, axis=1).astype(BF)


def middle_kernel(
    at, tok, a0, a1, a2, a3, o0, o1, o2, o3, v, own, oth, routed, kept, middle, ext, gates_ref, w, misc_scr
):
    misc = load_misc(at, own, oth, misc_scr)
    m = tok[...].astype(F32)
    for n, (a, o) in enumerate(((a0, o0), (a1, o1), (a2, o2), (a3, o3))):
        load_w_out(at, lambda k: o[k], (lambda k: oth[k, 528:784]) if n == 0 else (lambda k: v[n - 1, k]), w)
        m = m + dot(a[...], w[...])
    middle[...] = m
    h2 = (m * rms(m) * misc[11:12].astype(F32)).astype(BF)
    ext[:, :D] = h2
    logits = dot(h2, misc, 1, 1)
    named = routed[...] > 0.5
    e = jnp.where(named, logits, -1e30)
    e = jnp.where(named, jnp.exp(e - jnp.max(e, axis=-1, keepdims=True)), 0.0)
    gates = e / jnp.sum(e, axis=-1, keepdims=True)
    gates_ref[...] = gates
    weight = gates * kept[...]
    high = weight.astype(BF).astype(F32)
    ext[:, D:] = jnp.concatenate([high, weight - high, jnp.zeros((TOK, 96), F32)], axis=1).astype(BF)


def load_w_gu(at, ex, w):
    for r in range(2):
        core = (at[2] + r) % 2
        for zh in range(4):
            for y in range(4):
                row = pl.multiple_of((zh * 2 + core) * 128 + y * 32, 32)
                for e in range(HALF):
                    w[pl.ds(row, 32), e * 256 : e * 256 + 128] = ex[zh, y, r, e, 0:32, :]
                    w[pl.ds(row, 32), e * 256 + 128 : e * 256 + 256] = ex[zh, y, r, e, 32:64, :]


def load_w_dn(at, ex, w):
    for r in range(2):
        core = (at[2] + r) % 2
        for zh in range(4):
            col = pl.multiple_of((zh * 2 + core) * 128, 128)
            for y in range(4):
                for e in range(HALF):
                    w[e * 128 + y * 32 : e * 128 + y * 32 + 32, pl.ds(col, 128)] = ex[zh, y, r, e, 64:96, :]


def column(v, lane, e):
    return jnp.sum(jnp.where(lane == e, v, 0.0), axis=1, keepdims=True)


def assemble_kernel(at, ex, wg, wd):
    load_w_gu(at, ex, wg)
    load_w_dn(at, ex, wd)


def experts_kernel(at, e0, e1, e2, e3, c, wg, wd, pay, mix, d_gu, wact, h2):
    weight = []
    for s, e in enumerate((e0, e1, e2, e3)):
        h2[s * TOK : s * TOK + TOK] = e[:, :D]
        extra = e[:, D:].astype(F32)
        weight.append(extra[:, :16] + extra[:, 16:32])
    weight = jnp.concatenate(weight, axis=0)
    lane = iota((RING, 16), 1)
    dg = jnp.zeros((RING, 16), F32)
    for e in range(HALF):
        gu = dot(h2[...], wg[:, e * 256 : e * 256 + 256])
        cw = dot(c[...], wd[e * 128 : e * 128 + 128], 1, 1)
        g, u = gu[:, :128], gu[:, 128:]
        sig = 1.0 / (1.0 + jnp.exp(-g))
        silu = g * sig
        act = (silu * u).astype(BF).astype(F32)
        wt = column(weight, lane, at[2] * HALF + e)
        d_act = cw * wt
        d_gu[:, e * 256 : e * 256 + 128] = (d_act * u * sig * (1.0 + g * (1.0 - sig))).astype(BF)
        d_gu[:, e * 256 + 128 : e * 256 + 256] = (d_act * silu).astype(BF)
        wact[:, e * 128 : e * 128 + 128] = (act * wt).astype(BF)
        dg = dg + jnp.where(lane == at[2] * HALF + e, jnp.sum(act * cw, axis=1, keepdims=True), 0.0)
    pay[:, :D] = dot(d_gu[...], wg[...], 1, 1).astype(BF)
    high = dg.astype(BF).astype(F32)
    pay[:, D:] = jnp.concatenate([high, dg - high, jnp.zeros((RING, 96), F32)], axis=1).astype(BF)
    mix[...] = dot(wact[...], wd[...]).astype(BF)


def add_kernel(a, b, *outs):
    mark(outs[-1])
    for s, o in enumerate(outs[:-1]):
        rows = slice(s * TOK, s * TOK + TOK)
        o[...] = (a[rows].astype(F32) + b[rows].astype(F32)).astype(BF)


def expert_grads_kernel(h2, h2_oth, c, c_oth, d_gu, d_gu_oth, wact, wact_oth, after, grads, tick):
    mark(tick)
    for e in range(HALF):
        cols = slice(e * 256, e * 256 + 256)
        g = (dot(h2[...], d_gu[:, cols], 0, 0) + dot(h2_oth[...], d_gu_oth[:, cols], 0, 0)).astype(BF)
        for zh in range(4):
            for core in range(2):
                for y in range(4):
                    s = (zh * 2 + core) * 128 + y * 32
                    grads[core, y, zh, e, 0:32, :] = g[s : s + 32, 0:128]
                    grads[core, y, zh, e, 32:64, :] = g[s : s + 32, 128:256]
        cols = slice(e * 128, e * 128 + 128)
        g = (dot(wact[:, cols], c[...], 0, 0) + dot(wact_oth[:, cols], c_oth[...], 0, 0)).astype(BF)
        for zh in range(4):
            for core in range(2):
                s = (zh * 2 + core) * 128
                for y in range(4):
                    grads[core, y, zh, e, 64:96, :] = g[y * 32 : y * 32 + 32, s : s + 128]


def hold_kernel(v, *rest):
    rest[-1][...] = v[...]


def stack_out_kernel(o1, o2, o3, after, out):
    for k, o in enumerate((o1, o2, o3)):
        out[k] = o[...]


def sum_of(v):
    total = v[0].astype(F32)
    for k in range(1, v.shape[0]):
        total = total + v[k].astype(F32)
    return total


def add_small_kernel(a, b, out):
    out[...] = (a[...].astype(F32) + b[...].astype(F32)).astype(BF)


def sum_four_kernel(v0, v1, v2, v3, out):
    out[...] = (v0[...].astype(F32) + v1[...].astype(F32) + v2[...].astype(F32) + v3[...].astype(F32)).astype(BF)


def sum_kernel(v, out):
    out[...] = sum_of(v).astype(BF)


def split_kernel(at, e, *outs):
    for k, out in zip(RING_ORDER, outs):
        zh = (at[3] + k) % 4
        for n in range(HALF):
            out[n * 96 : n * 96 + 96] = e[zh, n]


def middle_back_kernel(at, b0, b1, b2, b3, middle, ext, gates_ref, kept, cot, own, oth, after, d_middle, d_low, g_misc, misc_scr):
    misc = load_misc(at, own, oth, misc_scr)
    lane = iota((16, D), 0)
    back = b0[...].astype(F32) + b1[...].astype(F32) + b2[...].astype(F32) + b3[...].astype(F32)
    gates = gates_ref[...]
    d_gates = (back[:, D : D + 16] + back[:, D + 16 : D + 32]) * kept[...]
    d_logits = (gates * (d_gates - jnp.sum(gates * d_gates, axis=1, keepdims=True))).astype(BF)
    g_router = dot(d_logits, ext[:, :D], 0, 0)
    d_h2 = back[:, :D] + dot(d_logits, misc)
    m = middle[...]
    rstd = rms(m)
    norm = m * rstd
    g_gain = jnp.sum(d_h2 * norm, axis=0, keepdims=True)
    g_misc[...] = jnp.where(lane == 11, g_gain, g_router)
    u = d_h2 * misc[11:12].astype(F32)
    d = cot[...].astype(F32) + rstd * (u - norm * jnp.mean(u * norm, axis=-1, keepdims=True))
    d_middle[...] = d
    d_low[...] = d.astype(BF)


def prepare_kernel(at, qk, own, oth, mix, mix_in, after, probs, w, wo, mix_out):
    mix_out[...] = (mix[...].astype(F32) + mix_in[...].astype(F32)).astype(BF)
    load_w_att(at, own, oth, w)
    load_w_out(at, lambda k: own[k, 528:784], lambda k: oth[k, 528:784], wo)
    for s in range(4):
        turned = qk[s * TOK : s * TOK + TOK]
        for kv in range(2):
            probs[2 * s + kv] = softmax_of(pair_of(turned, kv), turned[:, 256 + kv * HD : 256 + kv * HD + HD])


def attention_back_kernel(
    at, m0, m1, m2, m3, t0, t1, t2, t3, a0, a1, a2, a3, h1, qk, vv, probs, w, wo, mix, cosine, sine, g_in,
    parts, mine, send, dm, att, dqkv, grads, sem,
):
    me = at[2]
    for s, (m, a) in enumerate(((m0, a0), (m1, a1), (m2, a2), (m3, a3))):
        rows = slice(s * TOK, s * TOK + TOK)
        dm[rows] = m[...]
        att[rows] = a[...]
    for s in range(4):
        rows = slice(s * TOK, s * TOK + TOK)
        d_att = dot(dm[rows], wo[...], 1, 1).astype(BF)
        turned, values = qk[rows], vv[rows]
        dq, dk, dv = [], [], []
        for kv in range(2):
            k = turned[:, 256 + kv * HD : 256 + kv * HD + HD]
            v = values[:, kv * HD : kv * HD + HD]
            q = pair_of(turned, kv)
            da = pair_of(d_att, kv)
            p = probs[2 * s + kv]
            dp = dot(da, v, 1, 1)
            dv.append(dot(p.astype(BF), da, 0, 0))
            ds = (p * (dp - jnp.sum(p * dp, axis=-1, keepdims=True))).astype(BF)
            dq.append(unpair(dot(ds, k)) * SCALE)
            dk.append(dot(ds, q, 0, 0) * SCALE)
        turned = rotate(jnp.concatenate(dq + dk, axis=1), cosine[...], -sine[...])
        dqkv[rows] = jnp.concatenate([turned] + dv, axis=1).astype(BF)
    g = dot(h1[...], dqkv[...], 0, 0).astype(BF)
    g_out = dot(att[...], dm[...], 0, 0).astype(BF)
    for y in range(4):
        for zh in range(4):
            for cc in range(2):
                s, to = (zh * 2 + cc) * 128, (cc + me) % 2
                grads[to, 0, y, zh] = g[s : s + 112, y * 128 : y * 128 + 128]
                grads[to, 1, y, zh, 0:16, :] = g[s + 112 : s + 128, y * 128 : y * 128 + 128]
                grads[to, 1, y, zh, 16:80, :] = g_out[y * 64 : y * 64 + 64, s : s + 128]
                grads[to, 1, y, zh, 80:112, :] = jnp.zeros((32, 128), BF)
    gain = jnp.zeros((1, D), F32)
    for s, t in enumerate((t0, t1, t2, t3)):
        rows = slice(s * TOK, s * TOK + TOK)
        to = (at[0] + RING_ORDER[s]) % 4
        d_h1 = dot(dqkv[rows], w[...], 1, 1)
        x = t[0].astype(F32)
        gain = gain + jnp.sum(d_h1 * (x * rms(x)), axis=0, keepdims=True)
        parts[to, :TOK] = d_h1.astype(BF)
        parts[to, TOK:] = mix[rows]
    g = jnp.where(iota((16, D), 0) == 10, gain, g_in[...]).astype(BF)
    for zh in range(4):
        for cc in range(2):
            s = (zh * 2 + cc) * 128
            grads[(cc + me) % 2, 1, 0, zh, 80:96, :] = g[:, s : s + 128]
    copies = []
    for r, out in ((0, mine), (1, send)):
        for zl in range(2):
            copies.append(pltpu.make_async_copy(grads.at[r, zl], out.at[4 * zl : 4 * zl + 4], sem.at[2 * r + zl]))
    for copy in copies:
        copy.start()
    for copy in copies:
        copy.wait()


def tokens_kernel(at, back, tok, d_middle, middle, own, oth, out, layer, tick, misc_scr):
    mark(tick)
    gain = load_misc(at, own, oth, misc_scr)[10:11].astype(F32)
    total = back[...].astype(F32)
    layer[...] = (middle[...] + total[TOK:]).astype(BF)
    u = total[:TOK] * gain
    x = tok[...].astype(F32)
    rstd = rms(x)
    norm = x * rstd
    out[...] = (d_middle[...] + rstd * (u - norm * jnp.mean(u * norm, axis=-1, keepdims=True))).astype(BF)


def pack_kernel(first, second, a, a_other, one, two):
    for v, rest, out in ((first, a, one), (second, a_other, two)):
        out[0:480] = v[...]
        out[480:PIECE] = rest[...]


def stack_two_kernel(a0, a1, a2, a3, b0, b1, b2, b3, after, one, two):
    for k, (a, b) in enumerate(((a0, b0), (a1, b1), (a2, b2), (a3, b3))):
        one[k] = a[...]
        two[k] = b[...]


def expert_places(at, s, t):
    for k in range(4):
        for n in range(4):
            yield 0, s[k], n, (at[0] + ORDER_ONE[n]) % 4, (at[1] + ORDER_ONE[k]) % 4
            yield 1, t[k], n, (at[0] + ORDER_TWO[k]) % 4, (at[1] + ORDER_TWO[n]) % 4


def spread_kernel(
    at, s0, s1, s2, s3, t0, t1, t2, t3, after, gu_out, dn_out, qkv_out, out_out, misc, gu, dn, whole, qkv, out, sem
):
    places = list(expert_places(at, (s0, s1, s2, s3), (t0, t1, t2, t3)))
    copies = []

    def send(source, target):
        copies.append(pltpu.make_async_copy(source, target, sem.at[len(copies)]))
        copies[-1].start()

    for r, v, n, x, y in places:
        whole[x * 4 + y, pl.ds(pl.multiple_of((at[4] + r) % 2 * SMALL_HALF, 16), SMALL_HALF)] = v[n, 480:PIECE]
    for x in range(4):
        for y in range(4):
            c = x * 256 + y * 128 if y < 2 else y * 512 + x * 128
            qkv[:, c : c + 128] = whole[x * 4 + y, 0:128].astype(F32)
            out[x * 256 + y * 64 : x * 256 + y * 64 + 64] = whole[x * 4 + y, 128:192].astype(F32)
    send(qkv, qkv_out)
    send(out, out_out)
    m = whole[0, 192:208].astype(F32)
    for x in range(1, 4):
        m = m + whole[x * 4, 192:208].astype(F32)
    misc[...] = m
    for half in range(2):
        for k in range(HALF):
            for r, v, n, x, y in places:
                if r == half:
                    rows = pl.ds(pl.multiple_of(y * 32, 32), 32)
                    row = pl.ds(pl.multiple_of(x * 128 + y * 32, 32), 32)
                    gu[r, k, rows, pl.ds(pl.multiple_of(x * 128, 128), 128)] = v[n, k * 96 : k * 96 + 32].astype(F32)
                    gu[r, k, rows, pl.ds(pl.multiple_of(512 + x * 128, 128), 128)] = v[n, k * 96 + 32 : k * 96 + 64].astype(F32)
                    dn[r, k, row] = v[n, k * 96 + 64 : k * 96 + 96].astype(F32)
            expert = ((at[4] + half) % 2) * HALF + k
            send(gu.at[half, k], gu_out.at[expert])
            send(dn.at[half, k], dn_out.at[expert])
    for copy in copies:
        copy.wait()


def local(tokens, cotangent, gain_one, gain_two, w_qkv, w_out, w_router, w_gate_up, w_down, routes, slot_order):
    at = jnp.stack([lax.axis_index(a) for a in ("x", "y", "core", "zh", "zl")]).astype(jnp.int32)
    swap = [(0, 1), (1, 0)]
    cosine, sine = (jnp.asarray(t) for t in rope_tables())

    misc = jnp.concatenate([w_router.T, gain_one[None], gain_two[None], jnp.zeros((4, 128), BF)], axis=0)
    (small,) = call(
        pick_kernel, "pick", [sds((784, 128), BF)], (at, w_qkv, w_out, misc),
        in_specs=[SMEM] + [ANY] * 3, scratch=[pltpu.SemaphoreType.DMA((6,))], moved=1 << 19,
    )
    keep, send = call(
        pick_experts_kernel, "pick_experts", [sds((HALF, 96, 128), BF)] * 2, (at, w_gate_up, w_down),
        in_specs=[SMEM] + [ANY] * 2, scratch=[pltpu.SemaphoreType.DMA((6,))], moved=1 << 19, vmem=56,
    )
    ex = jnp.stack([keep, lax.ppermute(send, "core", swap)])
    ex = lax.all_gather(ex, ("zh", "y"), axis=0).reshape(4, 4, 2, HALF, 96, 128)
    tok = ring_gather(jnp.stack([tokens, cotangent]), "x")
    own = lax.all_gather(small, "zh", axis=0)
    (own,) = call(hold_kernel, "stack", [sds((4, 784, 128), BF)], (own, *tok[1:]), in_specs=[VMEM] + [ANY] * 3, moved=2 << 20)
    oth = lax.ppermute(own, "core", swap)
    w_o = ring_gather(own[:, 528:], "x")

    routed, kept = call(
        plan_kernel, "plan", [sds((TOK, 16), F32)] * 2,
        (routes, routes.reshape(1, TOK * TOPK), slot_order), flops=2 * 1280 * 1280 * 64, moved=1 << 20, vmem=32,
    )
    misc_scr = pltpu.VMEM((8, 16, 128), BF)
    block = sds((TOK, D), BF)
    h1, qk, vv, *att, c_all, tick = call(
        attention_kernel, "attention",
        [sds((RING, D), BF), sds((RING, 384), BF), sds((RING, 128), BF)] + [sds((TOK, 256), BF)] * 4 + [sds((RING, D), BF), TICK],
        (at, *tok, own, oth, cosine, sine), in_specs=[SMEM] + [VMEM] * 8,
        scratch=[pltpu.VMEM((D, 512), BF), misc_scr], flops=2 * RING * D * 512 * 2, moved=10 << 20, vmem=16,
    )
    att_home = ring_return(att, "x")
    (w_o_oth,) = call(
        stack_out_kernel, "stack_out", [sds((3, 4, 256, 128), BF)], (*w_o[1:], tick), in_specs=[VMEM] * 3 + [ANY], moved=2 << 20,
    )
    w_o_oth = lax.ppermute(w_o_oth, "core", swap)
    c_oth = lax.ppermute(c_all, "core", swap)
    middle, ext, gates = call(
        middle_kernel, "middle", [sds((TOK, D), F32), sds((TOK, D + 128), BF), sds((TOK, 16), F32)],
        (at, tokens, *att_home, *w_o, w_o_oth, own, oth, routed, kept),
        in_specs=[SMEM] + [VMEM] * 14,
        scratch=[pltpu.VMEM((256, D), BF), misc_scr], flops=2 * TOK * D * D, moved=8 << 20,
    )
    exts = ring_gather(ext, "x")
    exts_oth = [lax.ppermute(e, "core", swap) for e in exts]

    wg, wd = call(
        assemble_kernel, "assemble", [sds((D, HALF * 256), BF), sds((HALF * 128, D), BF)], (at, ex), in_specs=[SMEM, VMEM],
        flops=30 * 10**9, moved=8 << 20,
    )

    def experts(pieces, c):
        return call(
            experts_kernel, "experts",
            [
                sds((RING, D + 128), BF), sds((RING, D), BF), sds((RING, HALF * 256), BF), sds((RING, HALF * 128), BF),
                sds((RING, D), BF),
            ],
            (at, *pieces, c, wg, wd), in_specs=[SMEM] + [VMEM] * 7,
            flops=2 * RING * D * 128 * HALF * 6, moved=12 << 20, vmem=20,
        )

    pay_oth, mix_oth, d_gu_oth, wact_oth, h2_oth = experts(exts_oth, c_oth)
    pay_in = lax.ppermute(pay_oth, "core", swap)
    mix_in = lax.ppermute(mix_oth, "core", swap)
    pay, mix, d_gu, wact, h2 = experts(exts, c_all)
    *part, tick = call(add_kernel, "add_pay", [sds((TOK, D + 128), BF)] * 4 + [TICK], (pay, pay_in), moved=5 << 20)
    back = ring_return(part, "x")
    grads, tick = call(
        expert_grads_kernel, "expert_grads", [sds((2, 4, 4, HALF, 96, 128), BF), TICK],
        (h2, h2_oth, c_all, c_oth, d_gu, d_gu_oth, wact, wact_oth, tick), in_specs=[VMEM] * 8 + [ANY],
        flops=2 * RING * D * 128 * HALF * 6, moved=20 << 20, vmem=20,
    )
    d_middle, d_low, g_misc = call(
        middle_back_kernel, "middle_back", [sds((TOK, D), F32), block, sds((16, D), F32)],
        (at, *back, middle, ext, gates, kept, cotangent, own, oth, tick), in_specs=[SMEM] + [VMEM] * 11 + [ANY],
        scratch=[misc_scr], flops=100 * 10**9, moved=4 << 20,
    )
    d_mid = ring_gather(d_low, "x")
    e = lax.psum_scatter(grads.reshape(8, 4, HALF, 96, 128), ("zl", "y"), scatter_dimension=0, tiled=False)
    prepared = call(
        prepare_kernel, "prepare", [sds((8, 2 * TOK, TOK), F32), sds((D, 512), BF), sds((256, D), BF), sds((RING, D), BF)],
        (at, qk, own, oth, mix, mix_in, g_misc), in_specs=[SMEM] + [VMEM] * 5 + [ANY], flops=10**10, moved=8 << 20, vmem=16,
    )
    part, a_mine, a_send = call(
        attention_back_kernel, "attention_back", [sds((4, 2 * TOK, D), BF)] + [sds((8, 4, SMALL_HALF, 128), BF)] * 2,
        (at, *d_mid, *tok, *att, h1, qk, vv, *prepared, cosine, sine, g_misc),
        in_specs=[SMEM] + [VMEM] * 22, out_specs=[VMEM] + [ANY] * 2,
        scratch=[
            pltpu.VMEM((RING, D), BF), pltpu.VMEM((RING, 256), BF),
            pltpu.VMEM((RING, 512), BF), pltpu.VMEM((2, 2, 4, 4, SMALL_HALF, 128), BF), pltpu.SemaphoreType.DMA((4,)),
        ],
        flops=10 * 10**9, moved=12 << 20, vmem=26,
    )

    back = lax.psum_scatter(part, "x", scatter_dimension=0, tiled=False)
    a = lax.ppermute(a_send, "core", swap)
    (a,) = call(add_small_kernel, "add_small", [sds((8, 4, SMALL_HALF, 128), BF)], (a_mine, a), moved=3 << 20)
    a = lax.all_to_all(a, ("zl", "y"), 0, 0, tiled=True)
    e_piece = sds((480, 128), BF)
    e = call(split_kernel, "split", [e_piece] * 4, (at, e), in_specs=[SMEM, VMEM], moved=2 << 20)
    e = ring_return(e, "zh")
    grad_tokens, layer_out, last_tick = call(
        tokens_kernel, "tokens", [block, block, TICK], (at, back, tokens, d_middle, middle, own, oth),
        in_specs=[SMEM] + [VMEM] * 6, scratch=[misc_scr], moved=6 << 20,
    )
    (e,) = call(sum_four_kernel, "sum_four", [e_piece], e, moved=1 << 20)
    (a,) = call(sum_kernel, "sum_eight", [sds((4, SMALL_HALF, 128), BF)], (a,), moved=1 << 20)
    a = lax.all_to_all(a, "zh", 0, 0, tiled=True)
    (a,) = call(sum_kernel, "sum_last", [sds((SMALL_HALF, 128), BF)], (a,), moved=1 << 18)
    pairs = [(a, b) for a in range(2) for b in range(2)]
    first = lax.ppermute(e, ("core", "zl"), [(a * 2 + b, b * 2 + a) for a, b in pairs])
    second = lax.ppermute(e, ("core", "zl"), [(a * 2 + b, b * 2 + 1 - a) for a, b in pairs])
    a_other = lax.ppermute(a, "zl", swap)
    one, two = call(pack_kernel, "pack", [sds((PIECE, 128), BF)] * 2, (first, second, a, a_other), moved=1 << 20)
    one, two = ring_gather(one, "x", ORDER_ONE), ring_gather(two, "y", ORDER_TWO)
    one, two = call(stack_two_kernel, "stack_two", [sds((4, PIECE, 128), BF)] * 2, (*one, *two, back), in_specs=[VMEM] * 8 + [ANY], moved=2 << 20)
    spread = (*ring_gather(one, "y", ORDER_ONE), *ring_gather(two, "x", ORDER_TWO))
    grad_gate_up, grad_down, grad_qkv, grad_out, g_misc = call(
        spread_kernel, "spread",
        [
            sds((EXPERTS, 128, 1024), F32), sds((EXPERTS, 512, 128), F32), sds((128, 2048), F32), sds((1024, 128), F32),
            sds((16, 128), F32),
        ],
        (at, *spread, last_tick), in_specs=[SMEM] + [VMEM] * 8 + [ANY], out_specs=[ANY] * 4 + [VMEM],
        scratch=[
            pltpu.VMEM((2, HALF, 128, 1024), F32), pltpu.VMEM((2, HALF, 512, 128), F32), pltpu.VMEM((16, SMALL, 128), BF),
            pltpu.VMEM((128, 2048), F32), pltpu.VMEM((1024, 128), F32), pltpu.SemaphoreType.DMA((22,)),
        ],
        moved=14 << 20, vmem=20,
    )
    return (
        layer_out, grad_tokens, g_misc[10], g_misc[11], grad_qkv, grad_out, g_misc[:10].T, grad_gate_up, grad_down,
    )


def solution(mesh):
    fine = Mesh(mesh.devices.reshape(SIZES), AXES)
    rows = P(AXES, None)
    s = ("zh", "core")
    return jax.shard_map(
        local,
        mesh=fine,
        in_specs=(
            rows, rows, P(s), P(s), P(s, None), P(None, s), P(s, None), P(None, s, None), P(None, None, s), rows, rows,
        ),
        out_specs=(rows, rows, P(s), P(s), P(s, None), P(None, s), P(s, None), P(None, s, None), P(None, None, s)),
        check_vma=False,
    )
```
